32 devices in a mesh: xy: 4 (over y, core), gz: 8 (over z, x).
Axes of the slice: x: 2, y: 2, z: 4, core: 2. Of those that a mesh axis runs over, the one named last changes fastest.
Arguments:
- concentration: float32 [256, 64, 2048], P('gz', None, 'xy'), may hold values from -1 to 1
- geometry: float32 [2, 2048], P(None, 'xy'), may hold values from 0.5 to 2
- nbr_elem: int32 [4, 2048], P(None, 'xy'), may hold values from -1 to 2047, as said below
- nbr_edge: int32 [4, 2048], P(None, 'xy'), may hold values from 0 to 7, as said below
- wall_flags: int32 [256], P('gz'), may hold values 0 or 1
Outputs:
- modes: float32 [256, 64, 2048], P('gz', None, 'xy')
The draws below stay inside these ranges and needn't reach their ends.
Inputs may be any that keep to these rules, and one draw needn't show every extreme that they name: `nbr_elem`: entry [a, e] is the global number of the element across local edge a of element e, or -1 where that edge lies on a wall of the slab; the pairing is mutual. The neighbour is held by the same index of xy or by the index just before or after it, wrapping around; an element with a neighbour on the index before is among the first 64 elements of its device, one with a neighbour on the index after is among the last 64. No element has more than one edge whose neighbour is held by another index of xy. `nbr_edge`: the neighbour's local edge, plus 4 where the two elements number the shared nodes in opposite orders; 0 at walls; the same pairing read from both sides.
All inputs are finite; a program needn't handle non-finite values. No bound on the sum of `wall_flags` on one device may be relied on, other than what follows from the above.
Results may differ from the reference program's by a relative error of at most 0.0001.
Values sent between devices are 32-bit elements; how exact they have to be, the bound alone decides.
No kernel may reach another device: no remote copies, remote signals or barrier semaphores. Data moves between devices by JAX's collectives and lax.ppermute only.
A program may use at most 128 MiB of HBM per device.

```python
import math
import jax
import jax.numpy as jnp
import numpy as np
from jax import lax

NZ = 256
NODES = 64
COLS = 8
ROWS = 64
ITERS = 2
ELEMS = 2048


def connect_tables(key):
    cells = ELEMS
    columns = cells // ROWS
    cell_ids = jnp.arange(cells, dtype=jnp.int32)
    column = cell_ids // ROWS
    height = cell_ids % ROWS
    device = column // COLS
    within = column % COLS
    band_id = jnp.where(within == 0, 0, jnp.where(within == COLS - 1, 2, 1))
    shuffle = jax.random.permutation(jax.random.fold_in(key, 101), cells).astype(jnp.int32)
    ranking = (device * 3 + band_id) * cells + shuffle
    sorted_ids = jnp.argsort(ranking)
    number = jnp.zeros(cells, jnp.int32).at[sorted_ids].set(cell_ids)
    flip_bits = jax.random.randint(jax.random.fold_in(key, 202), (2, cells), 0, 2).astype(jnp.int32)
    flip_x = flip_bits[0]
    flip_y = flip_bits[1]
    elem_tab = jnp.zeros((4, cells), jnp.int32)
    edge_tab = jnp.zeros((4, cells), jnp.int32)
    offsets = ((0, -1), (1, 0), (0, 1), (-1, 0))
    for global_side in range(4):
        step_x, step_y = offsets[global_side]
        next_col = (column + step_x) % columns
        next_row = height + step_y
        inside = (next_row >= 0) & (next_row < ROWS)
        next_cell = next_col * ROWS + jnp.clip(next_row, 0, ROWS - 1)
        if global_side % 2 == 0:
            label_me = flip_y
            label_nb = flip_y[next_cell]
            order_me = flip_x
            order_nb = flip_x[next_cell]
        else:
            label_me = flip_x
            label_nb = flip_x[next_cell]
            order_me = flip_y
            order_nb = flip_y[next_cell]
        my_edge = jnp.bitwise_xor(global_side, 2 * label_me)
        theirs = jnp.bitwise_xor((global_side + 2) % 4, 2 * label_nb)
        edge_code = theirs + 4 * jnp.bitwise_xor(order_me, order_nb)
        elem_tab = elem_tab.at[my_edge, number].set(jnp.where(inside, number[next_cell], -1))
        edge_tab = edge_tab.at[my_edge, number].set(jnp.where(inside, edge_code, 0))
    return (elem_tab, edge_tab)


def draw_nbr_elem(key, part):
    return connect_tables(key)[0]


def draw_nbr_edge(key, part):
    return connect_tables(key)[1]


def plant(values, stream_key, smallest, largest):
    place = [jax.random.randint(jax.random.fold_in(stream_key, axis), (), 0, length) for axis, length in enumerate(values.shape)]
    longest = values.shape.index(max(values.shape))
    neighbour = place[:longest] + [(place[longest] + 1) % values.shape[longest]] + place[longest + 1:]
    return values.at[tuple(place)].set(smallest).at[tuple(neighbour)].set(largest)


def shard_levels(stream_key, shape, cuts, low, largest):
    def one(dim, parts):
        steps = jax.random.uniform(jax.random.fold_in(jax.random.fold_in(stream_key, 6), dim), (parts,), jnp.float32, low / len(cuts), largest / len(cuts))
        return jnp.repeat(jnp.exp(steps), shape[dim] // parts).reshape((-1,) + (1,) * (len(shape) - dim - 1))

    gain = one(*cuts[0])
    for cut in cuts[1:]:
        gain = gain * one(*cut)
    return gain


def setup_inputs(seed: int = 0) -> dict:
    arg_keys = jax.random.split(jax.random.key(seed), 6)
    return {
        "concentration": jnp.clip(jax.random.uniform(arg_keys[0], (NZ, NODES, ELEMS), jnp.float32, -1.0, 1.0) * shard_levels(arg_keys[0], (NZ, NODES, ELEMS), ((0, 8), (2, 4)), -0.4, 0.0), -1.0, 1.0),
        "geometry": jnp.clip(jnp.exp(math.log(2.0) - 1.3862944 * jax.random.uniform(arg_keys[1], (2, ELEMS), jnp.float32) ** shard_levels(arg_keys[1], (2, ELEMS), ((1, 4),), -0.2, 0.2)), 0.5, 2.0),
        "nbr_elem": draw_nbr_elem(jax.random.fold_in(arg_keys[5], 71), 0),
        "nbr_edge": draw_nbr_edge(jax.random.fold_in(arg_keys[5], 71), 0),
        "wall_flags": plant((jax.random.randint(arg_keys[4], (NZ,), 0, 2) < 1).astype(jnp.int32), jax.random.fold_in(arg_keys[4], 1), 0, 1),
    }


time_step = 0.2
axial_stiffness = 0.002
plane_stiffness = 1.0
edge_penalty = 4.0
axial_mobility = 0.002
mobility_floor = 0.05
highest = lax.Precision.HIGHEST

def point_tables():
    degree = 7
    points = np.arange(degree + 1)
    theta = np.pi * points / degree
    nodes_x = np.cos(theta)
    signs = np.where((points == 0) | (points == degree), 2.0, 1.0) * (-1.0) ** points
    differ = nodes_x[:, None] - nodes_x[None, :]
    deriv = np.outer(signs, 1.0 / signs) / (differ + np.eye(degree + 1))
    deriv = deriv - np.eye(degree + 1) * deriv.sum(axis=1)[:, None]
    inner = np.ones(degree - 1)
    for number in range(1, (degree - 1) // 2 + 1):
        inner = inner - 2.0 * np.cos(2 * number * theta[1:degree]) / (4 * number * number - 1)
    weights = np.zeros(degree + 1)
    weights[1:degree] = 2.0 * inner / degree
    weights[0] = 1.0 / degree ** 2
    weights[degree] = 1.0 / degree ** 2
    return (deriv, weights)

def make_tables():
    deriv, weights = point_tables()
    grad_x = np.kron(np.eye(8), deriv)
    grad_y = np.kron(deriv, np.eye(8))
    mass_w = np.kron(weights, weights)
    return (jnp.asarray(grad_x, jnp.float32), jnp.asarray(grad_y, jnp.float32), jnp.asarray(mass_w, jnp.float32), jnp.asarray(weights, jnp.float32))

def fourier_table(length):
    planes = np.arange(length)
    wave_no = (planes + 1) // 2
    phase = np.outer(wave_no, planes) % length * (2.0 * np.pi / length)
    table = np.where((planes % 2 == 1)[:, None], np.cos(phase), np.sin(phase)) * np.sqrt(2.0 / length)
    table[0] = 1.0 / np.sqrt(length)
    table[length - 1] = np.cos(phase[length - 1]) / np.sqrt(length)
    return table

def weak_flux(field, mobility, grad_x, grad_y, mass_w, jacobian, scale_x, scale_y):
    along_x = jnp.einsum('nm,ame->ane', grad_x, field, precision=highest)
    along_y = jnp.einsum('nm,ame->ane', grad_y, field, precision=highest)
    flux_x = mass_w[:, None] * mobility * along_x * (jacobian * scale_x * scale_x)
    flux_y = mass_w[:, None] * mobility * along_y * (jacobian * scale_y * scale_y)
    return jnp.einsum('mn,ame->ane', grad_x, flux_x, precision=highest) + jnp.einsum('mn,ame->ane', grad_y, flux_y, precision=highest)

def edge_traces(field):
    grid = field.reshape(field.shape[0], 8, 8, field.shape[2])
    return jnp.stack([grid[:, 0, :, :], grid[:, :, 7, :], grid[:, 7, :, :], grid[:, :, 0, :]], axis=2)

def add_edges(field, penalty):
    grid = field.reshape(field.shape[0], 8, 8, field.shape[2])
    grid = grid.at[:, 0, :, :].add(penalty[:, :, 0])
    grid = grid.at[:, :, 7, :].add(penalty[:, :, 1])
    grid = grid.at[:, 7, :, :].add(penalty[:, :, 2])
    grid = grid.at[:, :, 0, :].add(penalty[:, :, 3])
    return grid.reshape(field.shape)

def reference(concentration, geometry, nbr_elem, nbr_edge, wall_flags):
    grad_x, grad_y, mass_w, edge_w = make_tables()
    scale_x = geometry[0]
    scale_y = geometry[1]
    jacobian = 1.0 / (scale_x * scale_y)
    planes = concentration.shape[0]
    elems = concentration.shape[2]

    def plane_block(field):
        chem = field * field * field - field
        mobility = jnp.maximum(1.0 - field * field, mobility_floor)
        explicit = jacobian * mass_w[:, None] * field / time_step - weak_flux(chem, mobility, grad_x, grad_y, mass_w, jacobian, scale_x, scale_y)
        bulk = jacobian * mass_w[:, None] * chem
        return (explicit, bulk)
    explicit, bulk = lax.map(plane_block, concentration.reshape(planes // 16, 16, 64, elems))
    explicit = explicit.reshape(planes, 64, elems)
    bulk = bulk.reshape(planes, 64, elems)
    fourier = jnp.asarray(fourier_table(planes), jnp.float32)
    wave_all = ((jnp.arange(planes, dtype=jnp.int32) + 1) // 2).astype(jnp.float32)
    explicit_hat = jnp.einsum('kp,pne->kne', fourier, explicit, precision=highest)
    bulk_hat = jnp.einsum('kp,pne->kne', fourier, bulk, precision=highest)
    right_side = explicit_hat - axial_mobility * (wave_all * wave_all)[:, None, None] * bulk_hat
    wall = nbr_elem < 0
    safe_ids = jnp.maximum(nbr_elem, 0).astype(jnp.int32)
    position = (nbr_edge % 4 * elems + safe_ids).astype(jnp.int32).reshape(-1)
    reverse = nbr_edge >= 4

    def solve_block(block):
        rhs_b, wave_b, flag_b = block
        count = rhs_b.shape[0]
        mass_coef = 1.0 / time_step + axial_stiffness * wave_b * wave_b
        flag_f = flag_b.astype(jnp.float32)

        def helm_apply(field):
            result = jacobian * mass_w[:, None] * mass_coef[:, None, None] * field
            result = result + plane_stiffness * weak_flux(field, 1.0, grad_x, grad_y, mass_w, jacobian, scale_x, scale_y)
            traces = edge_traces(field)
            flat = traces.reshape(count, 8, 4 * elems)
            values = jnp.take(flat, position, axis=2).reshape(count, 8, 4, elems)
            values = jnp.where(reverse[None, None], values[:, ::-1], values)
            jump = jnp.where(wall[None, None], flag_f[:, None, None, None] * traces, traces - values)
            penalty = edge_penalty * edge_w[None, :, None, None] * jump
            return add_edges(result, penalty)
        solution = jnp.zeros_like(rhs_b)
        residual = rhs_b
        direction = rhs_b
        norm_now = lax.optimization_barrier(jnp.sum(residual * residual, axis=(1, 2)))
        for sweep in range(ITERS):
            image = helm_apply(direction)
            alpha = norm_now / lax.optimization_barrier(jnp.sum(direction * image, axis=(1, 2)))
            solution = solution + alpha[:, None, None] * direction
            residual = residual - alpha[:, None, None] * image
            if sweep + 1 < ITERS:
                norm_next = lax.optimization_barrier(jnp.sum(residual * residual, axis=(1, 2)))
                direction = residual + (norm_next / norm_now)[:, None, None] * direction
                norm_now = norm_next
        return solution
    result = lax.map(solve_block, (right_side.reshape(planes // 16, 16, 64, elems), wave_all.reshape(planes // 16, 16), wall_flags.reshape(planes // 16, 16)))
    return result.reshape(planes, 64, elems)
```

```python
import functools

import jax
import jax.numpy as jnp
import ml_dtypes
import numpy as np
from jax import lax
from jax.experimental import pallas as pl
from jax.experimental.pallas import tpu as pltpu
from jax.sharding import PartitionSpec as P

ROWS = 64
LANES = 128
MIB = 1024 * 1024

time_step = 0.2
axial_stiffness = 0.002
plane_stiffness = 1.0
edge_penalty = 4.0
axial_mobility = 0.002
mobility_floor = 0.05


def point_tables():
    degree = 7
    points = np.arange(degree + 1)
    theta = np.pi * points / degree
    nodes_x = np.cos(theta)
    signs = np.where((points == 0) | (points == degree), 2.0, 1.0) * (-1.0) ** points
    differ = nodes_x[:, None] - nodes_x[None, :]
    deriv = np.outer(signs, 1.0 / signs) / (differ + np.eye(degree + 1))
    deriv = deriv - np.eye(degree + 1) * deriv.sum(axis=1)[:, None]
    inner = np.ones(degree - 1)
    for number in range(1, (degree - 1) // 2 + 1):
        inner = inner - 2.0 * np.cos(2 * number * theta[1:degree]) / (4 * number * number - 1)
    weights = np.zeros(degree + 1)
    weights[1:degree] = 2.0 * inner / degree
    weights[0] = 1.0 / degree**2
    weights[degree] = 1.0 / degree**2
    return (deriv, weights)


def fourier_table(length):
    planes = np.arange(length)
    wave_no = (planes + 1) // 2
    phase = np.outer(wave_no, planes) % length * (2.0 * np.pi / length)
    table = np.where((planes % 2 == 1)[:, None], np.cos(phase), np.sin(phase)) * np.sqrt(
        2.0 / length
    )
    table[0] = 1.0 / np.sqrt(length)
    table[length - 1] = np.cos(phase[length - 1]) / np.sqrt(length)
    return table


DERIV, WEIGHTS = point_tables()
BACK = DERIV.T * WEIGHTS[None, :]
STIFF = BACK @ DERIV


def two_parts(table):
    upper = table.astype(np.float32).astype(ml_dtypes.bfloat16)
    lower = (table - upper.astype(np.float64)).astype(np.float32).astype(ml_dtypes.bfloat16)
    return upper, lower


def split(value):
    upper = value.astype(jnp.bfloat16)
    lower = (value - upper.astype(jnp.float32)).astype(jnp.bfloat16)
    return upper, lower


class Fold:
    def __init__(self, width):
        self.width = width
        self.parts = LANES // width
        self.fold_j = 2 if self.parts >= 2 else 1
        self.fold_i = 2 if self.parts >= 4 else 1
        self.count_j = 8 // self.fold_j
        self.count_i = 8 // self.fold_i
        self.slots = self.count_j * self.count_i

    def slot(self, jp, ip):
        return jp * self.count_i + ip

    def node(self, jp, ip, part):
        half_j, half_i = part // self.fold_i, part % self.fold_i
        j = 7 - jp if half_j else jp
        i = 7 - ip if half_i else ip
        return 8 * j + i

    def place(self, node):
        j, i = node // 8, node % 8
        half_j = 1 if j >= self.count_j else 0
        half_i = 1 if i >= self.count_i else 0
        jp = 7 - j if half_j else j
        ip = 7 - i if half_i else i
        return self.slot(jp, ip), half_j * self.fold_i + half_i


def lane_of(shape):
    return lax.broadcasted_iota(jnp.int32, shape, len(shape) - 1)


def rolled(value, lanes):
    lanes = lanes % LANES
    return value if lanes == 0 else pltpu.roll(value, lanes, value.ndim - 1)


def by_part(values, lane, width):
    out = values[0]
    for r in range(1, len(values)):
        out = jnp.where(lane >= r * width, values[r], out)
    return out


def mirrored(value, lane, shift):
    if 2 * shift == LANES:
        return rolled(value, shift)
    return jnp.where((lane & shift) == 0, rolled(value, -shift), rolled(value, shift))


def combine(coefs, values):
    total = None
    for c, v in zip(coefs, values):
        term = v * np.float32(c)
        total = term if total is None else total + term
    return total


def line_apply(matrix, values, sign):
    even = [values[k] + values[7 - k] for k in range(4)]
    odd = [values[k] - values[7 - k] for k in range(4)]
    out = [None] * 8
    for a in range(4):
        from_even = combine([(matrix[a, b] + matrix[a, 7 - b]) / 2 for b in range(4)], even)
        from_odd = combine([(matrix[a, b] - matrix[a, 7 - b]) / 2 for b in range(4)], odd)
        out[a] = from_even + from_odd
        out[7 - a] = from_even - from_odd if sign > 0 else from_odd - from_even
    return out


def derivative_line(matrix, values, back, swap):
    if swap is None:
        return line_apply(matrix, values, -1)
    other = [swap(v) for v in values]
    sign = -1.0 if back else 1.0
    out = []
    for a in range(4):
        coefs = [matrix[a, b] for b in range(4)] + [sign * matrix[a, 7 - b] for b in range(4)]
        out.append(combine(coefs, list(values) + other))
    return out


EDGE_NODES = [
    [t for t in range(8)],
    [8 * t + 7 for t in range(8)],
    [56 + t for t in range(8)],
    [8 * t for t in range(8)],
]


def pack_kernel(fold, c_ref, out_ref):
    lane = lane_of((c_ref.shape[0], LANES))
    for jp in range(fold.count_j):
        for ip in range(fold.count_i):
            loads = [c_ref[:, fold.node(jp, ip, q), :] for q in range(fold.parts)]
            for r in range(fold.parts):
                parts = [rolled(loads[q], (q - r) * fold.width) for q in range(fold.parts)]
                out_ref[r, fold.slot(jp, ip)] = by_part(parts, lane, fold.width)


def pack(conc, fold, groups):
    planes, nodes, elems = conc.shape
    blocks = elems // LANES
    return pl.pallas_call(
        functools.partial(pack_kernel, fold),
        grid=(blocks,),
        in_specs=[pl.BlockSpec((planes, nodes, LANES), lambda b: (0, 0, b))],
        out_specs=pl.BlockSpec((fold.parts, fold.slots, planes, LANES), lambda b: (b, 0, 0, 0)),
        out_shape=jax.ShapeDtypeStruct((groups, fold.slots, planes, LANES), jnp.float32),
        compiler_params=pltpu.CompilerParams(vmem_limit_bytes=24 * MIB),
        cost_estimate=pl.CostEstimate(
            flops=conc.size, bytes_accessed=8 * conc.size, transcendentals=0
        ),
    )(conc)


def rhs_kernel(fold, groups, planes, first_ref, second_ref, y_ref, geo_ref, out_ref, x_ref, acc_ref):
    step = pl.program_id(0)
    total = groups * planes

    @pl.when(step < groups)
    def _():
        def chunk(part, _):
            base = pl.multiple_of(part * 16, 16)
            lane = lane_of((16, LANES))
            jac = jnp.broadcast_to(geo_ref[0:1, :], (16, LANES))
            ratio_x = jnp.broadcast_to(geo_ref[1:2, :], (16, LANES))
            ratio_y = jnp.broadcast_to(geo_ref[2:3, :], (16, LANES))

            def conc(jp, ip):
                return y_ref[0, fold.slot(jp, ip), pl.ds(base, 16), :]

            def potential(c):
                square = c * c
                return square * c - c, jnp.maximum(1.0 - square, mobility_floor)

            def flux(fields, swap):
                pairs = [potential(c) for c in fields]
                slope = derivative_line(DERIV, [p[0] for p in pairs], False, swap)
                scaled = [s * p[1] for s, p in zip(slope, pairs)]
                return derivative_line(BACK, scaled, True, swap), pairs

            swap_i = None
            if fold.fold_i == 2:
                swap_i = lambda v: mirrored(v, lane, fold.width)
            swap_j = None
            if fold.fold_j == 2:
                swap_j = lambda v: mirrored(v, lane, fold.width * fold.fold_i)
            for jp in range(fold.count_j):
                fields = [conc(jp, ip) for ip in range(fold.count_i)]
                result, _unused = flux(fields, swap_i)
                scale = ratio_x * np.float32(WEIGHTS[jp])
                for ip in range(fold.count_i):
                    acc_ref[fold.slot(jp, ip)] = result[ip] * scale
            row = pl.multiple_of(step * planes + base, 16)
            for ip in range(fold.count_i):
                fields = [conc(jp, ip) for jp in range(fold.count_j)]
                result, pairs = flux(fields, swap_j)
                scale = ratio_y * np.float32(WEIGHTS[ip])
                for jp in range(fold.count_j):
                    slot = fold.slot(jp, ip)
                    mass = jac * np.float32(WEIGHTS[jp] * WEIGHTS[ip])
                    explicit = (
                        mass * (fields[jp] * np.float32(1.0 / time_step))
                        - acc_ref[slot]
                        - result[jp] * scale
                    )
                    bulk = mass * pairs[jp][0]
                    where = pl.ds((slot % 2) * LANES, LANES)
                    upper, lower = split(explicit)
                    x_ref[slot // 2, pl.ds(row, 16), where] = upper
                    x_ref[slot // 2, pl.ds(2 * total + row, 16), where] = lower
                    upper, lower = split(bulk)
                    x_ref[slot // 2, pl.ds(total + row, 16), where] = upper
                    x_ref[slot // 2, pl.ds(3 * total + row, 16), where] = lower
            return 0

        lax.fori_loop(0, planes // 16, chunk, 0)

    @pl.when(step >= groups)
    def _():
        pair = step - groups
        data = x_ref[pair]
        result = jnp.dot(first_ref[...], data, preferred_element_type=jnp.float32)
        result = result + jnp.dot(
            second_ref[...], data[: 2 * total], preferred_element_type=jnp.float32
        )
        for h in range(groups):
            rows = result[h * planes : (h + 1) * planes]
            out_ref[h, 0] = rows[:, :LANES]
            out_ref[h, 1] = rows[:, LANES:]


def right_hand_side(field, geo, fold, total):
    groups, slots, planes, _ = field.shape
    table = fourier_table(total).astype(np.float32).astype(np.float64)
    wave = ((np.arange(total) + 1) // 2).astype(np.float64)
    upper, lower = two_parts(table)
    upper_b, lower_b = two_parts(-axial_mobility * (wave * wave)[:, None] * table)
    first = jnp.asarray(np.concatenate([upper, upper_b, upper, upper_b], axis=1))
    second = jnp.asarray(np.concatenate([lower, lower_b], axis=1))
    pairs = slots // 2
    return pl.pallas_call(
        functools.partial(rhs_kernel, fold, groups, planes),
        grid=(groups + pairs,),
        in_specs=[
            pl.BlockSpec((total, 4 * total), lambda s: (0, 0)),
            pl.BlockSpec((total, 2 * total), lambda s: (0, 0)),
            pl.BlockSpec(
                (1, slots, planes, LANES), lambda s: (jnp.minimum(s, groups - 1), 0, 0, 0)
            ),
            pl.BlockSpec((8, LANES), lambda s: (0, 0)),
        ],
        out_specs=pl.BlockSpec(
            (groups, 2, planes, LANES), lambda s: (0, jnp.maximum(s - groups, 0), 0, 0)
        ),
        out_shape=jax.ShapeDtypeStruct((groups, slots, planes, LANES), jnp.float32),
        scratch_shapes=[
            pltpu.VMEM((pairs, 4 * total, 2 * LANES), jnp.bfloat16),
            pltpu.VMEM((slots, 16, LANES), jnp.float32),
        ],
        compiler_params=pltpu.CompilerParams(vmem_limit_bytes=40 * MIB),
        cost_estimate=pl.CostEstimate(
            flops=12 * total * field.size, bytes_accessed=8 * field.size, transcendentals=0
        ),
    )(first, second, field, geo)


def edge_send(mask_ref, edge, out_ref):
    for t in range(8):
        total = None
        for a in range(4):
            term = edge(a, t) * mask_ref[a : a + 1, :]
            total = term if total is None else total + term
        out_ref[t] = total


def first_send_kernel(fold, rhs_ref, mask_ref, out_ref):
    half = rhs_ref.shape[0] // 2
    lane = lane_of(out_ref.shape[1:])

    def edge(a, t):
        slot, part = fold.place(EDGE_NODES[a][t])
        parts = []
        for r in range(2 * half):
            parts.append(rolled(rhs_ref[r, slot], (r - part) * fold.width))
        return by_part(parts, lane, fold.width)

    edge_send(mask_ref, edge, out_ref)


def first_send(rhs, mask, fold):
    groups, slots, modes, _ = rhs.shape
    half = ROWS // fold.width
    ends = jnp.concatenate([rhs[:half], rhs[groups - half :]], axis=0)
    return pl.pallas_call(
        functools.partial(first_send_kernel, fold),
        out_shape=jax.ShapeDtypeStruct((8, modes, LANES), jnp.float32),
        compiler_params=pltpu.CompilerParams(vmem_limit_bytes=16 * MIB),
    )(ends, mask)


def unpack(fold, r_ref, out_ref, rows, lanes):
    lane = lane_of((8, LANES))
    for jp in range(fold.count_j):
        for ip in range(fold.count_i):
            loads = [r_ref[r, fold.slot(jp, ip), rows, :] for r in range(fold.parts)]
            for q in range(fold.parts):
                parts = [rolled(loads[r], (r - q) * fold.width) for r in range(fold.parts)]
                out_ref[fold.node(jp, ip, q), rows, lanes] = by_part(parts, lane, fold.width)


def volume(field, acc_ref, geo_ref, mass_ref, rows, lanes, visit):
    jac = geo_ref[0:1, :] * mass_ref[rows, :]
    ratio_x = jnp.broadcast_to(geo_ref[1:2, :], (8, LANES))
    ratio_y = jnp.broadcast_to(geo_ref[2:3, :], (8, LANES))
    for j in range(8):
        result = line_apply(plane_stiffness * STIFF, [field(8 * j + i) for i in range(8)], 1)
        scale = ratio_x * np.float32(WEIGHTS[j])
        for i in range(8):
            acc_ref[8 * j + i] = result[i] * scale
    for i in range(8):
        values = [field(8 * j + i) for j in range(8)]
        result = line_apply(plane_stiffness * STIFF, values, 1)
        scale = ratio_y * np.float32(WEIGHTS[i])
        for j in range(8):
            mass = jac * np.float32(WEIGHTS[j] * WEIGHTS[i])
            visit(8 * j + i, values[j], acc_ref[8 * j + i] + result[j] * scale + mass * values[j])


def fill_traces(field_ref, trace_ref):
    modes, elems = field_ref.shape[1:]
    for a in range(4):
        for t in range(8):
            upper, lower = split(field_ref[EDGE_NODES[a][t]])
            where = pl.ds(a * elems, elems)
            trace_ref[pl.ds(t * modes, modes), where] = upper
            trace_ref[pl.ds((8 + t) * modes, modes), where] = lower


def fill_halo(halo_ref, parts_ref):
    modes = halo_ref.shape[2]
    lane = lane_of((modes, LANES))
    for t in range(8):
        upper, lower = split(jnp.where(lane < ROWS, halo_ref[0, t], halo_ref[1, t]))
        parts_ref[pl.ds(t * modes, modes), :] = upper
        parts_ref[pl.ds((8 + t) * modes, modes), :] = lower


def gathered(trace_ref, parts_ref, local_ref, far_ref, val_ref):
    modes, elems = val_ref.shape[1:]
    rows = 8 * modes
    value = jnp.dot(trace_ref[...], local_ref[...], preferred_element_type=jnp.float32)
    val_ref[...] = (value[:rows] + value[rows:]).reshape(8, modes, elems)
    value = jnp.dot(parts_ref[...], far_ref[...], preferred_element_type=jnp.float32)
    far = (value[:rows] + value[rows:]).reshape(8, modes, LANES)
    lane = lane_of(far.shape)
    val_ref[:, :, :LANES] += jnp.where(lane < ROWS, far, 0.0)
    val_ref[:, :, elems - LANES :] += jnp.where(lane < ROWS, 0.0, far)


def penalties(edge, field_ref, val_ref, edges_ref, flag_ref, visit):
    modes, elems = val_ref.shape[1:]
    for block in range(elems // LANES):
        lanes = pl.ds(block * LANES, LANES)
        wall = edges_ref[0:1, lanes]
        reverse = jnp.broadcast_to(edges_ref[1:2, lanes], (modes, LANES)) > 0.5
        coef = 1.0 - wall * (1.0 - flag_ref[...])
        for t in range(8):
            node = EDGE_NODES[edge][t]
            mine = field_ref[node, :, lanes]
            other = jnp.where(reverse, val_ref[7 - t, :, lanes], val_ref[t, :, lanes])
            weight = np.float32(edge_penalty * WEIGHTS[t])
            visit(node, lanes, mine, weight * (coef * mine - other))


def first_apply_kernel(
    fold,
    blocks,
    r_ref,
    geo_ref,
    mass_ref,
    flag_ref,
    mask_ref,
    halo_ref,
    far_ref,
    local_ref,
    edges_ref,
    r0_ref,
    q0_ref,
    send_ref,
    sums_ref,
    trace_ref,
    parts_ref,
    val_ref,
    acc_ref,
):
    step = pl.program_id(0)
    modes, elems = val_ref.shape[1:]

    @pl.when(step == 0)
    def _():
        sums_ref[...] = jnp.zeros_like(sums_ref)

    @pl.when(step < blocks)
    def _():
        lanes = pl.ds(pl.multiple_of(step * LANES, LANES), LANES)

        def tile(part, _):
            rows = pl.ds(pl.multiple_of(part * 8, 8), 8)
            unpack(fold, r_ref, r0_ref, rows, lanes)
            totals = [None, None]

            def visit(node, value, image):
                q0_ref[node, rows, lanes] = image
                for k, term in enumerate((value * value, value * image)):
                    totals[k] = term if totals[k] is None else totals[k] + term

            volume(
                lambda node: r0_ref[node, rows, lanes],
                acc_ref,
                geo_ref,
                mass_ref,
                rows,
                lanes,
                visit,
            )
            for k in range(2):
                sums_ref[k, rows, :] += totals[k]
            return 0

        lax.fori_loop(0, modes // 8, tile, 0)

    @pl.when(step == blocks)
    def _():
        fill_traces(r0_ref, trace_ref)
        fill_halo(halo_ref, parts_ref)

    for edge in range(4):

        @pl.when(step == blocks + edge)
        def _():
            gathered(trace_ref, parts_ref, local_ref, far_ref, val_ref)
            totals = [None]

            def visit(node, lanes, mine, term):
                q0_ref[node, :, lanes] += term
                product = mine * term
                totals[0] = product if totals[0] is None else totals[0] + product

            penalties(edge, r0_ref, val_ref, edges_ref, flag_ref, visit)
            sums_ref[1] += totals[0]

    @pl.when(step == blocks + 3)
    def _():
        lane = lane_of((modes, LANES))

        def edge_value(a, t):
            node = EDGE_NODES[a][t]
            return jnp.where(
                lane < ROWS, q0_ref[node, :, :LANES], q0_ref[node, :, elems - LANES :]
            )

        edge_send(mask_ref, edge_value, send_ref)


def edge_specs(blocks, elems):
    def at(step):
        return jnp.maximum(step - blocks, 0)

    far = pl.BlockSpec((LANES, LANES), lambda s: (0, at(s)))
    local = pl.BlockSpec((4 * elems, elems), lambda s: (0, at(s)))
    flags = pl.BlockSpec((8, elems), lambda s: (at(s), 0))
    return far, local, flags


def whole(shape):
    return pl.BlockSpec(shape, lambda s: (0,) * len(shape))


def edge_scratch(modes, elems):
    return [
        pltpu.VMEM((16 * modes, 4 * elems), jnp.bfloat16),
        pltpu.VMEM((16 * modes, LANES), jnp.bfloat16),
        pltpu.VMEM((8, modes, elems), jnp.float32),
        pltpu.VMEM((64, 8, LANES), jnp.float32),
    ]


def first_apply(rhs, geo, mass, flag, mask, halo, far, local, edges, fold):
    groups, slots, modes, _ = rhs.shape
    blocks = groups // fold.parts
    elems = blocks * LANES
    block_of = lambda s: jnp.minimum(s, blocks - 1)
    far_spec, local_spec, edges_spec = edge_specs(blocks, elems)
    field = jax.ShapeDtypeStruct((64, modes, elems), jnp.float32)
    return pl.pallas_call(
        functools.partial(first_apply_kernel, fold, blocks),
        grid=(blocks + 4,),
        in_specs=[
            pl.BlockSpec((fold.parts, slots, modes, LANES), lambda s: (block_of(s), 0, 0, 0)),
            pl.BlockSpec((8, LANES), lambda s: (0, block_of(s))),
            whole((modes, LANES)),
            whole((modes, LANES)),
            whole((8, LANES)),
            whole((2, 8, modes, LANES)),
            far_spec,
            local_spec,
            edges_spec,
        ],
        out_specs=[
            whole((64, modes, elems)),
            whole((64, modes, elems)),
            whole((8, modes, LANES)),
            whole((2, modes, LANES)),
        ],
        out_shape=[
            field,
            field,
            jax.ShapeDtypeStruct((8, modes, LANES), jnp.float32),
            jax.ShapeDtypeStruct((2, modes, LANES), jnp.float32),
        ],
        scratch_shapes=edge_scratch(modes, elems),
        compiler_params=pltpu.CompilerParams(vmem_limit_bytes=48 * MIB),
        cost_estimate=pl.CostEstimate(
            flops=256 * modes * elems * elems, bytes_accessed=24 * MIB, transcendentals=0
        ),
    )(rhs, geo, mass, flag, mask, halo, far, local, edges)


def second_apply_kernel(
    blocks,
    q0_ref,
    geo_ref,
    mass_ref,
    flag_ref,
    halo_ref,
    far_ref,
    local_ref,
    edges_ref,
    sums_ref,
    out_ref,
    trace_ref,
    parts_ref,
    val_ref,
    acc_ref,
    more_ref,
):
    step = pl.program_id(0)
    modes, elems = val_ref.shape[1:]

    @pl.when(step == 0)
    def _():
        more_ref[...] = jnp.zeros_like(more_ref)

    @pl.when(step < blocks)
    def _():
        lanes = pl.ds(pl.multiple_of(step * LANES, LANES), LANES)

        def tile(part, _):
            rows = pl.ds(pl.multiple_of(part * 8, 8), 8)
            totals = [None, None]

            def visit(node, value, image):
                for k, term in enumerate((value * value, value * image)):
                    totals[k] = term if totals[k] is None else totals[k] + term

            volume(
                lambda node: q0_ref[node, rows, lanes],
                acc_ref,
                geo_ref,
                mass_ref,
                rows,
                lanes,
                visit,
            )
            for k in range(2):
                more_ref[k, rows, :] += totals[k]
            return 0

        lax.fori_loop(0, modes // 8, tile, 0)

    @pl.when(step == blocks)
    def _():
        fill_traces(q0_ref, trace_ref)
        fill_halo(halo_ref, parts_ref)

    for edge in range(4):

        @pl.when(step == blocks + edge)
        def _():
            gathered(trace_ref, parts_ref, local_ref, far_ref, val_ref)
            totals = [None]

            def visit(node, lanes, mine, term):
                product = mine * term
                totals[0] = product if totals[0] is None else totals[0] + product

            penalties(edge, q0_ref, val_ref, edges_ref, flag_ref, visit)
            more_ref[1] += totals[0]

    @pl.when(step == blocks + 3)
    def _():
        lane = lane_of((modes, LANES))
        sums = [sums_ref[0], sums_ref[1], more_ref[0], more_ref[1]]
        packed = jnp.zeros((modes, LANES), jnp.float32)
        for k, value in enumerate(sums):
            packed = jnp.where(lane == k, jnp.sum(value, axis=1, keepdims=True), packed)
        out_ref[...] = packed


def second_apply(q0, geo, mass, flag, halo, far, local, edges, sums):
    _, modes, elems = q0.shape
    blocks = elems // LANES
    block_of = lambda s: jnp.minimum(s, blocks - 1)
    far_spec, local_spec, edges_spec = edge_specs(blocks, elems)
    return pl.pallas_call(
        functools.partial(second_apply_kernel, blocks),
        grid=(blocks + 4,),
        in_specs=[
            whole((64, modes, elems)),
            pl.BlockSpec((8, LANES), lambda s: (0, block_of(s))),
            whole((modes, LANES)),
            whole((modes, LANES)),
            whole((2, 8, modes, LANES)),
            far_spec,
            local_spec,
            edges_spec,
            whole((2, modes, LANES)),
        ],
        out_specs=whole((modes, LANES)),
        out_shape=jax.ShapeDtypeStruct((modes, LANES), jnp.float32),
        scratch_shapes=edge_scratch(modes, elems) + [pltpu.VMEM((2, modes, LANES), jnp.float32)],
        compiler_params=pltpu.CompilerParams(vmem_limit_bytes=48 * MIB),
        cost_estimate=pl.CostEstimate(
            flops=256 * modes * elems * elems, bytes_accessed=12 * MIB, transcendentals=0
        ),
    )(q0, geo, mass, flag, halo, far, local, edges, sums)


def finish_kernel(r0_ref, q0_ref, sums_ref, out_ref):
    modes = out_ref.shape[0]
    total = sums_ref[0]
    for k in range(1, sums_ref.shape[0]):
        total = total + sums_ref[k]
    m0, m1, m2, m3 = [total[:, k : k + 1] for k in range(4)]
    alpha = m0 / m1
    norm = alpha * (alpha * m2) - 2.0 * (alpha * m1) + m0
    energy = m1 - 2.0 * (alpha * m2) + alpha * (alpha * m3)
    beta = norm / m0
    second = norm / (energy - beta * (norm / alpha))
    on_r = jnp.broadcast_to(alpha + second * (1.0 + beta), (modes, LANES))
    on_q = jnp.broadcast_to(second * alpha, (modes, LANES))
    for node in range(64):
        out_ref[:, node, :] = on_r * r0_ref[node] - on_q * q0_ref[node]


def finish(r0, q0, sums):
    _, modes, elems = r0.shape
    field = pl.BlockSpec((64, modes, LANES), lambda b: (0, 0, b))
    return pl.pallas_call(
        finish_kernel,
        grid=(elems // LANES,),
        in_specs=[field, field, whole(sums.shape)],
        out_specs=pl.BlockSpec((modes, 64, LANES), lambda b: (0, 0, b)),
        out_shape=jax.ShapeDtypeStruct((modes, 64, elems), jnp.float32),
        compiler_params=pltpu.CompilerParams(vmem_limit_bytes=24 * MIB),
    )(r0, q0, sums)


def shifted(value, axis, steps):
    size = lax.axis_size(axis)
    return lax.ppermute(value, axis, [(i, (i + steps) % size) for i in range(size)])


def both_sides(send):
    return jnp.stack([shifted(send, "xy", -1), shifted(send, "xy", 1)])


def pad_rows(values, rows=8):
    return jnp.pad(values, ((0, rows - values.shape[0]), (0, 0)))


def edge_tables(nbr_elem, nbr_edge):
    elems = nbr_elem.shape[1]
    me, size = lax.axis_index("xy"), lax.axis_size("xy")
    wall = nbr_elem < 0
    ids = jnp.maximum(nbr_elem, 0)
    owner, local_id = ids // elems, ids % elems
    here = (owner == me) & ~wall
    after = (owner == (me + 1) % size) & ~wall & ~here
    before = ~wall & ~here & ~after
    place = jnp.where(here, nbr_edge % 4 * elems + local_id, -1).reshape(-1)
    source = jnp.arange(4 * elems, dtype=jnp.int32)[:, None]
    local = (source == place[None, :]).astype(jnp.bfloat16)
    first = jnp.arange(LANES) < ROWS

    def ends(table):
        return jnp.where(first[None, :], table[:, :LANES], table[:, elems - LANES :])

    send = jnp.where(first[None, :], before[:, :LANES], after[:, elems - LANES :])
    slot = jnp.where(after, local_id, local_id - (elems - ROWS) + ROWS)
    slot = jnp.where(send, ends(slot), -1).reshape(-1)
    far = (jnp.arange(LANES, dtype=jnp.int32)[:, None] == slot[None, :]).astype(jnp.bfloat16)
    flags = jnp.stack([wall, nbr_edge >= 4], axis=1).astype(jnp.float32)
    flags = jnp.pad(flags, ((0, 0), (0, 6), (0, 0))).reshape(32, elems)
    return local, far, pad_rows(send.astype(jnp.float32)), flags


def per_device(concentration, geometry, nbr_elem, nbr_edge, wall_flags):
    planes, _, elems = concentration.shape
    groups = lax.axis_size("gz")
    me = lax.axis_index("gz")
    total = planes * groups
    fold = Fold(elems // groups)
    scale_x, scale_y = geometry[0], geometry[1]
    jacobian = 1.0 / (scale_x * scale_y)
    geo = pad_rows(
        jnp.stack([jacobian, jacobian * scale_x * scale_x, jacobian * scale_y * scale_y])
    )
    mine = lax.dynamic_slice_in_dim(geo, me * fold.width, fold.width, axis=1)
    sent = pack(concentration, fold, groups)
    field = lax.all_to_all(sent, "gz", split_axis=0, concat_axis=0, tiled=True)
    modes_of = right_hand_side(field, jnp.tile(mine, (1, fold.parts)), fold, total)
    rhs = lax.all_to_all(modes_of, "gz", split_axis=0, concat_axis=0, tiled=True)

    mode_ids = me * planes + jnp.arange(planes, dtype=jnp.int32)
    wave = ((mode_ids + 1) // 2).astype(jnp.float32)
    mass = jnp.broadcast_to(
        (1.0 / time_step + axial_stiffness * wave * wave)[:, None], (planes, LANES)
    )
    flag = jnp.broadcast_to(wall_flags.astype(jnp.float32)[:, None], (planes, LANES))
    local, far, mask, edges = edge_tables(nbr_elem, nbr_edge)
    halo = both_sides(first_send(rhs, mask, fold))
    r0, q0, send, sums = first_apply(rhs, geo, mass, flag, mask, halo, far, local, edges, fold)
    packed = second_apply(q0, geo, mass, flag, both_sides(send), far, local, edges, sums)
    size = lax.axis_size("xy")
    packs = jnp.stack([packed] + [shifted(packed, "xy", k) for k in range(1, size)])
    return finish(r0, q0, packs)


def solution(mesh):
    return jax.shard_map(
        per_device,
        mesh=mesh,
        in_specs=(P("gz", None, "xy"), P(None, "xy"), P(None, "xy"), P(None, "xy"), P("gz")),
        out_specs=P("gz", None, "xy"),
        check_vma=False,
    )
```

```python
import functools

import jax
import jax.numpy as jnp
import ml_dtypes
import numpy as np
from jax import lax
from jax.experimental import pallas as pl
from jax.experimental.pallas import tpu as pltpu
from jax.sharding import PartitionSpec as P

ROWS = 64
LANES = 128
MIB = 1024 * 1024

time_step = 0.2
axial_stiffness = 0.002
plane_stiffness = 1.0
edge_penalty = 4.0
axial_mobility = 0.002
mobility_floor = 0.05


def point_tables():
    degree = 7
    points = np.arange(degree + 1)
    theta = np.pi * points / degree
    nodes_x = np.cos(theta)
    signs = np.where((points == 0) | (points == degree), 2.0, 1.0) * (-1.0) ** points
    differ = nodes_x[:, None] - nodes_x[None, :]
    deriv = np.outer(signs, 1.0 / signs) / (differ + np.eye(degree + 1))
    deriv = deriv - np.eye(degree + 1) * deriv.sum(axis=1)[:, None]
    inner = np.ones(degree - 1)
    for number in range(1, (degree - 1) // 2 + 1):
        inner = inner - 2.0 * np.cos(2 * number * theta[1:degree]) / (4 * number * number - 1)
    weights = np.zeros(degree + 1)
    weights[1:degree] = 2.0 * inner / degree
    weights[0] = 1.0 / degree**2
    weights[degree] = 1.0 / degree**2
    return (deriv, weights)


def fourier_table(length):
    planes = np.arange(length)
    wave_no = (planes + 1) // 2
    phase = np.outer(wave_no, planes) % length * (2.0 * np.pi / length)
    table = np.where((planes % 2 == 1)[:, None], np.cos(phase), np.sin(phase)) * np.sqrt(
        2.0 / length
    )
    table[0] = 1.0 / np.sqrt(length)
    table[length - 1] = np.cos(phase[length - 1]) / np.sqrt(length)
    return table


DERIV, WEIGHTS = point_tables()
BACK = DERIV.T * WEIGHTS[None, :]
STIFF = BACK @ DERIV
BACK_SCALED = BACK / WEIGHTS[:, None]


def two_parts(table):
    upper = table.astype(np.float32).astype(ml_dtypes.bfloat16)
    lower = (table - upper.astype(np.float64)).astype(np.float32).astype(ml_dtypes.bfloat16)
    return upper, lower


def split(value):
    upper = value.astype(jnp.bfloat16)
    lower = (value - upper.astype(jnp.float32)).astype(jnp.bfloat16)
    return upper, lower


class Fold:
    def __init__(self, width):
        self.width = width
        self.parts = LANES // width
        self.fold_j = 2 if self.parts >= 2 else 1
        self.fold_i = 2 if self.parts >= 4 else 1
        self.count_j = 8 // self.fold_j
        self.count_i = 8 // self.fold_i
        self.slots = self.count_j * self.count_i

    def slot(self, jp, ip):
        return jp * self.count_i + ip

    def node(self, jp, ip, part):
        half_j, half_i = part // self.fold_i, part % self.fold_i
        j = 7 - jp if half_j else jp
        i = 7 - ip if half_i else ip
        return 8 * j + i

    def place(self, node):
        j, i = node // 8, node % 8
        half_j = 1 if j >= self.count_j else 0
        half_i = 1 if i >= self.count_i else 0
        jp = 7 - j if half_j else j
        ip = 7 - i if half_i else i
        return self.slot(jp, ip), half_j * self.fold_i + half_i


def lane_of(shape):
    return lax.broadcasted_iota(jnp.int32, shape, len(shape) - 1)


def rolled(value, lanes):
    lanes = lanes % LANES
    return value if lanes == 0 else pltpu.roll(value, lanes, value.ndim - 1)


def by_part(values, lane, width):
    out = values[0]
    for r in range(1, len(values)):
        out = jnp.where(lane >= r * width, values[r], out)
    return out


def mirrored(value, lane, shift):
    if 2 * shift == LANES:
        return rolled(value, shift)
    return jnp.where((lane & shift) == 0, rolled(value, -shift), rolled(value, shift))


def combine(coefs, values):
    total = None
    for c, v in zip(coefs, values):
        term = v * np.float32(c)
        total = term if total is None else total + term
    return total


def line_apply(matrix, values, sign):
    even = [values[k] + values[7 - k] for k in range(4)]
    odd = [values[k] - values[7 - k] for k in range(4)]
    out = [None] * 8
    for a in range(4):
        from_even = combine([(matrix[a, b] + matrix[a, 7 - b]) / 2 for b in range(4)], even)
        from_odd = combine([(matrix[a, b] - matrix[a, 7 - b]) / 2 for b in range(4)], odd)
        out[a] = from_even + from_odd
        out[7 - a] = from_even - from_odd if sign > 0 else from_odd - from_even
    return out


def derivative_line(matrix, values, back, swap):
    if swap is None:
        return line_apply(matrix, values, -1)
    other = [swap(v) for v in values]
    sign = -1.0 if back else 1.0
    out = []
    for a in range(4):
        coefs = [matrix[a, b] for b in range(4)] + [sign * matrix[a, 7 - b] for b in range(4)]
        out.append(combine(coefs, list(values) + other))
    return out


EDGE_NODES = [
    [t for t in range(8)],
    [8 * t + 7 for t in range(8)],
    [56 + t for t in range(8)],
    [8 * t for t in range(8)],
]


def swapped(me, values):
    bit = 1
    while bit < len(values):
        flip = (me & bit) != 0
        values = [jnp.where(flip, values[r ^ bit], values[r]) for r in range(len(values))]
        bit *= 2
    return values


def pack_kernel(fold, me_ref, c_ref, *out_refs):
    lane = lane_of((c_ref.shape[0], LANES))
    me = me_ref[0]
    for step in range(len(out_refs) // fold.parts):

        @pl.when(pl.program_id(0) == step)
        def _():
            for jp in range(fold.count_j):
                for ip in range(fold.count_i):
                    loads = [c_ref[:, fold.node(jp, ip, q), :] for q in range(fold.parts)]
                    made = []
                    for r in range(fold.parts):
                        parts = [rolled(loads[q], (q - r) * fold.width) for q in range(fold.parts)]
                        made.append(by_part(parts, lane, fold.width))
                    for p, value in enumerate(swapped(me, made)):
                        out_refs[step * fold.parts + p][fold.slot(jp, ip)] = value


def pack(me, conc, fold, groups, first):
    planes, nodes, elems = conc.shape
    count = groups // 2
    offset = first // fold.parts

    def block(step, me_ref):
        return (0, 0, (step + offset) ^ (me_ref[0] // fold.parts))

    slot = jax.ShapeDtypeStruct((fold.slots, planes, LANES), jnp.float32)
    return pl.pallas_call(
        functools.partial(pack_kernel, fold),
        grid_spec=pltpu.PrefetchScalarGridSpec(
            num_scalar_prefetch=1,
            grid=(count // fold.parts,),
            in_specs=[pl.BlockSpec((planes, nodes, LANES), block)],
            out_specs=[pl.BlockSpec(slot.shape, lambda s, me_ref: (0, 0, 0))] * count,
        ),
        out_shape=[slot] * count,
        compiler_params=pltpu.CompilerParams(vmem_limit_bytes=60 * MIB),
        cost_estimate=pl.CostEstimate(
            flops=conc.size, bytes_accessed=4 * conc.size, transcendentals=0
        ),
    )(me, conc)


def plane_terms(fold, y_ref, geo_ref, x_ref, acc_ref, row, base, half):
    lane = lane_of((16, LANES))
    square_x = jnp.broadcast_to(geo_ref[1:2, :], (16, LANES))
    square_y = jnp.broadcast_to(geo_ref[2:3, :], (16, LANES))

    def conc(jp, ip):
        return y_ref[fold.slot(jp, ip), pl.ds(base, 16), :]

    def potential(c):
        square = c * c
        return square * c - c, jnp.maximum(1.0 - square, mobility_floor)

    def flux(fields, swap):
        pairs = [potential(c) for c in fields]
        slope = derivative_line(DERIV, [p[0] for p in pairs], False, swap)
        scaled = [s * p[1] for s, p in zip(slope, pairs)]
        return derivative_line(BACK_SCALED, scaled, True, swap), pairs

    swap_i = None
    if fold.fold_i == 2:
        swap_i = lambda v: mirrored(v, lane, fold.width)
    swap_j = None
    if fold.fold_j == 2:
        swap_j = lambda v: mirrored(v, lane, fold.width * fold.fold_i)
    for jp in range(fold.count_j):
        fields = [conc(jp, ip) for ip in range(fold.count_i)]
        result, _unused = flux(fields, swap_i)
        for ip in range(fold.count_i):
            acc_ref[fold.slot(jp, ip)] = (
                fields[ip] * np.float32(1.0 / time_step) - result[ip] * square_x
            )
    for ip in range(fold.count_i):
        fields = [conc(jp, ip) for jp in range(fold.count_j)]
        result, pairs = flux(fields, swap_j)
        for jp in range(fold.count_j):
            slot = fold.slot(jp, ip)
            explicit = acc_ref[slot] - result[jp] * square_y
            where = pl.ds((slot % 2) * LANES, LANES)
            for kind, value in enumerate((explicit, pairs[jp][0])):
                upper, lower = split(value)
                x_ref[slot // 2, pl.ds(kind * half + row, 16), where] = upper
                x_ref[slot // 2, pl.ds((2 + kind) * half + row, 16), where] = lower


def half_terms(fold, me, first, y_refs, geo_ref, x_ref, acc_ref):
    planes = y_refs[0].shape[1]
    half = len(y_refs) * planes
    for number, y_ref in enumerate(y_refs):
        place = (me ^ (first + number)) % len(y_refs)

        def chunk(part, _, y_ref=y_ref, place=place):
            base = pl.multiple_of(part * 16, 16)
            row = pl.multiple_of(place * planes + base, 16)
            plane_terms(fold, y_ref, geo_ref, x_ref, acc_ref, row, base, half)
            return 0

        lax.fori_loop(0, planes // 16, chunk, 0)


def near_kernel(fold, count, me_ref, geo_ref, *refs):
    y_refs, (x_ref, acc_ref) = refs[:count], refs[count:]
    half_terms(fold, me_ref[0], 0, y_refs, geo_ref, x_ref, acc_ref)


def far_kernel(fold, count, me_ref, geo_ref, table_ref, near_ref, *refs):
    y_refs, out_refs = refs[:count], refs[count : 3 * count]
    x_ref, acc_ref, result_ref = refs[3 * count :]
    planes = y_refs[0].shape[1]
    half = count * planes
    me = me_ref[0]
    half_terms(fold, me, count, y_refs, geo_ref, x_ref, acc_ref)
    mine = me // count
    jac = jnp.broadcast_to(geo_ref[0:1, :], (planes, LANES))

    def product(which, data):
        table = table_ref[which]
        return jnp.dot(
            table[:, : 4 * half], data, preferred_element_type=jnp.float32
        ) + jnp.dot(table[:, 4 * half :], data[: 2 * half], preferred_element_type=jnp.float32)

    for pair in range(fold.slots // 2):
        result_ref[...] = product(mine, near_ref[pair]) + product(1 - mine, x_ref[pair])
        for number, out_ref in enumerate(out_refs):
            rows = pl.ds(pl.multiple_of((me ^ number) * planes, 16), planes)
            for k in range(2):
                slot = 2 * pair + k
                jp, ip = slot // fold.count_i, slot % fold.count_i
                scale = jac * np.float32(WEIGHTS[jp] * WEIGHTS[ip])
                out_ref[slot] = result_ref[rows, k * LANES : (k + 1) * LANES] * scale


def smem():
    return pl.BlockSpec(memory_space=pltpu.SMEM)


def vmem(count):
    return [pl.BlockSpec(memory_space=pltpu.VMEM)] * count


def near_terms(me, geo, fields, fold):
    slots, planes, _ = fields[0].shape
    count = len(fields)
    size = count * fields[0].size
    return pl.pallas_call(
        functools.partial(near_kernel, fold, count),
        in_specs=[smem()] + vmem(1 + count),
        out_specs=vmem(1)[0],
        out_shape=jax.ShapeDtypeStruct(
            (slots // 2, 4 * count * planes, 2 * LANES), jnp.bfloat16
        ),
        scratch_shapes=[pltpu.VMEM((slots, 16, LANES), jnp.float32)],
        compiler_params=pltpu.CompilerParams(vmem_limit_bytes=16 * MIB),
        cost_estimate=pl.CostEstimate(
            flops=80 * size, bytes_accessed=12 * size, transcendentals=0
        ),
    )(me, geo, *fields)


def right_hand_side(me, geo, near, fields, fold):
    slots, planes, _ = fields[0].shape
    count = len(fields)
    total = 2 * count * planes
    half = total // 2
    size = count * fields[0].size
    table = fourier_table(total).astype(np.float32).astype(np.float64)
    wave = ((np.arange(total) + 1) // 2).astype(np.float64)
    upper, lower = two_parts(table)
    upper_b, lower_b = two_parts(-axial_mobility * (wave * wave)[:, None] * table)
    kinds = [upper, upper_b, upper, upper_b, lower, lower_b]
    tables = np.stack(
        [np.concatenate([k[:, h * half : (h + 1) * half] for k in kinds], axis=1) for h in (0, 1)]
    )
    slot = jax.ShapeDtypeStruct((slots, planes, LANES), jnp.float32)
    return pl.pallas_call(
        functools.partial(far_kernel, fold, count),
        in_specs=[smem()] + vmem(3 + count),
        out_specs=vmem(2 * count),
        out_shape=[slot] * (2 * count),
        scratch_shapes=[
            pltpu.VMEM(near.shape, jnp.bfloat16),
            pltpu.VMEM((slots, 16, LANES), jnp.float32),
            pltpu.VMEM((total, 2 * LANES), jnp.float32),
        ],
        compiler_params=pltpu.CompilerParams(vmem_limit_bytes=24 * MIB),
        cost_estimate=pl.CostEstimate(
            flops=12 * total * 2 * size, bytes_accessed=8 * size, transcendentals=0
        ),
    )(me, geo, jnp.asarray(tables), near, *fields)


def edge_send(mask_ref, edge, out_ref):
    for t in range(8):
        total = None
        for a in range(4):
            term = edge(a, t) * mask_ref[a : a + 1, :]
            total = term if total is None else total + term
        out_ref[t] = total


def send_from(field_ref, mask_ref, out_ref):
    modes, elems = field_ref.shape[1:]
    lane = lane_of((modes, LANES))

    def edge(a, t):
        node = EDGE_NODES[a][t]
        ends = field_ref[node, :, :LANES], field_ref[node, :, elems - LANES :]
        return jnp.where(lane < ROWS, ends[0], ends[1])

    edge_send(mask_ref, edge, out_ref)


def unpack_kernel(fold, groups, me_ref, mask_ref, *refs):
    parts, (r0_ref, send_ref) = refs[:groups], refs[groups:]
    modes = r0_ref.shape[1]
    me = me_ref[0]

    def tile(part, _):
        rows = pl.ds(pl.multiple_of(part * 8, 8), 8)
        lane = lane_of((8, LANES))
        for k in range(groups // fold.parts):
            block = k ^ (me // fold.parts)
            lanes = pl.ds(pl.multiple_of(block * LANES, LANES), LANES)
            mine = parts[k * fold.parts : (k + 1) * fold.parts]
            for jp in range(fold.count_j):
                for ip in range(fold.count_i):
                    loads = swapped(me, [ref[fold.slot(jp, ip), rows, :] for ref in mine])
                    for q in range(fold.parts):
                        shifts = [
                            rolled(loads[r], (r - q) * fold.width) for r in range(fold.parts)
                        ]
                        value = by_part(shifts, lane, fold.width)
                        r0_ref[fold.node(jp, ip, q), rows, lanes] = value
        return 0

    lax.fori_loop(0, modes // 8, tile, 0)
    send_from(r0_ref, mask_ref, send_ref)


def unpack(me, mask, parts, fold):
    slots, modes, _ = parts[0].shape
    groups = len(parts)
    elems = groups * fold.width
    size = groups * parts[0].size
    return pl.pallas_call(
        functools.partial(unpack_kernel, fold, groups),
        in_specs=[smem()] + vmem(1 + groups),
        out_specs=vmem(2),
        out_shape=[
            jax.ShapeDtypeStruct((64, modes, elems), jnp.float32),
            jax.ShapeDtypeStruct((8, modes, LANES), jnp.float32),
        ],
        compiler_params=pltpu.CompilerParams(vmem_limit_bytes=4 * MIB),
        cost_estimate=pl.CostEstimate(flops=8 * size, bytes_accessed=8 * size, transcendentals=0),
    )(me, mask, *parts)


def volume_kernel(want_image, field_ref, geo_ref, mass_ref, *refs):
    if want_image:
        image_ref, sums_ref, acc_ref = refs
    else:
        sums_ref, acc_ref = refs
    modes, elems = field_ref.shape[1:]
    sums_ref[...] = jnp.zeros_like(sums_ref)
    tiles = modes // 8

    def tile(number, _):
        rows = pl.ds(pl.multiple_of(number % tiles * 8, 8), 8)
        lanes = pl.ds(pl.multiple_of(number // tiles * LANES, LANES), LANES)
        jac = geo_ref[0:1, lanes] * mass_ref[rows, :]
        square_x = jnp.broadcast_to(geo_ref[0:1, lanes] * geo_ref[1:2, lanes], (8, LANES))
        square_y = jnp.broadcast_to(geo_ref[0:1, lanes] * geo_ref[2:3, lanes], (8, LANES))
        stiff = plane_stiffness * STIFF
        for j in range(8):
            values = [field_ref[8 * j + i, rows, lanes] for i in range(8)]
            result = line_apply(stiff, values, 1)
            scale = square_x * np.float32(WEIGHTS[j])
            mass = jac * np.float32(WEIGHTS[j])
            for i in range(8):
                acc_ref[8 * j + i] = result[i] * scale + (mass * np.float32(WEIGHTS[i])) * values[i]
        totals = [None, None]
        for i in range(8):
            values = [field_ref[8 * j + i, rows, lanes] for j in range(8)]
            result = line_apply(stiff, values, 1)
            scale = square_y * np.float32(WEIGHTS[i])
            for j in range(8):
                image = acc_ref[8 * j + i] + result[j] * scale
                if want_image:
                    image_ref[8 * j + i, rows, lanes] = image
                for k, term in enumerate((values[j] * values[j], values[j] * image)):
                    totals[k] = term if totals[k] is None else totals[k] + term
        for k in range(2):
            sums_ref[k, rows, :] += totals[k]
        return 0

    lax.fori_loop(0, tiles * (elems // LANES), tile, 0)


def volume(field, geo, mass, want_image):
    _, modes, elems = field.shape
    sums = jax.ShapeDtypeStruct((2, modes, LANES), jnp.float32)
    shapes = [jax.ShapeDtypeStruct(field.shape, jnp.float32), sums] if want_image else [sums]
    return pl.pallas_call(
        functools.partial(volume_kernel, want_image),
        in_specs=vmem(3),
        out_specs=vmem(len(shapes)),
        out_shape=shapes,
        scratch_shapes=[pltpu.VMEM((64, 8, LANES), jnp.float32)],
        compiler_params=pltpu.CompilerParams(vmem_limit_bytes=4 * MIB),
        cost_estimate=pl.CostEstimate(
            flops=40 * field.size, bytes_accessed=8 * field.size, transcendentals=0
        ),
    )(field, geo, mass)


def gather_edges(
    field_ref, flag_ref, after_ref, before_ref, far_ref, local_ref, edges_ref, scratch, visit
):
    trace_ref, parts_ref, val_ref = scratch
    modes, elems = field_ref.shape[1:]
    rows = 8 * modes
    lane = lane_of((modes, LANES))
    for a in range(4):
        for t in range(8):
            upper, lower = split(field_ref[EDGE_NODES[a][t]])
            where = pl.ds(a * elems, elems)
            trace_ref[pl.ds(t * modes, modes), where] = upper
            trace_ref[pl.ds((8 + t) * modes, modes), where] = lower
    for t in range(8):
        upper, lower = split(jnp.where(lane < ROWS, after_ref[t], before_ref[t]))
        parts_ref[pl.ds(t * modes, modes), :] = upper
        parts_ref[pl.ds((8 + t) * modes, modes), :] = lower
    for edge in range(4):
        mine = slice(edge * elems, (edge + 1) * elems)
        value = jnp.dot(trace_ref[...], local_ref[:, mine], preferred_element_type=jnp.float32)
        val_ref[...] = (value[:rows] + value[rows:]).reshape(8, modes, elems)
        mine = slice(edge * LANES, (edge + 1) * LANES)
        value = jnp.dot(parts_ref[...], far_ref[:, mine], preferred_element_type=jnp.float32)
        far = (value[:rows] + value[rows:]).reshape(8, modes, LANES)
        wide = lane_of(far.shape)
        val_ref[:, :, :LANES] += jnp.where(wide < ROWS, far, 0.0)
        val_ref[:, :, elems - LANES :] += jnp.where(wide < ROWS, 0.0, far)
        for block in range(elems // LANES):
            lanes = pl.ds(block * LANES, LANES)
            wall = edges_ref[8 * edge : 8 * edge + 1, lanes]
            turned = edges_ref[8 * edge + 1 : 8 * edge + 2, lanes]
            turned = jnp.broadcast_to(turned, (modes, LANES)) > 0.5
            coef = 1.0 - wall * (1.0 - flag_ref[...])
            for t in range(8):
                node = EDGE_NODES[edge][t]
                value = field_ref[node, :, lanes]
                other = jnp.where(turned, val_ref[7 - t, :, lanes], val_ref[t, :, lanes])
                weight = np.float32(edge_penalty * WEIGHTS[t])
                visit(node, lanes, value, weight * (coef * value - other))


def gather_scratch(modes, elems):
    return [
        pltpu.VMEM((16 * modes, 4 * elems), jnp.bfloat16),
        pltpu.VMEM((16 * modes, LANES), jnp.bfloat16),
        pltpu.VMEM((8, modes, elems), jnp.float32),
    ]


def first_edges_kernel(
    q_ref,
    sums_ref,
    mask_ref,
    r0_ref,
    flag_ref,
    after_ref,
    before_ref,
    far_ref,
    local_ref,
    edges_ref,
    q0_ref,
    send_ref,
    out_ref,
    *scratch,
):
    totals = [sums_ref[1]]
    q0_ref[...] = q_ref[...]

    def visit(node, lanes, value, term):
        q0_ref[node, :, lanes] += term
        totals[0] = totals[0] + value * term

    gather_edges(
        r0_ref, flag_ref, after_ref, before_ref, far_ref, local_ref, edges_ref, scratch, visit
    )
    out_ref[0] = sums_ref[0]
    out_ref[1] = totals[0]
    send_from(q0_ref, mask_ref, send_ref)


def second_edges_kernel(
    first_ref,
    second_ref,
    q0_ref,
    flag_ref,
    after_ref,
    before_ref,
    far_ref,
    local_ref,
    edges_ref,
    out_ref,
    *scratch,
):
    totals = [second_ref[1]]

    def visit(node, lanes, value, term):
        totals[0] = totals[0] + value * term

    gather_edges(
        q0_ref, flag_ref, after_ref, before_ref, far_ref, local_ref, edges_ref, scratch, visit
    )
    modes = q0_ref.shape[1]
    lane = lane_of((modes, LANES))
    sums = [first_ref[0], first_ref[1], second_ref[0], totals[0]]
    packed = jnp.zeros((modes, LANES), jnp.float32)
    for k, value in enumerate(sums):
        packed = jnp.where(lane == k, jnp.sum(value, axis=1, keepdims=True), packed)
    out_ref[...] = packed


def edges_cost(modes, elems):
    return pl.CostEstimate(
        flops=256 * modes * elems * elems,
        bytes_accessed=8 * elems * elems * 4,
        transcendentals=0,
    )


def first_edges(image, sums, mask, field, rest):
    _, modes, elems = field.shape
    return pl.pallas_call(
        first_edges_kernel,
        in_specs=vmem(4 + len(rest)),
        out_specs=vmem(3),
        out_shape=[
            jax.ShapeDtypeStruct(field.shape, jnp.float32),
            jax.ShapeDtypeStruct((8, modes, LANES), jnp.float32),
            jax.ShapeDtypeStruct((2, modes, LANES), jnp.float32),
        ],
        scratch_shapes=gather_scratch(modes, elems),
        input_output_aliases={0: 0},
        compiler_params=pltpu.CompilerParams(vmem_limit_bytes=16 * MIB),
        cost_estimate=edges_cost(modes, elems),
    )(image, sums, mask, field, *rest)


def second_edges(first, second, field, rest):
    _, modes, elems = field.shape
    return pl.pallas_call(
        second_edges_kernel,
        in_specs=vmem(3 + len(rest)),
        out_specs=vmem(1)[0],
        out_shape=jax.ShapeDtypeStruct((modes, LANES), jnp.float32),
        scratch_shapes=gather_scratch(modes, elems),
        compiler_params=pltpu.CompilerParams(vmem_limit_bytes=16 * MIB),
        cost_estimate=edges_cost(modes, elems),
    )(first, second, field, *rest)


def finish_kernel(count, r0_ref, q0_ref, *refs):
    sum_refs, out_ref = refs[:count], refs[count]
    modes = out_ref.shape[0]
    total = sum_refs[0][...]
    for ref in sum_refs[1:]:
        total = total + ref[...]
    m0, m1, m2, m3 = [total[:, k : k + 1] for k in range(4)]
    alpha = m0 / m1
    norm = alpha * (alpha * m2) - 2.0 * (alpha * m1) + m0
    energy = m1 - 2.0 * (alpha * m2) + alpha * (alpha * m3)
    beta = norm / m0
    second = norm / (energy - beta * (norm / alpha))
    on_r = jnp.broadcast_to(alpha + second * (1.0 + beta), (modes, LANES))
    on_q = jnp.broadcast_to(second * alpha, (modes, LANES))
    for j in range(8):
        rows = slice(8 * j, 8 * j + 8)
        value = on_r * r0_ref[rows] - on_q * q0_ref[rows]
        out_ref[:, rows, :] = jnp.swapaxes(value, 0, 1)


def finish(r0, q0, sums):
    _, modes, elems = r0.shape
    field = pl.BlockSpec((64, modes, LANES), lambda b: (0, 0, b))
    small = pl.BlockSpec((modes, LANES), lambda b: (0, 0))
    return pl.pallas_call(
        functools.partial(finish_kernel, len(sums)),
        grid=(elems // LANES,),
        in_specs=[field, field] + [small] * len(sums),
        out_specs=pl.BlockSpec((modes, 64, LANES), lambda b: (0, 0, b)),
        out_shape=jax.ShapeDtypeStruct((modes, 64, elems), jnp.float32),
        compiler_params=pltpu.CompilerParams(vmem_limit_bytes=16 * MIB),
    )(r0, q0, *sums)


def shifted(value, axis, steps):
    size = lax.axis_size(axis)
    return lax.ppermute(value, axis, [(i, (i + steps) % size) for i in range(size)])


def exchanged(slots, first=0):
    size = lax.axis_size("gz")
    out = []
    for number, value in enumerate(slots):
        d = first + number
        out.append(lax.ppermute(value, "gz", [(i, i ^ d) for i in range(size)]) if d else value)
    return out


def both_sides(send):
    return [shifted(send, "xy", -1), shifted(send, "xy", 1)]


def pad_rows(values, rows=8):
    return jnp.pad(values, ((0, rows - values.shape[0]), (0, 0)))


def edge_tables(nbr_elem, nbr_edge):
    elems = nbr_elem.shape[1]
    me, size = lax.axis_index("xy"), lax.axis_size("xy")
    wall = nbr_elem < 0
    ids = jnp.maximum(nbr_elem, 0)
    owner, local_id = ids // elems, ids % elems
    here = (owner == me) & ~wall
    after = (owner == (me + 1) % size) & ~wall & ~here
    before = ~wall & ~here & ~after
    place = jnp.where(here, nbr_edge % 4 * elems + local_id, -1).reshape(-1)
    source = jnp.arange(4 * elems, dtype=jnp.int32)[:, None]
    local = (source == place[None, :]).astype(jnp.bfloat16)
    first = jnp.arange(LANES) < ROWS

    def ends(table):
        return jnp.where(first[None, :], table[:, :LANES], table[:, elems - LANES :])

    send = jnp.where(first[None, :], before[:, :LANES], after[:, elems - LANES :])
    slot = jnp.where(after, local_id, local_id - (elems - ROWS) + ROWS)
    slot = jnp.where(send, ends(slot), -1).reshape(-1)
    far = (jnp.arange(LANES, dtype=jnp.int32)[:, None] == slot[None, :]).astype(jnp.bfloat16)
    flags = jnp.stack([wall, nbr_edge >= 4], axis=1).astype(jnp.float32)
    flags = jnp.pad(flags, ((0, 0), (0, 6), (0, 0))).reshape(32, elems)
    return local, far, pad_rows(send.astype(jnp.float32)), flags


def per_device(concentration, geometry, nbr_elem, nbr_edge, wall_flags):
    planes, _, elems = concentration.shape
    groups = lax.axis_size("gz")
    me = lax.axis_index("gz")
    fold = Fold(elems // groups)
    scale_x, scale_y = geometry[0], geometry[1]
    geo = pad_rows(jnp.stack([1.0 / (scale_x * scale_y), scale_x * scale_x, scale_y * scale_y]))
    mine = lax.dynamic_slice_in_dim(geo, me * fold.width, fold.width, axis=1)
    mine = jnp.tile(mine, (1, fold.parts))
    index = me.astype(jnp.int32).reshape(1)
    near_sent = pack(index, concentration, fold, groups, 0)
    far_sent = pack(index, concentration, fold, groups, groups // 2)
    near_field = exchanged(near_sent)
    far_field = exchanged(far_sent, groups // 2)
    near = near_terms(index, mine, near_field, fold)
    parts = exchanged(right_hand_side(index, mine, near, far_field, fold))

    mode_ids = me * planes + jnp.arange(planes, dtype=jnp.int32)
    wave = ((mode_ids + 1) // 2).astype(jnp.float32)
    mass = jnp.broadcast_to(
        (1.0 / time_step + axial_stiffness * wave * wave)[:, None], (planes, LANES)
    )
    flag = jnp.broadcast_to(wall_flags.astype(jnp.float32)[:, None], (planes, LANES))
    local, far, mask, edges = edge_tables(nbr_elem, nbr_edge)
    r0, send = unpack(index, mask, parts, fold)
    image, sums = volume(r0, geo, mass, True)
    halo = both_sides(send)
    q0, send, sums = first_edges(image, sums, mask, r0, [flag, *halo, far, local, edges])
    (more,) = volume(q0, geo, mass, False)
    halo = both_sides(send)
    packed = second_edges(sums, more, q0, [flag, *halo, far, local, edges])
    size = lax.axis_size("xy")
    packs = [packed] + [shifted(packed, "xy", k) for k in range(1, size)]
    return finish(r0, q0, packs)


def solution(mesh):
    return jax.shard_map(
        per_device,
        mesh=mesh,
        in_specs=(P("gz", None, "xy"), P(None, "xy"), P(None, "xy"), P(None, "xy"), P("gz")),
        out_specs=P("gz", None, "xy"),
        check_vma=False,
    )
```

```python
import functools

import jax
import jax.numpy as jnp
import ml_dtypes
import numpy as np
from jax import lax
from jax.experimental import pallas as pl
from jax.experimental.pallas import tpu as pltpu
from jax.sharding import PartitionSpec as P

ROWS = 64
LANES = 128
MIB = 1024 * 1024

time_step = 0.2
axial_stiffness = 0.002
plane_stiffness = 1.0
edge_penalty = 4.0
axial_mobility = 0.002
mobility_floor = 0.05


def point_tables():
    degree = 7
    points = np.arange(degree + 1)
    theta = np.pi * points / degree
    nodes_x = np.cos(theta)
    signs = np.where((points == 0) | (points == degree), 2.0, 1.0) * (-1.0) ** points
    differ = nodes_x[:, None] - nodes_x[None, :]
    deriv = np.outer(signs, 1.0 / signs) / (differ + np.eye(degree + 1))
    deriv = deriv - np.eye(degree + 1) * deriv.sum(axis=1)[:, None]
    inner = np.ones(degree - 1)
    for number in range(1, (degree - 1) // 2 + 1):
        inner = inner - 2.0 * np.cos(2 * number * theta[1:degree]) / (4 * number * number - 1)
    weights = np.zeros(degree + 1)
    weights[1:degree] = 2.0 * inner / degree
    weights[0] = 1.0 / degree**2
    weights[degree] = 1.0 / degree**2
    return (deriv, weights)


def fourier_table(length):
    planes = np.arange(length)
    wave_no = (planes + 1) // 2
    phase = np.outer(wave_no, planes) % length * (2.0 * np.pi / length)
    table = np.where((planes % 2 == 1)[:, None], np.cos(phase), np.sin(phase)) * np.sqrt(
        2.0 / length
    )
    table[0] = 1.0 / np.sqrt(length)
    table[length - 1] = np.cos(phase[length - 1]) / np.sqrt(length)
    return table


DERIV, WEIGHTS = point_tables()
BACK = DERIV.T * WEIGHTS[None, :]
STIFF = BACK @ DERIV
BACK_SCALED = BACK / WEIGHTS[:, None]


def two_parts(table):
    upper = table.astype(np.float32).astype(ml_dtypes.bfloat16)
    lower = (table - upper.astype(np.float64)).astype(np.float32).astype(ml_dtypes.bfloat16)
    return upper, lower


def split(value):
    upper = value.astype(jnp.bfloat16)
    lower = (value - upper.astype(jnp.float32)).astype(jnp.bfloat16)
    return upper, lower


class Fold:
    def __init__(self, width):
        self.width = width
        self.parts = LANES // width
        self.fold_j = 2 if self.parts >= 2 else 1
        self.fold_i = 2 if self.parts >= 4 else 1
        self.count_j = 8 // self.fold_j
        self.count_i = 8 // self.fold_i
        self.slots = self.count_j * self.count_i

    def slot(self, jp, ip):
        return jp * self.count_i + ip

    def node(self, jp, ip, part):
        half_j, half_i = part // self.fold_i, part % self.fold_i
        j = 7 - jp if half_j else jp
        i = 7 - ip if half_i else ip
        return 8 * j + i

    def place(self, node):
        j, i = node // 8, node % 8
        half_j = 1 if j >= self.count_j else 0
        half_i = 1 if i >= self.count_i else 0
        jp = 7 - j if half_j else j
        ip = 7 - i if half_i else i
        return self.slot(jp, ip), half_j * self.fold_i + half_i


def lane_of(shape):
    return lax.broadcasted_iota(jnp.int32, shape, len(shape) - 1)


def rolled(value, lanes):
    lanes = lanes % LANES
    return value if lanes == 0 else pltpu.roll(value, lanes, value.ndim - 1)


def by_part(values, lane, width):
    out = values[0]
    for r in range(1, len(values)):
        out = jnp.where(lane >= r * width, values[r], out)
    return out


def mirrored(value, lane, shift):
    if 2 * shift == LANES:
        return rolled(value, shift)
    return jnp.where((lane & shift) == 0, rolled(value, -shift), rolled(value, shift))


def combine(coefs, values):
    total = None
    for c, v in zip(coefs, values):
        term = v * np.float32(c)
        total = term if total is None else total + term
    return total


def line_apply(matrix, values, sign):
    even = [values[k] + values[7 - k] for k in range(4)]
    odd = [values[k] - values[7 - k] for k in range(4)]
    out = [None] * 8
    for a in range(4):
        from_even = combine([(matrix[a, b] + matrix[a, 7 - b]) / 2 for b in range(4)], even)
        from_odd = combine([(matrix[a, b] - matrix[a, 7 - b]) / 2 for b in range(4)], odd)
        out[a] = from_even + from_odd
        out[7 - a] = from_even - from_odd if sign > 0 else from_odd - from_even
    return out


def derivative_line(matrix, values, back, swap):
    if swap is None:
        return line_apply(matrix, values, -1)
    other = [swap(v) for v in values]
    sign = -1.0 if back else 1.0
    out = []
    for a in range(4):
        coefs = [matrix[a, b] for b in range(4)] + [sign * matrix[a, 7 - b] for b in range(4)]
        out.append(combine(coefs, list(values) + other))
    return out


EDGE_NODES = [
    [t for t in range(8)],
    [8 * t + 7 for t in range(8)],
    [56 + t for t in range(8)],
    [8 * t for t in range(8)],
]


def swapped(me, values):
    bit = 1
    while bit < len(values):
        flip = (me & bit) != 0
        values = [jnp.where(flip, values[r ^ bit], values[r]) for r in range(len(values))]
        bit *= 2
    return values


def pack_kernel(fold, me_ref, c_ref, *out_refs):
    lane = lane_of((c_ref.shape[0], LANES))
    me = me_ref[0]
    for step in range(len(out_refs) // fold.parts):

        @pl.when(pl.program_id(0) == step)
        def _():
            by_node = jnp.swapaxes(c_ref[...], 0, 1)
            for jp in range(fold.count_j):
                for ip in range(fold.count_i):
                    loads = [by_node[fold.node(jp, ip, q)] for q in range(fold.parts)]
                    made = []
                    for r in range(fold.parts):
                        parts = [rolled(loads[q], (q - r) * fold.width) for q in range(fold.parts)]
                        made.append(by_part(parts, lane, fold.width))
                    for p, value in enumerate(swapped(me, made)):
                        out_refs[step * fold.parts + p][fold.slot(jp, ip)] = value


def pack(me, conc, fold, groups, first):
    planes, nodes, elems = conc.shape
    count = groups // 2
    offset = first // fold.parts

    def block(step, me_ref):
        return (0, 0, (step + offset) ^ (me_ref[0] // fold.parts))

    slot = jax.ShapeDtypeStruct((fold.slots, planes, LANES), jnp.float32)
    return pl.pallas_call(
        functools.partial(pack_kernel, fold),
        grid_spec=pltpu.PrefetchScalarGridSpec(
            num_scalar_prefetch=1,
            grid=(count // fold.parts,),
            in_specs=[pl.BlockSpec((planes, nodes, LANES), block)],
            out_specs=[pl.BlockSpec(slot.shape, lambda s, me_ref: (0, 0, 0))] * count,
        ),
        out_shape=[slot] * count,
        compiler_params=pltpu.CompilerParams(vmem_limit_bytes=60 * MIB),
        cost_estimate=pl.CostEstimate(
            flops=conc.size, bytes_accessed=4 * conc.size, transcendentals=0
        ),
    )(me, conc)


def plane_terms(fold, y_ref, geo_ref, x_ref, acc_ref, row, base, half):
    lane = lane_of((16, LANES))
    square_x = jnp.broadcast_to(geo_ref[1:2, :], (16, LANES))
    square_y = jnp.broadcast_to(geo_ref[2:3, :], (16, LANES))

    def conc(jp, ip):
        return y_ref[fold.slot(jp, ip), pl.ds(base, 16), :]

    def potential(c):
        square = c * c
        return square * c - c, jnp.maximum(1.0 - square, mobility_floor)

    def flux(fields, swap):
        pairs = [potential(c) for c in fields]
        slope = derivative_line(DERIV, [p[0] for p in pairs], False, swap)
        scaled = [s * p[1] for s, p in zip(slope, pairs)]
        return derivative_line(BACK_SCALED, scaled, True, swap), pairs

    swap_i = None
    if fold.fold_i == 2:
        swap_i = lambda v: mirrored(v, lane, fold.width)
    swap_j = None
    if fold.fold_j == 2:
        swap_j = lambda v: mirrored(v, lane, fold.width * fold.fold_i)
    for jp in range(fold.count_j):
        fields = [conc(jp, ip) for ip in range(fold.count_i)]
        result, _unused = flux(fields, swap_i)
        for ip in range(fold.count_i):
            acc_ref[fold.slot(jp, ip)] = (
                fields[ip] * np.float32(1.0 / time_step) - result[ip] * square_x
            )
    for ip in range(fold.count_i):
        fields = [conc(jp, ip) for jp in range(fold.count_j)]
        result, pairs = flux(fields, swap_j)
        for jp in range(fold.count_j):
            slot = fold.slot(jp, ip)
            explicit = acc_ref[slot] - result[jp] * square_y
            where = pl.ds((slot % 2) * LANES, LANES)
            for kind, value in enumerate((explicit, pairs[jp][0])):
                upper, lower = split(value)
                x_ref[slot // 2, pl.ds(kind * half + row, 16), where] = upper
                x_ref[slot // 2, pl.ds((2 + kind) * half + row, 16), where] = lower


def half_terms(fold, me, first, y_refs, geo_ref, x_ref, acc_ref):
    planes = y_refs[0].shape[1]
    half = len(y_refs) * planes
    for number, y_ref in enumerate(y_refs):
        place = (me ^ (first + number)) % len(y_refs)

        def chunk(part, _, y_ref=y_ref, place=place):
            base = pl.multiple_of(part * 16, 16)
            row = pl.multiple_of(place * planes + base, 16)
            plane_terms(fold, y_ref, geo_ref, x_ref, acc_ref, row, base, half)
            return 0

        lax.fori_loop(0, planes // 16, chunk, 0)


def near_kernel(fold, count, me_ref, geo_ref, *refs):
    y_refs, (x_ref, acc_ref) = refs[:count], refs[count:]
    half_terms(fold, me_ref[0], 0, y_refs, geo_ref, x_ref, acc_ref)


def far_kernel(fold, count, me_ref, geo_ref, table_ref, near_ref, *refs):
    y_refs, out_refs = refs[:count], refs[count : 3 * count]
    x_ref, acc_ref, result_ref = refs[3 * count :]
    planes = y_refs[0].shape[1]
    half = count * planes
    me = me_ref[0]
    half_terms(fold, me, count, y_refs, geo_ref, x_ref, acc_ref)
    mine = me // count
    jac = jnp.broadcast_to(geo_ref[0:1, :], (planes, LANES))

    def product(which, data):
        table = table_ref[which]
        return jnp.dot(
            table[:, : 4 * half], data, preferred_element_type=jnp.float32
        ) + jnp.dot(table[:, 4 * half :], data[: 2 * half], preferred_element_type=jnp.float32)

    for pair in range(fold.slots // 2):
        result_ref[...] = product(mine, near_ref[pair]) + product(1 - mine, x_ref[pair])
        for number, out_ref in enumerate(out_refs):
            rows = pl.ds(pl.multiple_of((me ^ number) * planes, 16), planes)
            for k in range(2):
                slot = 2 * pair + k
                jp, ip = slot // fold.count_i, slot % fold.count_i
                scale = jac * np.float32(WEIGHTS[jp] * WEIGHTS[ip])
                out_ref[slot] = result_ref[rows, k * LANES : (k + 1) * LANES] * scale


def smem():
    return pl.BlockSpec(memory_space=pltpu.SMEM)


def vmem(count):
    return [pl.BlockSpec(memory_space=pltpu.VMEM)] * count


def near_terms(me, geo, fields, fold):
    slots, planes, _ = fields[0].shape
    count = len(fields)
    size = count * fields[0].size
    return pl.pallas_call(
        functools.partial(near_kernel, fold, count),
        in_specs=[smem()] + vmem(1 + count),
        out_specs=vmem(1)[0],
        out_shape=jax.ShapeDtypeStruct(
            (slots // 2, 4 * count * planes, 2 * LANES), jnp.bfloat16
        ),
        scratch_shapes=[pltpu.VMEM((slots, 16, LANES), jnp.float32)],
        compiler_params=pltpu.CompilerParams(vmem_limit_bytes=16 * MIB),
        cost_estimate=pl.CostEstimate(
            flops=80 * size, bytes_accessed=12 * size, transcendentals=0
        ),
    )(me, geo, *fields)


def right_hand_side(me, geo, near, fields, fold):
    slots, planes, _ = fields[0].shape
    count = len(fields)
    total = 2 * count * planes
    half = total // 2
    size = count * fields[0].size
    table = fourier_table(total).astype(np.float32).astype(np.float64)
    wave = ((np.arange(total) + 1) // 2).astype(np.float64)
    upper, lower = two_parts(table)
    upper_b, lower_b = two_parts(-axial_mobility * (wave * wave)[:, None] * table)
    kinds = [upper, upper_b, upper, upper_b, lower, lower_b]
    tables = np.stack(
        [np.concatenate([k[:, h * half : (h + 1) * half] for k in kinds], axis=1) for h in (0, 1)]
    )
    slot = jax.ShapeDtypeStruct((slots, planes, LANES), jnp.float32)
    return pl.pallas_call(
        functools.partial(far_kernel, fold, count),
        in_specs=[smem()] + vmem(3 + count),
        out_specs=vmem(2 * count),
        out_shape=[slot] * (2 * count),
        scratch_shapes=[
            pltpu.VMEM(near.shape, jnp.bfloat16),
            pltpu.VMEM((slots, 16, LANES), jnp.float32),
            pltpu.VMEM((total, 2 * LANES), jnp.float32),
        ],
        compiler_params=pltpu.CompilerParams(vmem_limit_bytes=24 * MIB),
        cost_estimate=pl.CostEstimate(
            flops=12 * total * 2 * size, bytes_accessed=8 * size, transcendentals=0
        ),
    )(me, geo, jnp.asarray(tables), near, *fields)


def edge_send(mask_ref, edge, out_ref):
    for t in range(8):
        total = None
        for a in range(4):
            term = edge(a, t) * mask_ref[a : a + 1, :]
            total = term if total is None else total + term
        out_ref[t] = total


def send_from(field_ref, mask_ref, out_ref):
    modes, elems = field_ref.shape[1:]
    lane = lane_of((modes, LANES))

    def edge(a, t):
        node = EDGE_NODES[a][t]
        ends = field_ref[node, :, :LANES], field_ref[node, :, elems - LANES :]
        return jnp.where(lane < ROWS, ends[0], ends[1])

    edge_send(mask_ref, edge, out_ref)


def unpack_kernel(fold, groups, me_ref, mask_ref, *refs):
    parts, (r0_ref, send_ref) = refs[:groups], refs[groups:]
    modes = r0_ref.shape[1]
    me = me_ref[0]

    def tile(part, _):
        rows = pl.ds(pl.multiple_of(part * 8, 8), 8)
        lane = lane_of((8, LANES))
        for k in range(groups // fold.parts):
            block = k ^ (me // fold.parts)
            lanes = pl.ds(pl.multiple_of(block * LANES, LANES), LANES)
            mine = parts[k * fold.parts : (k + 1) * fold.parts]
            for jp in range(fold.count_j):
                for ip in range(fold.count_i):
                    loads = swapped(me, [ref[fold.slot(jp, ip), rows, :] for ref in mine])
                    for q in range(fold.parts):
                        shifts = [
                            rolled(loads[r], (r - q) * fold.width) for r in range(fold.parts)
                        ]
                        value = by_part(shifts, lane, fold.width)
                        r0_ref[fold.node(jp, ip, q), rows, lanes] = value
        return 0

    lax.fori_loop(0, modes // 8, tile, 0)
    send_from(r0_ref, mask_ref, send_ref)


def unpack(me, mask, parts, fold):
    slots, modes, _ = parts[0].shape
    groups = len(parts)
    elems = groups * fold.width
    size = groups * parts[0].size
    return pl.pallas_call(
        functools.partial(unpack_kernel, fold, groups),
        in_specs=[smem()] + vmem(1 + groups),
        out_specs=vmem(2),
        out_shape=[
            jax.ShapeDtypeStruct((64, modes, elems), jnp.float32),
            jax.ShapeDtypeStruct((8, modes, LANES), jnp.float32),
        ],
        compiler_params=pltpu.CompilerParams(vmem_limit_bytes=4 * MIB),
        cost_estimate=pl.CostEstimate(flops=8 * size, bytes_accessed=8 * size, transcendentals=0),
    )(me, mask, *parts)


def volume_kernel(want_image, field_ref, geo_ref, mass_ref, *refs):
    if want_image:
        image_ref, sums_ref, acc_ref = refs
    else:
        sums_ref, acc_ref = refs
    modes, elems = field_ref.shape[1:]
    sums_ref[...] = jnp.zeros_like(sums_ref)
    tiles = modes // 8

    def tile(number, _):
        rows = pl.ds(pl.multiple_of(number % tiles * 8, 8), 8)
        lanes = pl.ds(pl.multiple_of(number // tiles * LANES, LANES), LANES)
        jac = geo_ref[0:1, lanes] * mass_ref[rows, :]
        square_x = jnp.broadcast_to(geo_ref[0:1, lanes] * geo_ref[1:2, lanes], (8, LANES))
        square_y = jnp.broadcast_to(geo_ref[0:1, lanes] * geo_ref[2:3, lanes], (8, LANES))
        stiff = plane_stiffness * STIFF
        for j in range(8):
            values = [field_ref[8 * j + i, rows, lanes] for i in range(8)]
            result = line_apply(stiff, values, 1)
            scale = square_x * np.float32(WEIGHTS[j])
            mass = jac * np.float32(WEIGHTS[j])
            for i in range(8):
                acc_ref[8 * j + i] = result[i] * scale + (mass * np.float32(WEIGHTS[i])) * values[i]
        totals = [None, None]
        for i in range(8):
            values = [field_ref[8 * j + i, rows, lanes] for j in range(8)]
            result = line_apply(stiff, values, 1)
            scale = square_y * np.float32(WEIGHTS[i])
            for j in range(8):
                image = acc_ref[8 * j + i] + result[j] * scale
                if want_image:
                    image_ref[8 * j + i, rows, lanes] = image
                for k, term in enumerate((values[j] * values[j], values[j] * image)):
                    totals[k] = term if totals[k] is None else totals[k] + term
        for k in range(2):
            sums_ref[k, rows, :] += totals[k]
        return 0

    lax.fori_loop(0, tiles * (elems // LANES), tile, 0)


def volume(field, geo, mass, want_image):
    _, modes, elems = field.shape
    sums = jax.ShapeDtypeStruct((2, modes, LANES), jnp.float32)
    shapes = [jax.ShapeDtypeStruct(field.shape, jnp.float32), sums] if want_image else [sums]
    return pl.pallas_call(
        functools.partial(volume_kernel, want_image),
        in_specs=vmem(3),
        out_specs=vmem(len(shapes)),
        out_shape=shapes,
        scratch_shapes=[pltpu.VMEM((64, 8, LANES), jnp.float32)],
        compiler_params=pltpu.CompilerParams(vmem_limit_bytes=4 * MIB),
        cost_estimate=pl.CostEstimate(
            flops=40 * field.size, bytes_accessed=8 * field.size, transcendentals=0
        ),
    )(field, geo, mass)


def gather_edges(
    field_ref, flag_ref, after_ref, before_ref, far_ref, local_ref, edges_ref, scratch, visit
):
    trace_ref, parts_ref, val_ref = scratch
    modes, elems = field_ref.shape[1:]
    rows = 8 * modes
    lane = lane_of((modes, LANES))
    for a in range(4):
        for t in range(8):
            upper, lower = split(field_ref[EDGE_NODES[a][t]])
            where = pl.ds(a * elems, elems)
            trace_ref[pl.ds(t * modes, modes), where] = upper
            trace_ref[pl.ds((8 + t) * modes, modes), where] = lower
    for t in range(8):
        upper, lower = split(jnp.where(lane < ROWS, after_ref[t], before_ref[t]))
        parts_ref[pl.ds(t * modes, modes), :] = upper
        parts_ref[pl.ds((8 + t) * modes, modes), :] = lower
    for edge in range(4):
        mine = slice(edge * elems, (edge + 1) * elems)
        value = jnp.dot(trace_ref[...], local_ref[:, mine], preferred_element_type=jnp.float32)
        val_ref[...] = (value[:rows] + value[rows:]).reshape(8, modes, elems)
        mine = slice(edge * LANES, (edge + 1) * LANES)
        value = jnp.dot(parts_ref[...], far_ref[:, mine], preferred_element_type=jnp.float32)
        far = (value[:rows] + value[rows:]).reshape(8, modes, LANES)
        wide = lane_of(far.shape)
        val_ref[:, :, :LANES] += jnp.where(wide < ROWS, far, 0.0)
        val_ref[:, :, elems - LANES :] += jnp.where(wide < ROWS, 0.0, far)
        for block in range(elems // LANES):
            lanes = pl.ds(block * LANES, LANES)
            wall = edges_ref[8 * edge : 8 * edge + 1, lanes]
            turned = edges_ref[8 * edge + 1 : 8 * edge + 2, lanes]
            turned = jnp.broadcast_to(turned, (modes, LANES)) > 0.5
            coef = 1.0 - wall * (1.0 - flag_ref[...])
            for t in range(8):
                node = EDGE_NODES[edge][t]
                value = field_ref[node, :, lanes]
                other = jnp.where(turned, val_ref[7 - t, :, lanes], val_ref[t, :, lanes])
                weight = np.float32(edge_penalty * WEIGHTS[t])
                visit(node, lanes, value, weight * (coef * value - other))


def gather_scratch(modes, elems):
    return [
        pltpu.VMEM((16 * modes, 4 * elems), jnp.bfloat16),
        pltpu.VMEM((16 * modes, LANES), jnp.bfloat16),
        pltpu.VMEM((8, modes, elems), jnp.float32),
    ]


def first_edges_kernel(
    q_ref,
    sums_ref,
    mask_ref,
    r0_ref,
    flag_ref,
    after_ref,
    before_ref,
    far_ref,
    local_ref,
    edges_ref,
    q0_ref,
    send_ref,
    out_ref,
    *scratch,
):
    totals = [sums_ref[1]]
    q0_ref[...] = q_ref[...]

    def visit(node, lanes, value, term):
        q0_ref[node, :, lanes] += term
        totals[0] = totals[0] + value * term

    gather_edges(
        r0_ref, flag_ref, after_ref, before_ref, far_ref, local_ref, edges_ref, scratch, visit
    )
    out_ref[0] = sums_ref[0]
    out_ref[1] = totals[0]
    send_from(q0_ref, mask_ref, send_ref)


def second_edges_kernel(
    first_ref,
    second_ref,
    q0_ref,
    flag_ref,
    after_ref,
    before_ref,
    far_ref,
    local_ref,
    edges_ref,
    out_ref,
    *scratch,
):
    totals = [second_ref[1]]

    def visit(node, lanes, value, term):
        totals[0] = totals[0] + value * term

    gather_edges(
        q0_ref, flag_ref, after_ref, before_ref, far_ref, local_ref, edges_ref, scratch, visit
    )
    modes = q0_ref.shape[1]
    lane = lane_of((modes, LANES))
    sums = [first_ref[0], first_ref[1], second_ref[0], totals[0]]
    packed = jnp.zeros((modes, LANES), jnp.float32)
    for k, value in enumerate(sums):
        packed = jnp.where(lane == k, jnp.sum(value, axis=1, keepdims=True), packed)
    out_ref[...] = packed


def edges_cost(modes, elems):
    return pl.CostEstimate(
        flops=256 * modes * elems * elems,
        bytes_accessed=8 * elems * elems * 4,
        transcendentals=0,
    )


def first_edges(image, sums, mask, field, rest):
    _, modes, elems = field.shape
    return pl.pallas_call(
        first_edges_kernel,
        in_specs=vmem(4 + len(rest)),
        out_specs=vmem(3),
        out_shape=[
            jax.ShapeDtypeStruct(field.shape, jnp.float32),
            jax.ShapeDtypeStruct((8, modes, LANES), jnp.float32),
            jax.ShapeDtypeStruct((2, modes, LANES), jnp.float32),
        ],
        scratch_shapes=gather_scratch(modes, elems),
        input_output_aliases={0: 0},
        compiler_params=pltpu.CompilerParams(vmem_limit_bytes=16 * MIB),
        cost_estimate=edges_cost(modes, elems),
    )(image, sums, mask, field, *rest)


def second_edges(first, second, field, rest):
    _, modes, elems = field.shape
    return pl.pallas_call(
        second_edges_kernel,
        in_specs=vmem(3 + len(rest)),
        out_specs=vmem(1)[0],
        out_shape=jax.ShapeDtypeStruct((modes, LANES), jnp.float32),
        scratch_shapes=gather_scratch(modes, elems),
        compiler_params=pltpu.CompilerParams(vmem_limit_bytes=16 * MIB),
        cost_estimate=edges_cost(modes, elems),
    )(first, second, field, *rest)


def finish_kernel(count, r0_ref, q0_ref, *refs):
    sum_refs, out_ref = refs[:count], refs[count]
    modes = out_ref.shape[0]
    total = sum_refs[0][...]
    for ref in sum_refs[1:]:
        total = total + ref[...]
    m0, m1, m2, m3 = [total[:, k : k + 1] for k in range(4)]
    alpha = m0 / m1
    norm = alpha * (alpha * m2) - 2.0 * (alpha * m1) + m0
    energy = m1 - 2.0 * (alpha * m2) + alpha * (alpha * m3)
    beta = norm / m0
    second = norm / (energy - beta * (norm / alpha))
    on_r = jnp.broadcast_to(alpha + second * (1.0 + beta), (modes, LANES))
    on_q = jnp.broadcast_to(second * alpha, (modes, LANES))
    for j in range(8):
        rows = slice(8 * j, 8 * j + 8)
        value = on_r * r0_ref[rows] - on_q * q0_ref[rows]
        out_ref[:, rows, :] = jnp.swapaxes(value, 0, 1)


def finish(r0, q0, sums):
    _, modes, elems = r0.shape
    field = pl.BlockSpec((64, modes, LANES), lambda b: (0, 0, b))
    small = pl.BlockSpec((modes, LANES), lambda b: (0, 0))
    return pl.pallas_call(
        functools.partial(finish_kernel, len(sums)),
        grid=(elems // LANES,),
        in_specs=[field, field] + [small] * len(sums),
        out_specs=pl.BlockSpec((modes, 64, LANES), lambda b: (0, 0, b)),
        out_shape=jax.ShapeDtypeStruct((modes, 64, elems), jnp.float32),
        compiler_params=pltpu.CompilerParams(vmem_limit_bytes=16 * MIB),
    )(r0, q0, *sums)


def shifted(value, axis, steps):
    size = lax.axis_size(axis)
    return lax.ppermute(value, axis, [(i, (i + steps) % size) for i in range(size)])


def exchanged(slots, first=0):
    size = lax.axis_size("gz")
    out = []
    for number, value in enumerate(slots):
        d = first + number
        out.append(lax.ppermute(value, "gz", [(i, i ^ d) for i in range(size)]) if d else value)
    return out


def both_sides(send):
    return [shifted(send, "xy", -1), shifted(send, "xy", 1)]


def pad_rows(values, rows=8):
    return jnp.pad(values, ((0, rows - values.shape[0]), (0, 0)))


def edge_tables(nbr_elem, nbr_edge):
    elems = nbr_elem.shape[1]
    me, size = lax.axis_index("xy"), lax.axis_size("xy")
    wall = nbr_elem < 0
    ids = jnp.maximum(nbr_elem, 0)
    owner, local_id = ids // elems, ids % elems
    here = (owner == me) & ~wall
    after = (owner == (me + 1) % size) & ~wall & ~here
    before = ~wall & ~here & ~after
    place = jnp.where(here, nbr_edge % 4 * elems + local_id, -1).reshape(-1)
    source = jnp.arange(4 * elems, dtype=jnp.int32)[:, None]
    local = (source == place[None, :]).astype(jnp.bfloat16)
    first = jnp.arange(LANES) < ROWS

    def ends(table):
        return jnp.where(first[None, :], table[:, :LANES], table[:, elems - LANES :])

    send = jnp.where(first[None, :], before[:, :LANES], after[:, elems - LANES :])
    slot = jnp.where(after, local_id, local_id - (elems - ROWS) + ROWS)
    slot = jnp.where(send, ends(slot), -1).reshape(-1)
    far = (jnp.arange(LANES, dtype=jnp.int32)[:, None] == slot[None, :]).astype(jnp.bfloat16)
    flags = jnp.stack([wall, nbr_edge >= 4], axis=1).astype(jnp.float32)
    flags = jnp.pad(flags, ((0, 0), (0, 6), (0, 0))).reshape(32, elems)
    return local, far, pad_rows(send.astype(jnp.float32)), flags


def per_device(concentration, geometry, nbr_elem, nbr_edge, wall_flags):
    planes, _, elems = concentration.shape
    groups = lax.axis_size("gz")
    me = lax.axis_index("gz")
    fold = Fold(elems // groups)
    scale_x, scale_y = geometry[0], geometry[1]
    geo = pad_rows(jnp.stack([1.0 / (scale_x * scale_y), scale_x * scale_x, scale_y * scale_y]))
    mine = lax.dynamic_slice_in_dim(geo, me * fold.width, fold.width, axis=1)
    mine = jnp.tile(mine, (1, fold.parts))
    index = me.astype(jnp.int32).reshape(1)
    mode_ids = me * planes + jnp.arange(planes, dtype=jnp.int32)
    wave = ((mode_ids + 1) // 2).astype(jnp.float32)
    mass = jnp.broadcast_to(
        (1.0 / time_step + axial_stiffness * wave * wave)[:, None], (planes, LANES)
    )
    flag = jnp.broadcast_to(wall_flags.astype(jnp.float32)[:, None], (planes, LANES))
    tables = edge_tables(nbr_elem, nbr_edge)
    near_sent = pack(index, concentration, fold, groups, 0)
    far_sent = pack(index, concentration, fold, groups, groups // 2)
    near_field = exchanged(near_sent)
    far_field = exchanged(far_sent, groups // 2)
    near_field, geo, mine, mass, flag, tables = lax.optimization_barrier(
        (near_field, geo, mine, mass, flag, tables)
    )
    local, far, mask, edges = tables
    near = near_terms(index, mine, near_field, fold)
    parts = exchanged(right_hand_side(index, mine, near, far_field, fold))

    r0, send = unpack(index, mask, parts, fold)
    image, sums = volume(r0, geo, mass, True)
    halo = both_sides(send)
    q0, send, sums = first_edges(image, sums, mask, r0, [flag, *halo, far, local, edges])
    (more,) = volume(q0, geo, mass, False)
    halo = both_sides(send)
    packed = second_edges(sums, more, q0, [flag, *halo, far, local, edges])
    size = lax.axis_size("xy")
    packs = [packed] + [shifted(packed, "xy", k) for k in range(1, size)]
    return finish(r0, q0, packs)


def solution(mesh):
    return jax.shard_map(
        per_device,
        mesh=mesh,
        in_specs=(P("gz", None, "xy"), P(None, "xy"), P(None, "xy"), P(None, "xy"), P("gz")),
        out_specs=P("gz", None, "xy"),
        check_vma=False,
    )
```

```python
import functools

import jax
import jax.numpy as jnp
import ml_dtypes
import numpy as np
from jax import lax
from jax.experimental import pallas as pl
from jax.experimental.pallas import tpu as pltpu
from jax.sharding import PartitionSpec as P

ROWS = 64
LANES = 128
MIB = 1024 * 1024

time_step = 0.2
axial_stiffness = 0.002
plane_stiffness = 1.0
edge_penalty = 4.0
axial_mobility = 0.002
mobility_floor = 0.05


def point_tables():
    degree = 7
    points = np.arange(degree + 1)
    theta = np.pi * points / degree
    nodes_x = np.cos(theta)
    signs = np.where((points == 0) | (points == degree), 2.0, 1.0) * (-1.0) ** points
    differ = nodes_x[:, None] - nodes_x[None, :]
    deriv = np.outer(signs, 1.0 / signs) / (differ + np.eye(degree + 1))
    deriv = deriv - np.eye(degree + 1) * deriv.sum(axis=1)[:, None]
    inner = np.ones(degree - 1)
    for number in range(1, (degree - 1) // 2 + 1):
        inner = inner - 2.0 * np.cos(2 * number * theta[1:degree]) / (4 * number * number - 1)
    weights = np.zeros(degree + 1)
    weights[1:degree] = 2.0 * inner / degree
    weights[0] = 1.0 / degree**2
    weights[degree] = 1.0 / degree**2
    return (deriv, weights)


def fourier_table(length):
    planes = np.arange(length)
    wave_no = (planes + 1) // 2
    phase = np.outer(wave_no, planes) % length * (2.0 * np.pi / length)
    table = np.where((planes % 2 == 1)[:, None], np.cos(phase), np.sin(phase)) * np.sqrt(
        2.0 / length
    )
    table[0] = 1.0 / np.sqrt(length)
    table[length - 1] = np.cos(phase[length - 1]) / np.sqrt(length)
    return table


DERIV, WEIGHTS = point_tables()
BACK = DERIV.T * WEIGHTS[None, :]
STIFF = BACK @ DERIV
BACK_SCALED = BACK / WEIGHTS[:, None]


def two_parts(table):
    upper = table.astype(np.float32).astype(ml_dtypes.bfloat16)
    lower = (table - upper.astype(np.float64)).astype(np.float32).astype(ml_dtypes.bfloat16)
    return upper, lower


def split(value):
    upper = value.astype(jnp.bfloat16)
    lower = (value - upper.astype(jnp.float32)).astype(jnp.bfloat16)
    return upper, lower


class Fold:
    def __init__(self, width):
        self.width = width
        self.parts = LANES // width
        self.fold_j = 2 if self.parts >= 2 else 1
        self.fold_i = 2 if self.parts >= 4 else 1
        self.count_j = 8 // self.fold_j
        self.count_i = 8 // self.fold_i
        self.slots = self.count_j * self.count_i

    def slot(self, jp, ip):
        return jp * self.count_i + ip

    def node(self, jp, ip, part):
        half_j, half_i = part // self.fold_i, part % self.fold_i
        j = 7 - jp if half_j else jp
        i = 7 - ip if half_i else ip
        return 8 * j + i

    def place(self, node):
        j, i = node // 8, node % 8
        half_j = 1 if j >= self.count_j else 0
        half_i = 1 if i >= self.count_i else 0
        jp = 7 - j if half_j else j
        ip = 7 - i if half_i else i
        return self.slot(jp, ip), half_j * self.fold_i + half_i


def lane_of(shape):
    return lax.broadcasted_iota(jnp.int32, shape, len(shape) - 1)


def rolled(value, lanes):
    lanes = lanes % LANES
    return value if lanes == 0 else pltpu.roll(value, lanes, value.ndim - 1)


def by_part(values, lane, width):
    out = values[0]
    for r in range(1, len(values)):
        out = jnp.where(lane >= r * width, values[r], out)
    return out


def mirrored(value, lane, shift):
    if 2 * shift == LANES:
        return rolled(value, shift)
    return jnp.where((lane & shift) == 0, rolled(value, -shift), rolled(value, shift))


def combine(coefs, values):
    total = None
    for c, v in zip(coefs, values):
        term = v * np.float32(c)
        total = term if total is None else total + term
    return total


def line_apply(matrix, values, sign):
    even = [values[k] + values[7 - k] for k in range(4)]
    odd = [values[k] - values[7 - k] for k in range(4)]
    out = [None] * 8
    for a in range(4):
        from_even = combine([(matrix[a, b] + matrix[a, 7 - b]) / 2 for b in range(4)], even)
        from_odd = combine([(matrix[a, b] - matrix[a, 7 - b]) / 2 for b in range(4)], odd)
        out[a] = from_even + from_odd
        out[7 - a] = from_even - from_odd if sign > 0 else from_odd - from_even
    return out


def derivative_line(matrix, values, back, swap):
    if swap is None:
        return line_apply(matrix, values, -1)
    other = [swap(v) for v in values]
    sign = -1.0 if back else 1.0
    out = []
    for a in range(4):
        coefs = [matrix[a, b] for b in range(4)] + [sign * matrix[a, 7 - b] for b in range(4)]
        out.append(combine(coefs, list(values) + other))
    return out


EDGE_NODES = [
    [t for t in range(8)],
    [8 * t + 7 for t in range(8)],
    [56 + t for t in range(8)],
    [8 * t for t in range(8)],
]


def swapped(me, values):
    bit = 1
    while bit < len(values):
        flip = (me & bit) != 0
        values = [jnp.where(flip, values[r ^ bit], values[r]) for r in range(len(values))]
        bit *= 2
    return values


def pack_kernel(fold, me_ref, c_ref, *out_refs):
    lane = lane_of((c_ref.shape[0], LANES))
    me = me_ref[0]
    for step in range(len(out_refs) // fold.parts):

        @pl.when(pl.program_id(0) == step)
        def _():
            by_node = jnp.swapaxes(c_ref[...], 0, 1)
            for jp in range(fold.count_j):
                for ip in range(fold.count_i):
                    loads = [by_node[fold.node(jp, ip, q)] for q in range(fold.parts)]
                    made = []
                    for r in range(fold.parts):
                        parts = [rolled(loads[q], (q - r) * fold.width) for q in range(fold.parts)]
                        made.append(by_part(parts, lane, fold.width))
                    for p, value in enumerate(swapped(me, made)):
                        out_refs[step * fold.parts + p][fold.slot(jp, ip)] = value


def pack(me, conc, fold, groups, first):
    planes, nodes, elems = conc.shape
    count = groups // 2
    offset = first // fold.parts

    def block(step, me_ref):
        return (0, 0, (step + offset) ^ (me_ref[0] // fold.parts))

    slot = jax.ShapeDtypeStruct((fold.slots, planes, LANES), jnp.float32)
    return pl.pallas_call(
        functools.partial(pack_kernel, fold),
        grid_spec=pltpu.PrefetchScalarGridSpec(
            num_scalar_prefetch=1,
            grid=(count // fold.parts,),
            in_specs=[pl.BlockSpec((planes, nodes, LANES), block)],
            out_specs=[pl.BlockSpec(slot.shape, lambda s, me_ref: (0, 0, 0))] * count,
        ),
        out_shape=[slot] * count,
        compiler_params=pltpu.CompilerParams(vmem_limit_bytes=60 * MIB),
        cost_estimate=pl.CostEstimate(
            flops=conc.size, bytes_accessed=4 * conc.size, transcendentals=0
        ),
    )(me, conc)


def plane_terms(fold, y_ref, geo_ref, x_ref, acc_ref, row, base, half):
    lane = lane_of((16, LANES))
    square_x = jnp.broadcast_to(geo_ref[1:2, :], (16, LANES))
    square_y = jnp.broadcast_to(geo_ref[2:3, :], (16, LANES))

    def conc(jp, ip):
        return y_ref[fold.slot(jp, ip), pl.ds(base, 16), :]

    def potential(c):
        square = c * c
        return square * c - c, jnp.maximum(1.0 - square, mobility_floor)

    def flux(fields, swap):
        pairs = [potential(c) for c in fields]
        slope = derivative_line(DERIV, [p[0] for p in pairs], False, swap)
        scaled = [s * p[1] for s, p in zip(slope, pairs)]
        return derivative_line(BACK_SCALED, scaled, True, swap), pairs

    swap_i = None
    if fold.fold_i == 2:
        swap_i = lambda v: mirrored(v, lane, fold.width)
    swap_j = None
    if fold.fold_j == 2:
        swap_j = lambda v: mirrored(v, lane, fold.width * fold.fold_i)
    for jp in range(fold.count_j):
        fields = [conc(jp, ip) for ip in range(fold.count_i)]
        result, _unused = flux(fields, swap_i)
        for ip in range(fold.count_i):
            acc_ref[fold.slot(jp, ip)] = (
                fields[ip] * np.float32(1.0 / time_step) - result[ip] * square_x
            )
    for ip in range(fold.count_i):
        fields = [conc(jp, ip) for jp in range(fold.count_j)]
        result, pairs = flux(fields, swap_j)
        for jp in range(fold.count_j):
            slot = fold.slot(jp, ip)
            explicit = acc_ref[slot] - result[jp] * square_y
            where = pl.ds((slot % 2) * LANES, LANES)
            for kind, value in enumerate((explicit, pairs[jp][0])):
                upper, lower = split(value)
                x_ref[slot // 2, pl.ds(kind * half + row, 16), where] = upper
                x_ref[slot // 2, pl.ds((2 + kind) * half + row, 16), where] = lower


def half_terms(fold, me, first, y_refs, geo_ref, x_ref, acc_ref):
    planes = y_refs[0].shape[1]
    half = len(y_refs) * planes
    for number, y_ref in enumerate(y_refs):
        place = (me ^ (first + number)) % len(y_refs)

        def chunk(part, _, y_ref=y_ref, place=place):
            base = pl.multiple_of(part * 16, 16)
            row = pl.multiple_of(place * planes + base, 16)
            plane_terms(fold, y_ref, geo_ref, x_ref, acc_ref, row, base, half)
            return 0

        lax.fori_loop(0, planes // 16, chunk, 0)


def near_kernel(fold, count, me_ref, geo_ref, *refs):
    y_refs, (x_ref, acc_ref) = refs[:count], refs[count:]
    half_terms(fold, me_ref[0], 0, y_refs, geo_ref, x_ref, acc_ref)


def far_kernel(fold, count, sizes, me_ref, geo_ref, table_ref, near_ref, *refs):
    y_refs, refs = refs[:count], refs[count:]
    chunks = len(sizes)
    out_refs = [refs[k * chunks : (k + 1) * chunks] for k in range(count)]
    x_ref, acc_ref, result_ref = refs[count * chunks :]
    half_terms(fold, me_ref[0], count, y_refs, geo_ref, x_ref, acc_ref)
    transform(fold, 1, me_ref, geo_ref, table_ref, (near_ref, x_ref), out_refs, result_ref)


def near_modes_kernel(fold, me_ref, geo_ref, table_ref, near_ref, far_ref, *refs):
    out_refs, result_ref = [[ref] for ref in refs[:-1]], refs[-1]
    transform(fold, 0, me_ref, geo_ref, table_ref, (near_ref, far_ref), out_refs, result_ref)


def transform(fold, other, me_ref, geo_ref, table_ref, terms, out_refs, result_ref):
    count = len(out_refs)
    half = result_ref.shape[0]
    planes = half // count
    me = me_ref[0]
    mine = me // count
    jac = jnp.broadcast_to(geo_ref[0:1, :], (planes, LANES))
    rows = pl.ds(pl.multiple_of((mine ^ other) * half, 16), half)

    def product(which, data):
        upper, lower = slice(0, 4 * half), slice(4 * half, 6 * half)
        return jnp.dot(
            table_ref[which, rows, upper], data, preferred_element_type=jnp.float32
        ) + jnp.dot(
            table_ref[which, rows, lower], data[: 2 * half], preferred_element_type=jnp.float32
        )

    for pair in range(fold.slots // 2):
        result_ref[...] = product(mine, terms[0][pair]) + product(1 - mine, terms[1][pair])
        for k in range(2):
            slot = 2 * pair + k
            jp, ip = slot // fold.count_i, slot % fold.count_i
            scale = jac * np.float32(WEIGHTS[jp] * WEIGHTS[ip])
            for number, pieces in enumerate(out_refs):
                start = (me ^ number) % count * planes
                for out_ref in pieces:
                    size = out_ref.shape[1]
                    here = pl.ds(pl.multiple_of(start, 8), size)
                    value = result_ref[here, k * LANES : (k + 1) * LANES]
                    out_ref[slot] = value * scale[:size]
                    start = start + size


def small_cost():
    return pl.CostEstimate(flops=1, bytes_accessed=1, transcendentals=0)


def smem():
    return pl.BlockSpec(memory_space=pltpu.SMEM)


def vmem(count):
    return [pl.BlockSpec(memory_space=pltpu.VMEM)] * count


def near_terms(me, geo, fields, fold):
    slots, planes, _ = fields[0].shape
    count = len(fields)
    size = count * fields[0].size
    return pl.pallas_call(
        functools.partial(near_kernel, fold, count),
        in_specs=[smem()] + vmem(1 + count),
        out_specs=vmem(1)[0],
        out_shape=jax.ShapeDtypeStruct(
            (slots // 2, 4 * count * planes, 2 * LANES), jnp.bfloat16
        ),
        scratch_shapes=[pltpu.VMEM((slots, 16, LANES), jnp.float32)],
        compiler_params=pltpu.CompilerParams(vmem_limit_bytes=16 * MIB),
        cost_estimate=pl.CostEstimate(
            flops=80 * size, bytes_accessed=12 * size, transcendentals=0
        ),
    )(me, geo, *fields)


def transform_tables(total):
    table = fourier_table(total).astype(np.float32).astype(np.float64)
    wave = ((np.arange(total) + 1) // 2).astype(np.float64)
    upper, lower = two_parts(table)
    upper_b, lower_b = two_parts(-axial_mobility * (wave * wave)[:, None] * table)
    kinds = [upper, upper_b, upper, upper_b, lower, lower_b]
    halves = np.split(np.stack(kinds), 2, axis=2)
    return jnp.asarray(np.stack([np.concatenate(list(half), axis=1) for half in halves]))


def far_modes(me, geo, tables, near, fields, fold, sizes):
    slots, planes, _ = fields[0].shape
    count = len(fields)
    size = count * fields[0].size
    chunks = len(sizes)
    pieces = [jax.ShapeDtypeStruct((slots, k, LANES), jnp.float32) for k in sizes]
    *outs, far = pl.pallas_call(
        functools.partial(far_kernel, fold, count, sizes),
        in_specs=[smem()] + vmem(3 + count),
        out_specs=vmem(chunks * count + 1),
        out_shape=pieces * count + [jax.ShapeDtypeStruct(near.shape, jnp.bfloat16)],
        scratch_shapes=[
            pltpu.VMEM((slots, 16, LANES), jnp.float32),
            pltpu.VMEM((count * planes, 2 * LANES), jnp.float32),
        ],
        compiler_params=pltpu.CompilerParams(vmem_limit_bytes=24 * MIB),
        cost_estimate=pl.CostEstimate(
            flops=12 * count * planes * size, bytes_accessed=8 * size, transcendentals=0
        ),
    )(me, geo, tables, near, *fields)
    return [outs[k::chunks] for k in range(chunks)], far


def near_modes(me, geo, tables, near, far, fold, planes):
    slots = fold.slots
    count = near.shape[1] // (4 * planes)
    size = count * slots * planes * LANES
    slot = jax.ShapeDtypeStruct((slots, planes, LANES), jnp.float32)
    return pl.pallas_call(
        functools.partial(near_modes_kernel, fold),
        in_specs=[smem()] + vmem(4),
        out_specs=vmem(count),
        out_shape=[slot] * count,
        scratch_shapes=[pltpu.VMEM((count * planes, 2 * LANES), jnp.float32)],
        compiler_params=pltpu.CompilerParams(vmem_limit_bytes=16 * MIB),
        cost_estimate=pl.CostEstimate(
            flops=12 * count * planes * size, bytes_accessed=8 * size, transcendentals=0
        ),
    )(me, geo, tables, near, far)


def edge_send(mask_ref, edge, write):
    for t in range(8):
        total = None
        for a in range(4):
            term = edge(a, t) * mask_ref[a : a + 1, :]
            total = term if total is None else total + term
        write(t, total)


def send_from(field_ref, mask_ref, out_ref, start):
    modes, elems = field_ref.shape[1:]
    lane = lane_of((modes, LANES))

    def edge(a, t):
        node = EDGE_NODES[a][t]
        ends = field_ref[node, :, :LANES], field_ref[node, :, elems - LANES :]
        return jnp.where(lane < ROWS, ends[0], ends[1])

    def write(t, value):
        out_ref[t, start : start + modes, :] = value

    edge_send(mask_ref, edge, write)


def unpack_kernel(fold, groups, start, me_ref, mask_ref, *refs):
    parts, (r0_ref, send_ref) = refs[:groups], refs[-2:]
    modes = r0_ref.shape[1]
    me = me_ref[0]

    def tile(part, _):
        rows = pl.ds(pl.multiple_of(part * 8, 8), 8)
        whole_rows = pl.ds(pl.multiple_of(part * 8 + start, 8), 8)

        def load(ref, slot):
            return ref[slot, rows if ref.shape[1] == modes else whole_rows, :]

        lane = lane_of((8, LANES))
        for k in range(groups // fold.parts):
            block = k ^ (me // fold.parts)
            lanes = pl.ds(pl.multiple_of(block * LANES, LANES), LANES)
            mine = parts[k * fold.parts : (k + 1) * fold.parts]
            for jp in range(fold.count_j):
                for ip in range(fold.count_i):
                    loads = swapped(me, [load(ref, fold.slot(jp, ip)) for ref in mine])
                    for q in range(fold.parts):
                        shifts = [
                            rolled(loads[r], (r - q) * fold.width) for r in range(fold.parts)
                        ]
                        value = by_part(shifts, lane, fold.width)
                        r0_ref[fold.node(jp, ip, q), rows, lanes] = value
        return 0

    lax.fori_loop(0, modes // 8, tile, 0)
    if start:
        send_ref[:, :start, :] = refs[groups][...]
    send_from(r0_ref, mask_ref, send_ref, start)


def unpack(me, mask, parts, fold, sends):
    _, modes, _ = parts[-1].shape
    groups = len(parts)
    elems = groups * fold.width
    start = sum(value.shape[1] for value in sends)
    return pl.pallas_call(
        functools.partial(unpack_kernel, fold, groups, start),
        in_specs=[smem()] + vmem(1 + groups + len(sends)),
        out_specs=vmem(2),
        out_shape=[
            jax.ShapeDtypeStruct((64, modes, elems), jnp.float32),
            jax.ShapeDtypeStruct((8, start + modes, LANES), jnp.float32),
        ],
        compiler_params=pltpu.CompilerParams(vmem_limit_bytes=4 * MIB),
        cost_estimate=small_cost(),
    )(me, mask, *parts, *sends)


def volume(field_ref, geo_ref, mass_ref, first, image_ref, sums_ref, row_of_sums, acc_ref):
    modes, elems = field_ref.shape[1:]
    tiles = modes // 8

    def tile(number, _):
        row = pl.multiple_of(number % tiles * 8, 8)
        rows = pl.ds(row, 8)
        sum_rows = pl.ds(row + row_of_sums, 8)
        lanes = pl.ds(pl.multiple_of(number // tiles * LANES, LANES), LANES)
        jac = geo_ref[0:1, lanes] * mass_ref[pl.ds(row + first, 8), :]
        square_x = jnp.broadcast_to(geo_ref[0:1, lanes] * geo_ref[1:2, lanes], (8, LANES))
        square_y = jnp.broadcast_to(geo_ref[0:1, lanes] * geo_ref[2:3, lanes], (8, LANES))
        stiff = plane_stiffness * STIFF
        for j in range(8):
            values = [field_ref[8 * j + i, rows, lanes] for i in range(8)]
            result = line_apply(stiff, values, 1)
            scale = square_x * np.float32(WEIGHTS[j])
            mass = jac * np.float32(WEIGHTS[j])
            for i in range(8):
                acc_ref[8 * j + i] = result[i] * scale + (mass * np.float32(WEIGHTS[i])) * values[i]
        totals = [None, None]
        for i in range(8):
            values = [field_ref[8 * j + i, rows, lanes] for j in range(8)]
            result = line_apply(stiff, values, 1)
            scale = square_y * np.float32(WEIGHTS[i])
            for j in range(8):
                image = acc_ref[8 * j + i] + result[j] * scale
                if image_ref is not None:
                    image_ref[8 * j + i, rows, lanes] = image
                for k, term in enumerate((values[j] * values[j], values[j] * image)):
                    totals[k] = term if totals[k] is None else totals[k] + term
        for k in range(2):
            sums_ref[k, sum_rows, :] += totals[k]
        return 0

    lax.fori_loop(0, tiles * (elems // LANES), tile, 0)


def fill_pairs(target_ref, first, modes, lanes, value_of, parts):
    total = target_ref.shape[0] // (8 * parts)
    for t in range(0, 8, 2):
        pieces = split(jnp.concatenate([value_of(t), value_of(t + 1)], axis=0))
        for part in range(parts):
            row = (8 * part + t) * total
            target_ref[pl.ds(row, 2 * total), lanes] = pieces[part]


def gathered(trace_ref, table, parts):
    value = jnp.dot(trace_ref[...], table, preferred_element_type=jnp.float32)
    if parts == 2:
        half = value.shape[0] // 2
        value = value[:half] + value[half:]
    return value.reshape(8, value.shape[0] // 8, value.shape[1])


def local_edges(fields, first, flag_ref, local_ref, edges_ref, trace_ref, val_ref, parts, visit):
    elems = val_ref.shape[2]
    for a in range(4):

        def value_of(t):
            pieces = [field_ref[EDGE_NODES[a][t]] for field_ref in fields]
            return pieces[0] if len(pieces) == 1 else jnp.concatenate(pieces, axis=0)

        fill_pairs(trace_ref, 0, 0, pl.ds(a * elems, elems), value_of, parts)
    for edge in range(4):
        val_ref[...] = gathered(
            trace_ref, local_ref[:, edge * elems : (edge + 1) * elems], parts
        )
        for block in range(elems // LANES):
            lanes = pl.ds(block * LANES, LANES)
            wall = edges_ref[8 * edge : 8 * edge + 1, lanes]
            flip = edges_ref[8 * edge + 1 : 8 * edge + 2, lanes]
            start = 0
            for chunk, field_ref in enumerate(fields):
                modes = field_ref.shape[1]
                rows = slice(start, start + modes)
                start += modes
                turned = jnp.broadcast_to(flip, (modes, LANES)) > 0.5
                coef = 1.0 - wall * (1.0 - flag_ref[first + start - modes : first + start])
                for t in range(8):
                    node = EDGE_NODES[edge][t]
                    value = field_ref[node, :, lanes]
                    other = jnp.where(turned, val_ref[7 - t, rows, lanes], val_ref[t, rows, lanes])
                    weight = np.float32(edge_penalty * WEIGHTS[t])
                    visit(chunk, rows, node, lanes, value, weight * (coef * value - other))


def far_edges(after_ref, before_ref, far_ref, edges_ref, trace_ref, elems, visit):
    modes = after_ref.shape[1]
    lane = lane_of((modes, LANES))

    def value_of(t):
        return jnp.where(lane < ROWS, after_ref[t], before_ref[t])

    fill_pairs(trace_ref, 0, modes, pl.ds(0, LANES), value_of, 2)
    for edge in range(4):
        values = gathered(trace_ref, far_ref[:, edge * LANES : (edge + 1) * LANES], 2)
        flips = edges_ref[8 * edge + 1 : 8 * edge + 2, :]
        flip = jnp.where(lane < ROWS, flips[:, :LANES], flips[:, elems - LANES :])
        for t in range(8):
            other = jnp.where(flip > 0.5, values[7 - t], values[t])
            visit(edge, t, other * np.float32(-edge_penalty * WEIGHTS[t]))


def apply_kernel(want_image, count, first, *refs):
    fields, refs = refs[:count], refs[count:]
    geo_ref, mass_ref, flag_ref, local_ref, edges_ref = refs[:5]
    refs = refs[5:]
    image_ref = refs[0] if want_image else None
    sums_ref, trace_ref, val_ref, acc_ref = refs[-4:]
    sums_ref[...] = jnp.zeros_like(sums_ref)
    start = 0
    for field_ref in fields:
        row = first + start
        volume(field_ref, geo_ref, mass_ref, row, image_ref, sums_ref, start, acc_ref)
        start += field_ref.shape[1]
    totals = [None] * count

    def visit(chunk, rows, node, lanes, value, term):
        if want_image:
            image_ref[node, :, lanes] += term
        product = value * term
        totals[chunk] = product if totals[chunk] is None else totals[chunk] + product

    parts = 2 if want_image else 1
    local_edges(
        fields, first, flag_ref, local_ref, edges_ref, trace_ref, val_ref, parts, visit
    )
    start = 0
    for chunk, field_ref in enumerate(fields):
        rows = slice(start, start + field_ref.shape[1])
        start = rows.stop
        sums_ref[1, rows, :] += totals[chunk]


def apply_local(fields, first, geo, mass, flag, local, edges, want_image):
    elems = fields[0].shape[2]
    modes = sum(field.shape[1] for field in fields)
    sums = jax.ShapeDtypeStruct((2, modes, LANES), jnp.float32)
    shapes = [jax.ShapeDtypeStruct(fields[0].shape, jnp.float32), sums] if want_image else [sums]
    parts = 2 if want_image else 1
    return pl.pallas_call(
        functools.partial(apply_kernel, want_image, len(fields), first),
        in_specs=vmem(5 + len(fields)),
        out_specs=vmem(len(shapes)),
        out_shape=shapes,
        scratch_shapes=[
            pltpu.VMEM((parts * 8 * modes, 4 * elems), jnp.bfloat16),
            pltpu.VMEM((8, modes, elems), jnp.float32),
            pltpu.VMEM((64, 8, LANES), jnp.float32),
        ],
        compiler_params=pltpu.CompilerParams(vmem_limit_bytes=16 * MIB),
        cost_estimate=small_cost(),
    )(*fields, geo, mass, flag, local, edges)


def ends_of(node, field_refs, lane):
    elems = field_refs[0].shape[2]
    pieces = []
    for ref in field_refs:
        pieces.append((ref[node, :, :LANES], ref[node, :, elems - LANES :]))
    first = [p[0] for p in pieces]
    last = [p[1] for p in pieces]
    if len(pieces) > 1:
        first, last = [jnp.concatenate(first, axis=0)], [jnp.concatenate(last, axis=0)]
    return jnp.where(lane < ROWS, first[0], last[0])


def first_far_kernel(count, *refs):
    images, fields, refs = refs[:count], refs[count : 2 * count], refs[2 * count :]
    sum_refs, refs = refs[:count], refs[count:]
    after_ref, before_ref, far_ref, edges_ref, mask_ref = refs[:5]
    outs, (send_ref, out_ref, trace_ref) = refs[5 : 5 + count], refs[5 + count :]
    modes = after_ref.shape[1]
    elems = fields[0].shape[2]
    lane = lane_of((modes, LANES))
    sums = [[ref[k] for ref in sum_refs] for k in range(2)]
    sums = [jnp.concatenate(pieces, axis=0) if count > 1 else pieces[0] for pieces in sums]
    totals = [sums[1]]
    done = set()

    def visit(edge, t, term):
        node = EDGE_NODES[edge][t]
        totals[0] = totals[0] + ends_of(node, fields, lane) * term
        start = 0
        for image_ref, ref in zip(images, outs):
            size = ref.shape[1]
            part = term[start : start + size]
            here = lane_of((size, LANES)) < ROWS
            start += size
            source = ref if node in done else image_ref
            ref[node, :, :LANES] = source[node, :, :LANES] + jnp.where(here, part, 0.0)
            ref[node, :, elems - LANES :] = source[node, :, elems - LANES :] + jnp.where(
                here, 0.0, part
            )
        done.add(node)

    far_edges(after_ref, before_ref, far_ref, edges_ref, trace_ref, elems, visit)
    out_ref[0] = sums[0]
    out_ref[1] = totals[0]
    start = 0
    for ref in outs:
        send_from(ref, mask_ref, send_ref, start)
        start += ref.shape[1]


def first_far(images, fields, halo, far, edges, mask, sums):
    count = len(fields)
    modes = sum(value.shape[1] for value in sums)
    return pl.pallas_call(
        functools.partial(first_far_kernel, count),
        in_specs=vmem(3 * count + 5),
        out_specs=vmem(count + 2),
        out_shape=[jax.ShapeDtypeStruct(image.shape, jnp.float32) for image in images]
        + [
            jax.ShapeDtypeStruct((8, modes, LANES), jnp.float32),
            jax.ShapeDtypeStruct((2, modes, LANES), jnp.float32),
        ],
        scratch_shapes=[pltpu.VMEM((16 * modes, LANES), jnp.bfloat16)],
        input_output_aliases={k: k for k in range(count)},
        compiler_params=pltpu.CompilerParams(vmem_limit_bytes=8 * MIB),
        cost_estimate=small_cost(),
    )(*images, *fields, *sums, *halo, far, edges, mask)


def second_far_kernel(count, *refs):
    fields, refs = refs[:count], refs[count:]
    after_ref, before_ref, far_ref, edges_ref, first_ref, more_ref, out_ref, trace_ref = refs
    modes = after_ref.shape[1]
    elems = fields[0].shape[2]
    lane = lane_of((modes, LANES))
    totals = [more_ref[1]]

    def visit(edge, t, term):
        totals[0] = totals[0] + ends_of(EDGE_NODES[edge][t], fields, lane) * term

    far_edges(after_ref, before_ref, far_ref, edges_ref, trace_ref, elems, visit)
    sums = [first_ref[0], first_ref[1], more_ref[0], totals[0]]
    packed = jnp.zeros((modes, LANES), jnp.float32)
    for k, value in enumerate(sums):
        packed = jnp.where(lane == k, jnp.sum(value, axis=1, keepdims=True), packed)
    out_ref[...] = packed


def second_far(fields, halo, far, edges, first, more):
    modes = first.shape[1]
    return pl.pallas_call(
        functools.partial(second_far_kernel, len(fields)),
        in_specs=vmem(6 + len(fields)),
        out_specs=vmem(1)[0],
        out_shape=jax.ShapeDtypeStruct((modes, LANES), jnp.float32),
        scratch_shapes=[pltpu.VMEM((16 * modes, LANES), jnp.bfloat16)],
        compiler_params=pltpu.CompilerParams(vmem_limit_bytes=8 * MIB),
        cost_estimate=small_cost(),
    )(*fields, *halo, far, edges, first, more)


def finish_kernel(count, chunks, *refs):
    fields, refs = refs[: 2 * chunks], refs[2 * chunks :]
    sum_refs, out_ref = refs[:count], refs[count]
    total = sum_refs[0][...]
    for ref in sum_refs[1:]:
        total = total + ref[...]
    m0, m1, m2, m3 = [total[:, k : k + 1] for k in range(4)]
    alpha = m0 / m1
    norm = alpha * (alpha * m2) - 2.0 * (alpha * m1) + m0
    energy = m1 - 2.0 * (alpha * m2) + alpha * (alpha * m3)
    beta = norm / m0
    second = norm / (energy - beta * (norm / alpha))
    on_r = jnp.broadcast_to(alpha + second * (1.0 + beta), total.shape)
    on_q = jnp.broadcast_to(second * alpha, total.shape)
    start = 0
    for chunk in range(chunks):
        r0_ref, q0_ref = fields[2 * chunk : 2 * chunk + 2]
        mine = slice(start, start + r0_ref.shape[1])
        start = mine.stop
        for j in range(8):
            rows = slice(8 * j, 8 * j + 8)
            value = on_r[mine] * r0_ref[rows] - on_q[mine] * q0_ref[rows]
            out_ref[mine, rows, :] = jnp.swapaxes(value, 0, 1)


def finish(fields, sums):
    elems = fields[0].shape[2]
    chunks = len(fields) // 2
    total = sums[0].shape[0]
    blocks = [pl.BlockSpec((64, field.shape[1], LANES), lambda b: (0, 0, b)) for field in fields]
    small = pl.BlockSpec((total, LANES), lambda b: (0, 0))
    return pl.pallas_call(
        functools.partial(finish_kernel, len(sums), chunks),
        grid=(elems // LANES,),
        in_specs=blocks + [small] * len(sums),
        out_specs=pl.BlockSpec((total, 64, LANES), lambda b: (0, 0, b)),
        out_shape=jax.ShapeDtypeStruct((total, 64, elems), jnp.float32),
        compiler_params=pltpu.CompilerParams(vmem_limit_bytes=16 * MIB),
    )(*fields, *sums)


def shifted(value, axis, steps):
    size = lax.axis_size(axis)
    return lax.ppermute(value, axis, [(i, (i + steps) % size) for i in range(size)])


def exchanged(slots, first=0):
    size = lax.axis_size("gz")
    out = []
    for number, value in enumerate(slots):
        d = first + number
        out.append(lax.ppermute(value, "gz", [(i, i ^ d) for i in range(size)]) if d else value)
    return out


def both_sides(send):
    return [shifted(send, "xy", -1), shifted(send, "xy", 1)]


def pad_rows(values, rows=8):
    return jnp.pad(values, ((0, rows - values.shape[0]), (0, 0)))


def edge_tables(nbr_elem, nbr_edge):
    elems = nbr_elem.shape[1]
    me, size = lax.axis_index("xy"), lax.axis_size("xy")
    wall = nbr_elem < 0
    ids = jnp.maximum(nbr_elem, 0)
    owner, local_id = ids // elems, ids % elems
    here = (owner == me) & ~wall
    after = (owner == (me + 1) % size) & ~wall & ~here
    before = ~wall & ~here & ~after
    place = jnp.where(here, nbr_edge % 4 * elems + local_id, -1).reshape(-1)
    source = jnp.arange(4 * elems, dtype=jnp.int32)[:, None]
    local = (source == place[None, :]).astype(jnp.bfloat16)
    first = jnp.arange(LANES) < ROWS

    def ends(table):
        return jnp.where(first[None, :], table[:, :LANES], table[:, elems - LANES :])

    send = jnp.where(first[None, :], before[:, :LANES], after[:, elems - LANES :])
    slot = jnp.where(after, local_id, local_id - (elems - ROWS) + ROWS)
    slot = jnp.where(send, ends(slot), -1).reshape(-1)
    far = (jnp.arange(LANES, dtype=jnp.int32)[:, None] == slot[None, :]).astype(jnp.bfloat16)
    flags = jnp.stack([wall, nbr_edge >= 4], axis=1).astype(jnp.float32)
    flags = jnp.pad(flags, ((0, 0), (0, 6), (0, 0))).reshape(32, elems)
    return local, far, pad_rows(send.astype(jnp.float32)), flags


def per_device(concentration, geometry, nbr_elem, nbr_edge, wall_flags):
    planes, _, elems = concentration.shape
    groups = lax.axis_size("gz")
    me = lax.axis_index("gz")
    fold = Fold(elems // groups)
    scale_x, scale_y = geometry[0], geometry[1]
    geo = pad_rows(jnp.stack([1.0 / (scale_x * scale_y), scale_x * scale_x, scale_y * scale_y]))
    mine = lax.dynamic_slice_in_dim(geo, me * fold.width, fold.width, axis=1)
    mine = jnp.tile(mine, (1, fold.parts))
    index = me.astype(jnp.int32).reshape(1)
    mode_ids = me * planes + jnp.arange(planes, dtype=jnp.int32)
    wave = ((mode_ids + 1) // 2).astype(jnp.float32)
    mass = jnp.broadcast_to(
        (1.0 / time_step + axial_stiffness * wave * wave)[:, None], (planes, LANES)
    )
    flag = jnp.broadcast_to(wall_flags.astype(jnp.float32)[:, None], (planes, LANES))
    tables = edge_tables(nbr_elem, nbr_edge)
    near_sent = pack(index, concentration, fold, groups, 0)
    far_sent = pack(index, concentration, fold, groups, groups // 2)
    near_field = exchanged(near_sent)
    far_field = exchanged(far_sent, groups // 2)
    near_field, geo, mine, mass, flag, tables = lax.optimization_barrier(
        (near_field, geo, mine, mass, flag, tables)
    )
    local, far, mask, edges = tables
    near = near_terms(index, mine, near_field, fold)
    sizes = [planes - 8, 8] if planes > 16 else [planes]
    tables = transform_tables(planes * groups)
    sent, far_terms = far_modes(index, mine, tables, near, far_field, fold, sizes)
    far_parts = [exchanged(piece, groups // 2) for piece in sent]
    near_parts = exchanged(near_modes(index, mine, tables, near, far_terms, fold, planes))
    fields, images, sums, sends = [], [], [], []
    start = 0
    for piece, size in enumerate(sizes):
        parts = near_parts + far_parts[piece]
        field, send = unpack(index, mask, parts, fold, sends)
        sends = [send]
        image, more = apply_local([field], start, geo, mass, flag, local, edges, True)
        start += size
        mask, more = lax.optimization_barrier((mask, more))
        fields.append(field)
        images.append(image)
        sums.append(more)
    halo = both_sides(sends[0])
    *images, send, sums = first_far(images, fields, halo, far, edges, mask, sums)
    (more,) = apply_local(images, 0, geo, mass, flag, local, edges, False)
    packed = second_far(images, both_sides(send), far, edges, sums, more)
    size = lax.axis_size("xy")
    pairs = [value for pair in zip(fields, images) for value in pair]
    return finish(pairs, [packed] + [shifted(packed, "xy", k) for k in range(1, size)])


def solution(mesh):
    return jax.shard_map(
        per_device,
        mesh=mesh,
        in_specs=(P("gz", None, "xy"), P(None, "xy"), P(None, "xy"), P(None, "xy"), P("gz")),
        out_specs=P("gz", None, "xy"),
        check_vma=False,
    )
```

```python
import functools

import jax
import jax.numpy as jnp
import ml_dtypes
import numpy as np
from jax import lax
from jax.experimental import pallas as pl
from jax.experimental.pallas import tpu as pltpu
from jax.sharding import PartitionSpec as P

ROWS = 64
LANES = 128
MIB = 1024 * 1024

time_step = 0.2
axial_stiffness = 0.002
plane_stiffness = 1.0
edge_penalty = 4.0
axial_mobility = 0.002
mobility_floor = 0.05


def point_tables():
    degree = 7
    points = np.arange(degree + 1)
    theta = np.pi * points / degree
    nodes_x = np.cos(theta)
    signs = np.where((points == 0) | (points == degree), 2.0, 1.0) * (-1.0) ** points
    differ = nodes_x[:, None] - nodes_x[None, :]
    deriv = np.outer(signs, 1.0 / signs) / (differ + np.eye(degree + 1))
    deriv = deriv - np.eye(degree + 1) * deriv.sum(axis=1)[:, None]
    inner = np.ones(degree - 1)
    for number in range(1, (degree - 1) // 2 + 1):
        inner = inner - 2.0 * np.cos(2 * number * theta[1:degree]) / (4 * number * number - 1)
    weights = np.zeros(degree + 1)
    weights[1:degree] = 2.0 * inner / degree
    weights[0] = 1.0 / degree**2
    weights[degree] = 1.0 / degree**2
    return (deriv, weights)


def fourier_table(length):
    planes = np.arange(length)
    wave_no = (planes + 1) // 2
    phase = np.outer(wave_no, planes) % length * (2.0 * np.pi / length)
    table = np.where((planes % 2 == 1)[:, None], np.cos(phase), np.sin(phase)) * np.sqrt(
        2.0 / length
    )
    table[0] = 1.0 / np.sqrt(length)
    table[length - 1] = np.cos(phase[length - 1]) / np.sqrt(length)
    return table


DERIV, WEIGHTS = point_tables()
BACK = DERIV.T * WEIGHTS[None, :]
STIFF = BACK @ DERIV
BACK_SCALED = BACK / WEIGHTS[:, None]


def two_parts(table):
    upper = table.astype(np.float32).astype(ml_dtypes.bfloat16)
    lower = (table - upper.astype(np.float64)).astype(np.float32).astype(ml_dtypes.bfloat16)
    return upper, lower


def split(value):
    upper = value.astype(jnp.bfloat16)
    lower = (value - upper.astype(jnp.float32)).astype(jnp.bfloat16)
    return upper, lower


class Fold:
    def __init__(self, width):
        self.width = width
        self.parts = LANES // width
        self.fold_j = 2 if self.parts >= 2 else 1
        self.fold_i = 2 if self.parts >= 4 else 1
        self.count_j = 8 // self.fold_j
        self.count_i = 8 // self.fold_i
        self.slots = self.count_j * self.count_i

    def slot(self, jp, ip):
        return jp * self.count_i + ip

    def node(self, jp, ip, part):
        half_j, half_i = part // self.fold_i, part % self.fold_i
        j = 7 - jp if half_j else jp
        i = 7 - ip if half_i else ip
        return 8 * j + i

    def place(self, node):
        j, i = node // 8, node % 8
        half_j = 1 if j >= self.count_j else 0
        half_i = 1 if i >= self.count_i else 0
        jp = 7 - j if half_j else j
        ip = 7 - i if half_i else i
        return self.slot(jp, ip), half_j * self.fold_i + half_i


def lane_of(shape):
    return lax.broadcasted_iota(jnp.int32, shape, len(shape) - 1)


def rolled(value, lanes):
    lanes = lanes % LANES
    return value if lanes == 0 else pltpu.roll(value, lanes, value.ndim - 1)


def by_part(values, lane, width):
    out = values[0]
    for r in range(1, len(values)):
        out = jnp.where(lane >= r * width, values[r], out)
    return out


def mirrored(value, lane, shift):
    if 2 * shift == LANES:
        return rolled(value, shift)
    return jnp.where((lane & shift) == 0, rolled(value, -shift), rolled(value, shift))


def combine(coefs, values):
    total = None
    for c, v in zip(coefs, values):
        term = v * np.float32(c)
        total = term if total is None else total + term
    return total


def line_apply(matrix, values, sign):
    even = [values[k] + values[7 - k] for k in range(4)]
    odd = [values[k] - values[7 - k] for k in range(4)]
    out = [None] * 8
    for a in range(4):
        from_even = combine([(matrix[a, b] + matrix[a, 7 - b]) / 2 for b in range(4)], even)
        from_odd = combine([(matrix[a, b] - matrix[a, 7 - b]) / 2 for b in range(4)], odd)
        out[a] = from_even + from_odd
        out[7 - a] = from_even - from_odd if sign > 0 else from_odd - from_even
    return out


def derivative_line(matrix, values, back, swap):
    if swap is None:
        return line_apply(matrix, values, -1)
    other = [swap(v) for v in values]
    sign = -1.0 if back else 1.0
    out = []
    for a in range(4):
        coefs = [matrix[a, b] for b in range(4)] + [sign * matrix[a, 7 - b] for b in range(4)]
        out.append(combine(coefs, list(values) + other))
    return out


EDGE_NODES = [
    [t for t in range(8)],
    [8 * t + 7 for t in range(8)],
    [56 + t for t in range(8)],
    [8 * t for t in range(8)],
]


def swapped(me, values):
    bit = 1
    while bit < len(values):
        flip = (me & bit) != 0
        values = [jnp.where(flip, values[r ^ bit], values[r]) for r in range(len(values))]
        bit *= 2
    return values


def pack_kernel(fold, me_ref, c_ref, *out_refs):
    lane = lane_of((c_ref.shape[0], LANES))
    me = me_ref[0]
    for step in range(len(out_refs) // fold.parts):

        @pl.when(pl.program_id(0) == step)
        def _():
            by_node = jnp.swapaxes(c_ref[...], 0, 1)
            for jp in range(fold.count_j):
                for ip in range(fold.count_i):
                    loads = [by_node[fold.node(jp, ip, q)] for q in range(fold.parts)]
                    made = []
                    for r in range(fold.parts):
                        parts = [rolled(loads[q], (q - r) * fold.width) for q in range(fold.parts)]
                        made.append(by_part(parts, lane, fold.width))
                    for p, value in enumerate(swapped(me, made)):
                        out_refs[step * fold.parts + p][fold.slot(jp, ip)] = value


def pack(me, conc, fold, groups, first):
    planes, nodes, elems = conc.shape
    count = groups // 2
    offset = first // fold.parts

    def block(step, me_ref):
        return (0, 0, (step + offset) ^ (me_ref[0] // fold.parts))

    slot = jax.ShapeDtypeStruct((fold.slots, planes, LANES), jnp.float32)
    return pl.pallas_call(
        functools.partial(pack_kernel, fold),
        grid_spec=pltpu.PrefetchScalarGridSpec(
            num_scalar_prefetch=1,
            grid=(count // fold.parts,),
            in_specs=[pl.BlockSpec((planes, nodes, LANES), block)],
            out_specs=[pl.BlockSpec(slot.shape, lambda s, me_ref: (0, 0, 0))] * count,
        ),
        out_shape=[slot] * count,
        compiler_params=pltpu.CompilerParams(vmem_limit_bytes=60 * MIB),
        cost_estimate=pl.CostEstimate(
            flops=conc.size, bytes_accessed=4 * conc.size, transcendentals=0
        ),
    )(me, conc)


def plane_terms(fold, y_ref, geo_ref, x_ref, acc_ref, row, base, half):
    lane = lane_of((16, LANES))
    square_x = jnp.broadcast_to(geo_ref[1:2, :], (16, LANES))
    square_y = jnp.broadcast_to(geo_ref[2:3, :], (16, LANES))

    def conc(jp, ip):
        return y_ref[fold.slot(jp, ip), pl.ds(base, 16), :]

    def potential(c):
        square = c * c
        return square * c - c, jnp.maximum(1.0 - square, mobility_floor)

    def flux(fields, swap):
        pairs = [potential(c) for c in fields]
        slope = derivative_line(DERIV, [p[0] for p in pairs], False, swap)
        scaled = [s * p[1] for s, p in zip(slope, pairs)]
        return derivative_line(BACK_SCALED, scaled, True, swap), pairs

    swap_i = None
    if fold.fold_i == 2:
        swap_i = lambda v: mirrored(v, lane, fold.width)
    swap_j = None
    if fold.fold_j == 2:
        swap_j = lambda v: mirrored(v, lane, fold.width * fold.fold_i)
    for jp in range(fold.count_j):
        fields = [conc(jp, ip) for ip in range(fold.count_i)]
        result, _unused = flux(fields, swap_i)
        for ip in range(fold.count_i):
            acc_ref[fold.slot(jp, ip)] = (
                fields[ip] * np.float32(1.0 / time_step) - result[ip] * square_x
            )
    for ip in range(fold.count_i):
        fields = [conc(jp, ip) for jp in range(fold.count_j)]
        result, pairs = flux(fields, swap_j)
        for jp in range(fold.count_j):
            slot = fold.slot(jp, ip)
            explicit = acc_ref[slot] - result[jp] * square_y
            where = pl.ds((slot % 2) * LANES, LANES)
            for kind, value in enumerate((explicit, pairs[jp][0])):
                upper, lower = split(value)
                x_ref[slot // 2, pl.ds(kind * half + row, 16), where] = upper
                x_ref[slot // 2, pl.ds((2 + kind) * half + row, 16), where] = lower


def slot_terms(fold, me, first, count, y_refs, geo_ref, x_ref, acc_ref):
    planes = y_refs[0].shape[1]
    half = count * planes
    for number, y_ref in enumerate(y_refs):
        place = (me ^ (first + number)) % count

        def chunk(part, _, y_ref=y_ref, place=place):
            base = pl.multiple_of(part * 16, 16)
            row = pl.multiple_of(place * planes + base, 16)
            plane_terms(fold, y_ref, geo_ref, x_ref, acc_ref, row, base, half)
            return 0

        lax.fori_loop(0, planes // 16, chunk, 0)


def terms_kernel(fold, first, count, me_ref, geo_ref, *refs):
    y_refs, (x_ref, acc_ref) = refs[:-2], refs[-2:]
    slot_terms(fold, me_ref[0], first, count, y_refs, geo_ref, x_ref, acc_ref)


def far_kernel(fold, count, sizes, me_ref, geo_ref, table_ref, near_ref, given_ref, y_ref, *refs):
    chunks = len(sizes)
    out_refs = [refs[k * chunks : (k + 1) * chunks] for k in range(count)]
    x_ref, acc_ref, result_ref = refs[count * chunks :]
    slot_terms(fold, me_ref[0], 2 * count - 1, count, [y_ref], geo_ref, x_ref, acc_ref)
    transform(fold, 1, me_ref, geo_ref, table_ref, (near_ref, x_ref), out_refs, result_ref)


def near_modes_kernel(fold, me_ref, geo_ref, table_ref, near_ref, far_ref, *refs):
    out_refs, result_ref = [[ref] for ref in refs[:-1]], refs[-1]
    transform(fold, 0, me_ref, geo_ref, table_ref, (near_ref, far_ref), out_refs, result_ref)


def transform(fold, other, me_ref, geo_ref, table_ref, terms, out_refs, result_ref):
    count = len(out_refs)
    half = result_ref.shape[0]
    planes = half // count
    me = me_ref[0]
    mine = me // count
    jac = jnp.broadcast_to(geo_ref[0:1, :], (planes, LANES))
    rows = pl.ds(pl.multiple_of((mine ^ other) * half, 16), half)

    def product(which, data):
        upper, lower = slice(0, 4 * half), slice(4 * half, 6 * half)
        return jnp.dot(
            table_ref[which, rows, upper], data, preferred_element_type=jnp.float32
        ) + jnp.dot(
            table_ref[which, rows, lower], data[: 2 * half], preferred_element_type=jnp.float32
        )

    for pair in range(fold.slots // 2):
        result_ref[...] = product(mine, terms[0][pair]) + product(1 - mine, terms[1][pair])
        for k in range(2):
            slot = 2 * pair + k
            jp, ip = slot // fold.count_i, slot % fold.count_i
            scale = jac * np.float32(WEIGHTS[jp] * WEIGHTS[ip])
            for number, pieces in enumerate(out_refs):
                start = (me ^ number) % count * planes
                for out_ref in pieces:
                    size = out_ref.shape[1]
                    here = pl.ds(pl.multiple_of(start, 8), size)
                    value = result_ref[here, k * LANES : (k + 1) * LANES]
                    out_ref[slot] = value * scale[:size]
                    start = start + size


def small_cost():
    return pl.CostEstimate(flops=1, bytes_accessed=1, transcendentals=0)


def smem():
    return pl.BlockSpec(memory_space=pltpu.SMEM)


def vmem(count):
    return [pl.BlockSpec(memory_space=pltpu.VMEM)] * count


def some_terms(me, geo, fields, fold, first, count):
    slots, planes, _ = fields[0].shape
    size = len(fields) * fields[0].size
    return pl.pallas_call(
        functools.partial(terms_kernel, fold, first, count),
        in_specs=[smem()] + vmem(1 + len(fields)),
        out_specs=vmem(1)[0],
        out_shape=jax.ShapeDtypeStruct(
            (slots // 2, 4 * count * planes, 2 * LANES), jnp.bfloat16
        ),
        scratch_shapes=[pltpu.VMEM((slots, 16, LANES), jnp.float32)],
        compiler_params=pltpu.CompilerParams(vmem_limit_bytes=16 * MIB),
        cost_estimate=pl.CostEstimate(
            flops=80 * size, bytes_accessed=12 * size, transcendentals=0
        ),
    )(me, geo, *fields)


def transform_tables(total):
    table = fourier_table(total).astype(np.float32).astype(np.float64)
    wave = ((np.arange(total) + 1) // 2).astype(np.float64)
    upper, lower = two_parts(table)
    upper_b, lower_b = two_parts(-axial_mobility * (wave * wave)[:, None] * table)
    kinds = [upper, upper_b, upper, upper_b, lower, lower_b]
    halves = np.split(np.stack(kinds), 2, axis=2)
    return jnp.asarray(np.stack([np.concatenate(list(half), axis=1) for half in halves]))


def far_modes(me, geo, tables, near, far, field, fold, count, sizes):
    slots, planes, _ = field.shape
    size = count * field.size
    chunks = len(sizes)
    pieces = [jax.ShapeDtypeStruct((slots, k, LANES), jnp.float32) for k in sizes]
    *outs, far = pl.pallas_call(
        functools.partial(far_kernel, fold, count, sizes),
        in_specs=[smem()] + vmem(5),
        out_specs=vmem(chunks * count + 1),
        input_output_aliases={4: chunks * count},
        out_shape=pieces * count + [jax.ShapeDtypeStruct(near.shape, jnp.bfloat16)],
        scratch_shapes=[
            pltpu.VMEM((slots, 16, LANES), jnp.float32),
            pltpu.VMEM((count * planes, 2 * LANES), jnp.float32),
        ],
        compiler_params=pltpu.CompilerParams(vmem_limit_bytes=24 * MIB),
        cost_estimate=pl.CostEstimate(
            flops=12 * count * planes * size, bytes_accessed=8 * size, transcendentals=0
        ),
    )(me, geo, tables, near, far, field)
    return [outs[k::chunks] for k in range(chunks)], far


def near_modes(me, geo, tables, near, far, fold, planes):
    slots = fold.slots
    count = near.shape[1] // (4 * planes)
    size = count * slots * planes * LANES
    slot = jax.ShapeDtypeStruct((slots, planes, LANES), jnp.float32)
    return pl.pallas_call(
        functools.partial(near_modes_kernel, fold),
        in_specs=[smem()] + vmem(4),
        out_specs=vmem(count),
        out_shape=[slot] * count,
        scratch_shapes=[pltpu.VMEM((count * planes, 2 * LANES), jnp.float32)],
        compiler_params=pltpu.CompilerParams(vmem_limit_bytes=16 * MIB),
        cost_estimate=pl.CostEstimate(
            flops=12 * count * planes * size, bytes_accessed=8 * size, transcendentals=0
        ),
    )(me, geo, tables, near, far)


def edge_send(mask_ref, edge, write):
    for t in range(8):
        total = None
        for a in range(4):
            term = edge(a, t) * mask_ref[a : a + 1, :]
            total = term if total is None else total + term
        write(t, total)


def send_from(field_ref, mask_ref, out_ref, start):
    modes, elems = field_ref.shape[1:]
    lane = lane_of((modes, LANES))

    def edge(a, t):
        node = EDGE_NODES[a][t]
        ends = field_ref[node, :, :LANES], field_ref[node, :, elems - LANES :]
        return jnp.where(lane < ROWS, ends[0], ends[1])

    def write(t, value):
        out_ref[t, start : start + modes, :] = value

    edge_send(mask_ref, edge, write)


def unpack_kernel(fold, groups, start, me_ref, mask_ref, *refs):
    parts, (r0_ref, send_ref) = refs[:groups], refs[-2:]
    modes = r0_ref.shape[1]
    me = me_ref[0]

    def tile(part, _):
        rows = pl.ds(pl.multiple_of(part * 8, 8), 8)
        whole_rows = pl.ds(pl.multiple_of(part * 8 + start, 8), 8)

        def load(ref, slot):
            return ref[slot, rows if ref.shape[1] == modes else whole_rows, :]

        lane = lane_of((8, LANES))
        for k in range(groups // fold.parts):
            block = k ^ (me // fold.parts)
            lanes = pl.ds(pl.multiple_of(block * LANES, LANES), LANES)
            mine = parts[k * fold.parts : (k + 1) * fold.parts]
            for jp in range(fold.count_j):
                for ip in range(fold.count_i):
                    loads = swapped(me, [load(ref, fold.slot(jp, ip)) for ref in mine])
                    for q in range(fold.parts):
                        shifts = [
                            rolled(loads[r], (r - q) * fold.width) for r in range(fold.parts)
                        ]
                        value = by_part(shifts, lane, fold.width)
                        r0_ref[fold.node(jp, ip, q), rows, lanes] = value
        return 0

    lax.fori_loop(0, modes // 8, tile, 0)
    if start:
        send_ref[:, :start, :] = refs[groups][...]
    send_from(r0_ref, mask_ref, send_ref, start)


def unpack(me, mask, parts, fold, sends):
    _, modes, _ = parts[-1].shape
    groups = len(parts)
    elems = groups * fold.width
    start = sum(value.shape[1] for value in sends)
    return pl.pallas_call(
        functools.partial(unpack_kernel, fold, groups, start),
        in_specs=[smem()] + vmem(1 + groups + len(sends)),
        out_specs=vmem(2),
        out_shape=[
            jax.ShapeDtypeStruct((64, modes, elems), jnp.float32),
            jax.ShapeDtypeStruct((8, start + modes, LANES), jnp.float32),
        ],
        compiler_params=pltpu.CompilerParams(vmem_limit_bytes=4 * MIB),
        cost_estimate=small_cost(),
    )(me, mask, *parts, *sends)


def volume(field_ref, geo_ref, mass_ref, first, image_ref, sums_ref, row_of_sums, acc_ref):
    modes, elems = field_ref.shape[1:]
    tiles = modes // 8

    def tile(number, _):
        row = pl.multiple_of(number % tiles * 8, 8)
        rows = pl.ds(row, 8)
        sum_rows = pl.ds(row + row_of_sums, 8)
        lanes = pl.ds(pl.multiple_of(number // tiles * LANES, LANES), LANES)
        jac = geo_ref[0:1, lanes] * mass_ref[pl.ds(row + first, 8), :]
        square_x = jnp.broadcast_to(geo_ref[0:1, lanes] * geo_ref[1:2, lanes], (8, LANES))
        square_y = jnp.broadcast_to(geo_ref[0:1, lanes] * geo_ref[2:3, lanes], (8, LANES))
        stiff = plane_stiffness * STIFF
        for j in range(8):
            values = [field_ref[8 * j + i, rows, lanes] for i in range(8)]
            result = line_apply(stiff, values, 1)
            scale = square_x * np.float32(WEIGHTS[j])
            mass = jac * np.float32(WEIGHTS[j])
            for i in range(8):
                acc_ref[8 * j + i] = result[i] * scale + (mass * np.float32(WEIGHTS[i])) * values[i]
        totals = [None, None]
        for i in range(8):
            values = [field_ref[8 * j + i, rows, lanes] for j in range(8)]
            result = line_apply(stiff, values, 1)
            scale = square_y * np.float32(WEIGHTS[i])
            for j in range(8):
                image = acc_ref[8 * j + i] + result[j] * scale
                if image_ref is not None:
                    image_ref[8 * j + i, rows, lanes] = image
                for k, term in enumerate((values[j] * values[j], values[j] * image)):
                    totals[k] = term if totals[k] is None else totals[k] + term
        for k in range(2):
            sums_ref[k, sum_rows, :] += totals[k]
        return 0

    lax.fori_loop(0, tiles * (elems // LANES), tile, 0)


def fill_pairs(target_ref, first, modes, lanes, value_of, parts):
    total = target_ref.shape[0] // (8 * parts)
    for t in range(0, 8, 2):
        pieces = split(jnp.concatenate([value_of(t), value_of(t + 1)], axis=0))
        for part in range(parts):
            row = (8 * part + t) * total
            target_ref[pl.ds(row, 2 * total), lanes] = pieces[part]


def gathered(trace_ref, table, parts):
    value = jnp.dot(trace_ref[...], table, preferred_element_type=jnp.float32)
    if parts == 2:
        half = value.shape[0] // 2
        value = value[:half] + value[half:]
    return value.reshape(8, value.shape[0] // 8, value.shape[1])


def local_edges(fields, first, flag_ref, local_ref, edges_ref, trace_ref, val_ref, parts, visit):
    elems = val_ref.shape[2]
    for a in range(4):

        def value_of(t):
            pieces = [field_ref[EDGE_NODES[a][t]] for field_ref in fields]
            return pieces[0] if len(pieces) == 1 else jnp.concatenate(pieces, axis=0)

        fill_pairs(trace_ref, 0, 0, pl.ds(a * elems, elems), value_of, parts)
    for edge in range(4):
        val_ref[...] = gathered(
            trace_ref, local_ref[:, edge * elems : (edge + 1) * elems], parts
        )
        for block in range(elems // LANES):
            lanes = pl.ds(block * LANES, LANES)
            wall = edges_ref[8 * edge : 8 * edge + 1, lanes]
            flip = edges_ref[8 * edge + 1 : 8 * edge + 2, lanes]
            start = 0
            for chunk, field_ref in enumerate(fields):
                modes = field_ref.shape[1]
                rows = slice(start, start + modes)
                start += modes
                turned = jnp.broadcast_to(flip, (modes, LANES)) > 0.5
                coef = 1.0 - wall * (1.0 - flag_ref[first + start - modes : first + start])
                for t in range(8):
                    node = EDGE_NODES[edge][t]
                    value = field_ref[node, :, lanes]
                    other = jnp.where(turned, val_ref[7 - t, rows, lanes], val_ref[t, rows, lanes])
                    weight = np.float32(edge_penalty * WEIGHTS[t])
                    visit(chunk, rows, node, lanes, value, weight * (coef * value - other))


def far_edges(after_ref, before_ref, far_ref, edges_ref, trace_ref, elems, visit):
    modes = after_ref.shape[1]
    lane = lane_of((modes, LANES))

    def value_of(t):
        return jnp.where(lane < ROWS, after_ref[t], before_ref[t])

    fill_pairs(trace_ref, 0, modes, pl.ds(0, LANES), value_of, 2)
    for edge in range(4):
        values = gathered(trace_ref, far_ref[:, edge * LANES : (edge + 1) * LANES], 2)
        flips = edges_ref[8 * edge + 1 : 8 * edge + 2, :]
        flip = jnp.where(lane < ROWS, flips[:, :LANES], flips[:, elems - LANES :])
        for t in range(8):
            other = jnp.where(flip > 0.5, values[7 - t], values[t])
            visit(edge, t, other * np.float32(-edge_penalty * WEIGHTS[t]))


def apply_kernel(want_image, count, first, *refs):
    fields, refs = refs[:count], refs[count:]
    geo_ref, mass_ref, flag_ref, local_ref, edges_ref = refs[:5]
    refs = refs[5:]
    image_ref = refs[0] if want_image else None
    sums_ref, trace_ref, val_ref, acc_ref = refs[-4:]
    sums_ref[...] = jnp.zeros_like(sums_ref)
    start = 0
    for field_ref in fields:
        row = first + start
        volume(field_ref, geo_ref, mass_ref, row, image_ref, sums_ref, start, acc_ref)
        start += field_ref.shape[1]
    totals = [None] * count

    def visit(chunk, rows, node, lanes, value, term):
        if want_image:
            image_ref[node, :, lanes] += term
        product = value * term
        totals[chunk] = product if totals[chunk] is None else totals[chunk] + product

    parts = 2 if want_image else 1
    local_edges(
        fields, first, flag_ref, local_ref, edges_ref, trace_ref, val_ref, parts, visit
    )
    start = 0
    for chunk, field_ref in enumerate(fields):
        rows = slice(start, start + field_ref.shape[1])
        start = rows.stop
        sums_ref[1, rows, :] += totals[chunk]


def apply_local(fields, first, geo, mass, flag, local, edges, want_image):
    elems = fields[0].shape[2]
    modes = sum(field.shape[1] for field in fields)
    sums = jax.ShapeDtypeStruct((2, modes, LANES), jnp.float32)
    shapes = [jax.ShapeDtypeStruct(fields[0].shape, jnp.float32), sums] if want_image else [sums]
    parts = 2 if want_image else 1
    return pl.pallas_call(
        functools.partial(apply_kernel, want_image, len(fields), first),
        in_specs=vmem(5 + len(fields)),
        out_specs=vmem(len(shapes)),
        out_shape=shapes,
        scratch_shapes=[
            pltpu.VMEM((parts * 8 * modes, 4 * elems), jnp.bfloat16),
            pltpu.VMEM((8, modes, elems), jnp.float32),
            pltpu.VMEM((64, 8, LANES), jnp.float32),
        ],
        compiler_params=pltpu.CompilerParams(vmem_limit_bytes=16 * MIB),
        cost_estimate=small_cost(),
    )(*fields, geo, mass, flag, local, edges)


def ends_of(node, field_refs, lane):
    elems = field_refs[0].shape[2]
    pieces = []
    for ref in field_refs:
        pieces.append((ref[node, :, :LANES], ref[node, :, elems - LANES :]))
    first = [p[0] for p in pieces]
    last = [p[1] for p in pieces]
    if len(pieces) > 1:
        first, last = [jnp.concatenate(first, axis=0)], [jnp.concatenate(last, axis=0)]
    return jnp.where(lane < ROWS, first[0], last[0])


def first_far_kernel(count, *refs):
    images, fields, refs = refs[:count], refs[count : 2 * count], refs[2 * count :]
    sum_refs, refs = refs[:count], refs[count:]
    after_ref, before_ref, far_ref, edges_ref, mask_ref = refs[:5]
    outs, (send_ref, out_ref, trace_ref) = refs[5 : 5 + count], refs[5 + count :]
    modes = after_ref.shape[1]
    elems = fields[0].shape[2]
    lane = lane_of((modes, LANES))
    sums = [[ref[k] for ref in sum_refs] for k in range(2)]
    sums = [jnp.concatenate(pieces, axis=0) if count > 1 else pieces[0] for pieces in sums]
    totals = [sums[1]]
    done = set()

    def visit(edge, t, term):
        node = EDGE_NODES[edge][t]
        totals[0] = totals[0] + ends_of(node, fields, lane) * term
        start = 0
        for image_ref, ref in zip(images, outs):
            size = ref.shape[1]
            part = term[start : start + size]
            here = lane_of((size, LANES)) < ROWS
            start += size
            source = ref if node in done else image_ref
            ref[node, :, :LANES] = source[node, :, :LANES] + jnp.where(here, part, 0.0)
            ref[node, :, elems - LANES :] = source[node, :, elems - LANES :] + jnp.where(
                here, 0.0, part
            )
        done.add(node)

    far_edges(after_ref, before_ref, far_ref, edges_ref, trace_ref, elems, visit)
    out_ref[0] = sums[0]
    out_ref[1] = totals[0]
    start = 0
    for ref in outs:
        send_from(ref, mask_ref, send_ref, start)
        start += ref.shape[1]


def first_far(images, fields, halo, far, edges, mask, sums):
    count = len(fields)
    modes = sum(value.shape[1] for value in sums)
    return pl.pallas_call(
        functools.partial(first_far_kernel, count),
        in_specs=vmem(3 * count + 5),
        out_specs=vmem(count + 2),
        out_shape=[jax.ShapeDtypeStruct(image.shape, jnp.float32) for image in images]
        + [
            jax.ShapeDtypeStruct((8, modes, LANES), jnp.float32),
            jax.ShapeDtypeStruct((2, modes, LANES), jnp.float32),
        ],
        scratch_shapes=[pltpu.VMEM((16 * modes, LANES), jnp.bfloat16)],
        input_output_aliases={k: k for k in range(count)},
        compiler_params=pltpu.CompilerParams(vmem_limit_bytes=8 * MIB),
        cost_estimate=small_cost(),
    )(*images, *fields, *sums, *halo, far, edges, mask)


def second_far_kernel(count, *refs):
    fields, refs = refs[:count], refs[count:]
    after_ref, before_ref, far_ref, edges_ref, first_ref, more_ref, out_ref, trace_ref = refs
    modes = after_ref.shape[1]
    elems = fields[0].shape[2]
    lane = lane_of((modes, LANES))
    totals = [more_ref[1]]

    def visit(edge, t, term):
        totals[0] = totals[0] + ends_of(EDGE_NODES[edge][t], fields, lane) * term

    far_edges(after_ref, before_ref, far_ref, edges_ref, trace_ref, elems, visit)
    sums = [first_ref[0], first_ref[1], more_ref[0], totals[0]]
    packed = jnp.zeros((modes, LANES), jnp.float32)
    for k, value in enumerate(sums):
        packed = jnp.where(lane == k, jnp.sum(value, axis=1, keepdims=True), packed)
    out_ref[...] = packed


def second_far(fields, halo, far, edges, first, more):
    modes = first.shape[1]
    return pl.pallas_call(
        functools.partial(second_far_kernel, len(fields)),
        in_specs=vmem(6 + len(fields)),
        out_specs=vmem(1)[0],
        out_shape=jax.ShapeDtypeStruct((modes, LANES), jnp.float32),
        scratch_shapes=[pltpu.VMEM((16 * modes, LANES), jnp.bfloat16)],
        compiler_params=pltpu.CompilerParams(vmem_limit_bytes=8 * MIB),
        cost_estimate=small_cost(),
    )(*fields, *halo, far, edges, first, more)


def finish_kernel(count, chunks, *refs):
    fields, refs = refs[: 2 * chunks], refs[2 * chunks :]
    sum_refs, out_ref = refs[:count], refs[count]
    total = sum_refs[0][...]
    for ref in sum_refs[1:]:
        total = total + ref[...]
    m0, m1, m2, m3 = [total[:, k : k + 1] for k in range(4)]
    alpha = m0 / m1
    norm = alpha * (alpha * m2) - 2.0 * (alpha * m1) + m0
    energy = m1 - 2.0 * (alpha * m2) + alpha * (alpha * m3)
    beta = norm / m0
    second = norm / (energy - beta * (norm / alpha))
    on_r = jnp.broadcast_to(alpha + second * (1.0 + beta), total.shape)
    on_q = jnp.broadcast_to(second * alpha, total.shape)
    start = 0
    for chunk in range(chunks):
        r0_ref, q0_ref = fields[2 * chunk : 2 * chunk + 2]
        mine = slice(start, start + r0_ref.shape[1])
        start = mine.stop
        for j in range(8):
            rows = slice(8 * j, 8 * j + 8)
            value = on_r[mine] * r0_ref[rows] - on_q[mine] * q0_ref[rows]
            out_ref[mine, rows, :] = jnp.swapaxes(value, 0, 1)


def finish(fields, sums):
    elems = fields[0].shape[2]
    chunks = len(fields) // 2
    total = sums[0].shape[0]
    blocks = [pl.BlockSpec((64, field.shape[1], LANES), lambda b: (0, 0, b)) for field in fields]
    small = pl.BlockSpec((total, LANES), lambda b: (0, 0))
    return pl.pallas_call(
        functools.partial(finish_kernel, len(sums), chunks),
        grid=(elems // LANES,),
        in_specs=blocks + [small] * len(sums),
        out_specs=pl.BlockSpec((total, 64, LANES), lambda b: (0, 0, b)),
        out_shape=jax.ShapeDtypeStruct((total, 64, elems), jnp.float32),
        compiler_params=pltpu.CompilerParams(vmem_limit_bytes=16 * MIB),
    )(*fields, *sums)


def shifted(value, axis, steps):
    size = lax.axis_size(axis)
    return lax.ppermute(value, axis, [(i, (i + steps) % size) for i in range(size)])


def exchanged(slots, first=0):
    size = lax.axis_size("gz")
    out = []
    for number, value in enumerate(slots):
        d = first + number
        out.append(lax.ppermute(value, "gz", [(i, i ^ d) for i in range(size)]) if d else value)
    return out


def both_sides(send):
    return [shifted(send, "xy", -1), shifted(send, "xy", 1)]


def pad_rows(values, rows=8):
    return jnp.pad(values, ((0, rows - values.shape[0]), (0, 0)))


def edge_tables(nbr_elem, nbr_edge):
    elems = nbr_elem.shape[1]
    me, size = lax.axis_index("xy"), lax.axis_size("xy")
    wall = nbr_elem < 0
    ids = jnp.maximum(nbr_elem, 0)
    owner, local_id = ids // elems, ids % elems
    here = (owner == me) & ~wall
    after = (owner == (me + 1) % size) & ~wall & ~here
    before = ~wall & ~here & ~after
    place = jnp.where(here, nbr_edge % 4 * elems + local_id, -1).reshape(-1)
    source = jnp.arange(4 * elems, dtype=jnp.int32)[:, None]
    local = (source == place[None, :]).astype(jnp.bfloat16)
    first = jnp.arange(LANES) < ROWS

    def ends(table):
        return jnp.where(first[None, :], table[:, :LANES], table[:, elems - LANES :])

    send = jnp.where(first[None, :], before[:, :LANES], after[:, elems - LANES :])
    slot = jnp.where(after, local_id, local_id - (elems - ROWS) + ROWS)
    slot = jnp.where(send, ends(slot), -1).reshape(-1)
    far = (jnp.arange(LANES, dtype=jnp.int32)[:, None] == slot[None, :]).astype(jnp.bfloat16)
    flags = jnp.stack([wall, nbr_edge >= 4], axis=1).astype(jnp.float32)
    flags = jnp.pad(flags, ((0, 0), (0, 6), (0, 0))).reshape(32, elems)
    return local, far, pad_rows(send.astype(jnp.float32)), flags


def per_device(concentration, geometry, nbr_elem, nbr_edge, wall_flags):
    planes, _, elems = concentration.shape
    groups = lax.axis_size("gz")
    me = lax.axis_index("gz")
    fold = Fold(elems // groups)
    scale_x, scale_y = geometry[0], geometry[1]
    geo = pad_rows(jnp.stack([1.0 / (scale_x * scale_y), scale_x * scale_x, scale_y * scale_y]))
    mine = lax.dynamic_slice_in_dim(geo, me * fold.width, fold.width, axis=1)
    mine = jnp.tile(mine, (1, fold.parts))
    index = me.astype(jnp.int32).reshape(1)
    mode_ids = me * planes + jnp.arange(planes, dtype=jnp.int32)
    wave = ((mode_ids + 1) // 2).astype(jnp.float32)
    mass = jnp.broadcast_to(
        (1.0 / time_step + axial_stiffness * wave * wave)[:, None], (planes, LANES)
    )
    flag = jnp.broadcast_to(wall_flags.astype(jnp.float32)[:, None], (planes, LANES))
    tables = edge_tables(nbr_elem, nbr_edge)
    near_sent = pack(index, concentration, fold, groups, 0)
    far_sent = list(pack(index, concentration, fold, groups, groups // 2))
    half = groups // 2
    near_field = exchanged(near_sent)
    near_field[2], far_sent[-1] = lax.optimization_barrier((near_field[2], far_sent[-1]))
    far_field = exchanged(far_sent, half)
    near_field, geo, mine, mass, flag, tables = lax.optimization_barrier(
        (near_field, geo, mine, mass, flag, tables)
    )
    local, far, mask, edges = tables
    near = some_terms(index, mine, near_field, fold, 0, half)
    far_terms = some_terms(index, mine, far_field[:-1], fold, half, half)
    sizes = [planes - 8, 8] if planes > 16 else [planes]
    tables = transform_tables(planes * groups)
    sent, far_terms = far_modes(
        index, mine, tables, near, far_terms, far_field[-1], fold, half, sizes
    )
    far_parts = [exchanged(piece, groups // 2) for piece in sent]
    near_parts = exchanged(near_modes(index, mine, tables, near, far_terms, fold, planes))
    fields, images, sums, sends = [], [], [], []
    start = 0
    for piece, size in enumerate(sizes):
        parts = near_parts + far_parts[piece]
        field, send = unpack(index, mask, parts, fold, sends)
        sends = [send]
        image, more = apply_local([field], start, geo, mass, flag, local, edges, True)
        start += size
        mask, more = lax.optimization_barrier((mask, more))
        fields.append(field)
        images.append(image)
        sums.append(more)
    halo = both_sides(sends[0])
    *images, send, sums = first_far(images, fields, halo, far, edges, mask, sums)
    (more,) = apply_local(images, 0, geo, mass, flag, local, edges, False)
    packed = second_far(images, both_sides(send), far, edges, sums, more)
    size = lax.axis_size("xy")
    pairs = [value for pair in zip(fields, images) for value in pair]
    return finish(pairs, [packed] + [shifted(packed, "xy", k) for k in range(1, size)])


def solution(mesh):
    return jax.shard_map(
        per_device,
        mesh=mesh,
        in_specs=(P("gz", None, "xy"), P(None, "xy"), P(None, "xy"), P(None, "xy"), P("gz")),
        out_specs=P("gz", None, "xy"),
        check_vma=False,
    )
```

```python
import functools

import jax
import jax.numpy as jnp
import ml_dtypes
import numpy as np
from jax import lax
from jax.experimental import pallas as pl
from jax.experimental.pallas import tpu as pltpu
from jax.sharding import PartitionSpec as P

ROWS = 64
LANES = 128
MIB = 1024 * 1024

time_step = 0.2
axial_stiffness = 0.002
plane_stiffness = 1.0
edge_penalty = 4.0
axial_mobility = 0.002
mobility_floor = 0.05


def point_tables():
    degree = 7
    points = np.arange(degree + 1)
    theta = np.pi * points / degree
    nodes_x = np.cos(theta)
    signs = np.where((points == 0) | (points == degree), 2.0, 1.0) * (-1.0) ** points
    differ = nodes_x[:, None] - nodes_x[None, :]
    deriv = np.outer(signs, 1.0 / signs) / (differ + np.eye(degree + 1))
    deriv = deriv - np.eye(degree + 1) * deriv.sum(axis=1)[:, None]
    inner = np.ones(degree - 1)
    for number in range(1, (degree - 1) // 2 + 1):
        inner = inner - 2.0 * np.cos(2 * number * theta[1:degree]) / (4 * number * number - 1)
    weights = np.zeros(degree + 1)
    weights[1:degree] = 2.0 * inner / degree
    weights[0] = 1.0 / degree**2
    weights[degree] = 1.0 / degree**2
    return (deriv, weights)


def fourier_table(length):
    planes = np.arange(length)
    wave_no = (planes + 1) // 2
    phase = np.outer(wave_no, planes) % length * (2.0 * np.pi / length)
    table = np.where((planes % 2 == 1)[:, None], np.cos(phase), np.sin(phase)) * np.sqrt(
        2.0 / length
    )
    table[0] = 1.0 / np.sqrt(length)
    table[length - 1] = np.cos(phase[length - 1]) / np.sqrt(length)
    return table


DERIV, WEIGHTS = point_tables()
BACK = DERIV.T * WEIGHTS[None, :]
STIFF = BACK @ DERIV
BACK_SCALED = BACK / WEIGHTS[:, None]


def two_parts(table):
    upper = table.astype(np.float32).astype(ml_dtypes.bfloat16)
    lower = (table - upper.astype(np.float64)).astype(np.float32).astype(ml_dtypes.bfloat16)
    return upper, lower


def split(value):
    upper = value.astype(jnp.bfloat16)
    lower = (value - upper.astype(jnp.float32)).astype(jnp.bfloat16)
    return upper, lower


class Fold:
    def __init__(self, width):
        self.width = width
        self.parts = LANES // width
        self.fold_j = 2 if self.parts >= 2 else 1
        self.fold_i = 2 if self.parts >= 4 else 1
        self.count_j = 8 // self.fold_j
        self.count_i = 8 // self.fold_i
        self.slots = self.count_j * self.count_i

    def slot(self, jp, ip):
        return jp * self.count_i + ip

    def node(self, jp, ip, part):
        half_j, half_i = part // self.fold_i, part % self.fold_i
        j = 7 - jp if half_j else jp
        i = 7 - ip if half_i else ip
        return 8 * j + i

    def place(self, node):
        j, i = node // 8, node % 8
        half_j = 1 if j >= self.count_j else 0
        half_i = 1 if i >= self.count_i else 0
        jp = 7 - j if half_j else j
        ip = 7 - i if half_i else i
        return self.slot(jp, ip), half_j * self.fold_i + half_i


def lane_of(shape):
    return lax.broadcasted_iota(jnp.int32, shape, len(shape) - 1)


def rolled(value, lanes):
    lanes = lanes % LANES
    return value if lanes == 0 else pltpu.roll(value, lanes, value.ndim - 1)


def by_part(values, lane, width):
    out = values[0]
    for r in range(1, len(values)):
        out = jnp.where(lane >= r * width, values[r], out)
    return out


def mirrored(value, lane, shift):
    if 2 * shift == LANES:
        return rolled(value, shift)
    return jnp.where((lane & shift) == 0, rolled(value, -shift), rolled(value, shift))


def combine(coefs, values):
    total = None
    for c, v in zip(coefs, values):
        term = v * np.float32(c)
        total = term if total is None else total + term
    return total


def line_apply(matrix, values, sign):
    even = [values[k] + values[7 - k] for k in range(4)]
    odd = [values[k] - values[7 - k] for k in range(4)]
    out = [None] * 8
    for a in range(4):
        from_even = combine([(matrix[a, b] + matrix[a, 7 - b]) / 2 for b in range(4)], even)
        from_odd = combine([(matrix[a, b] - matrix[a, 7 - b]) / 2 for b in range(4)], odd)
        out[a] = from_even + from_odd
        out[7 - a] = from_even - from_odd if sign > 0 else from_odd - from_even
    return out


def derivative_line(matrix, values, back, swap):
    if swap is None:
        return line_apply(matrix, values, -1)
    other = [swap(v) for v in values]
    sign = -1.0 if back else 1.0
    out = []
    for a in range(4):
        coefs = [matrix[a, b] for b in range(4)] + [sign * matrix[a, 7 - b] for b in range(4)]
        out.append(combine(coefs, list(values) + other))
    return out


EDGE_NODES = [
    [t for t in range(8)],
    [8 * t + 7 for t in range(8)],
    [56 + t for t in range(8)],
    [8 * t for t in range(8)],
]


def swapped(me, values):
    bit = 1
    while bit < len(values):
        flip = (me & bit) != 0
        values = [jnp.where(flip, values[r ^ bit], values[r]) for r in range(len(values))]
        bit *= 2
    return values


def pack_kernel(fold, me_ref, c_ref, *out_refs):
    lane = lane_of((c_ref.shape[0], LANES))
    me = me_ref[0]
    for step in range(len(out_refs) // fold.parts):

        @pl.when(pl.program_id(0) == step)
        def _():
            by_node = jnp.swapaxes(c_ref[...], 0, 1)
            for jp in range(fold.count_j):
                for ip in range(fold.count_i):
                    loads = [by_node[fold.node(jp, ip, q)] for q in range(fold.parts)]
                    made = []
                    for r in range(fold.parts):
                        parts = [rolled(loads[q], (q - r) * fold.width) for q in range(fold.parts)]
                        made.append(by_part(parts, lane, fold.width))
                    for p, value in enumerate(swapped(me, made)):
                        out_refs[step * fold.parts + p][fold.slot(jp, ip)] = value


def pack(me, conc, fold, groups, first, count):
    planes, nodes, elems = conc.shape
    offset = first // fold.parts

    def block(step, me_ref):
        return (0, 0, (step + offset) ^ (me_ref[0] // fold.parts))

    slot = jax.ShapeDtypeStruct((fold.slots, planes, LANES), jnp.float32)
    return pl.pallas_call(
        functools.partial(pack_kernel, fold),
        grid_spec=pltpu.PrefetchScalarGridSpec(
            num_scalar_prefetch=1,
            grid=(count // fold.parts,),
            in_specs=[pl.BlockSpec((planes, nodes, LANES), block)],
            out_specs=[pl.BlockSpec(slot.shape, lambda s, me_ref: (0, 0, 0))] * count,
        ),
        out_shape=[slot] * count,
        compiler_params=pltpu.CompilerParams(vmem_limit_bytes=60 * MIB),
        cost_estimate=pl.CostEstimate(
            flops=conc.size, bytes_accessed=4 * conc.size, transcendentals=0
        ),
    )(me, conc)


def plane_terms(fold, y_ref, geo_ref, x_ref, acc_ref, row, base, half):
    lane = lane_of((16, LANES))
    square_x = jnp.broadcast_to(geo_ref[1:2, :], (16, LANES))
    square_y = jnp.broadcast_to(geo_ref[2:3, :], (16, LANES))

    def conc(jp, ip):
        return y_ref[fold.slot(jp, ip), pl.ds(base, 16), :]

    def potential(c):
        square = c * c
        return square * c - c, jnp.maximum(1.0 - square, mobility_floor)

    def flux(fields, swap):
        pairs = [potential(c) for c in fields]
        slope = derivative_line(DERIV, [p[0] for p in pairs], False, swap)
        scaled = [s * p[1] for s, p in zip(slope, pairs)]
        return derivative_line(BACK_SCALED, scaled, True, swap), pairs

    swap_i = None
    if fold.fold_i == 2:
        swap_i = lambda v: mirrored(v, lane, fold.width)
    swap_j = None
    if fold.fold_j == 2:
        swap_j = lambda v: mirrored(v, lane, fold.width * fold.fold_i)
    for jp in range(fold.count_j):
        fields = [conc(jp, ip) for ip in range(fold.count_i)]
        result, _unused = flux(fields, swap_i)
        for ip in range(fold.count_i):
            acc_ref[fold.slot(jp, ip)] = (
                fields[ip] * np.float32(1.0 / time_step) - result[ip] * square_x
            )
    for ip in range(fold.count_i):
        fields = [conc(jp, ip) for jp in range(fold.count_j)]
        result, pairs = flux(fields, swap_j)
        for jp in range(fold.count_j):
            slot = fold.slot(jp, ip)
            explicit = acc_ref[slot] - result[jp] * square_y
            where = pl.ds((slot % 2) * LANES, LANES)
            for kind, value in enumerate((explicit, pairs[jp][0])):
                upper, lower = split(value)
                x_ref[slot // 2, pl.ds(kind * half + row, 16), where] = upper
                x_ref[slot // 2, pl.ds((2 + kind) * half + row, 16), where] = lower


def slot_terms(fold, me, first, count, y_refs, geo_ref, x_ref, acc_ref):
    planes = y_refs[0].shape[1]
    half = count * planes
    for number, y_ref in enumerate(y_refs):
        place = (me ^ (first + number)) % count

        def chunk(part, _, y_ref=y_ref, place=place):
            base = pl.multiple_of(part * 16, 16)
            row = pl.multiple_of(place * planes + base, 16)
            plane_terms(fold, y_ref, geo_ref, x_ref, acc_ref, row, base, half)
            return 0

        lax.fori_loop(0, planes // 16, chunk, 0)


def terms_kernel(fold, first, count, me_ref, geo_ref, *refs):
    y_refs, (x_ref, acc_ref) = refs[:-2], refs[-2:]
    slot_terms(fold, me_ref[0], first, count, y_refs, geo_ref, x_ref, acc_ref)


def far_kernel(fold, count, sizes, me_ref, geo_ref, table_ref, near_ref, given_ref, y_ref, *refs):
    chunks = len(sizes)
    out_refs = [refs[k * chunks : (k + 1) * chunks] for k in range(count)]
    x_ref, acc_ref, result_ref = refs[count * chunks :]
    slot_terms(fold, me_ref[0], 2 * count - 1, count, [y_ref], geo_ref, x_ref, acc_ref)
    transform(fold, 1, me_ref, geo_ref, table_ref, (near_ref, x_ref), out_refs, result_ref)


def near_modes_kernel(fold, me_ref, geo_ref, table_ref, near_ref, far_ref, *refs):
    out_refs, result_ref = [[ref] for ref in refs[:-1]], refs[-1]
    transform(fold, 0, me_ref, geo_ref, table_ref, (near_ref, far_ref), out_refs, result_ref)


def transform(fold, other, me_ref, geo_ref, table_ref, terms, out_refs, result_ref):
    count = len(out_refs)
    half = result_ref.shape[0]
    planes = half // count
    me = me_ref[0]
    mine = me // count
    jac = jnp.broadcast_to(geo_ref[0:1, :], (planes, LANES))
    rows = pl.ds(pl.multiple_of((mine ^ other) * half, 16), half)

    def product(which, data):
        upper, lower = slice(0, 4 * half), slice(4 * half, 6 * half)
        return jnp.dot(
            table_ref[which, rows, upper], data, preferred_element_type=jnp.float32
        ) + jnp.dot(
            table_ref[which, rows, lower], data[: 2 * half], preferred_element_type=jnp.float32
        )

    for pair in range(fold.slots // 2):
        result_ref[...] = product(mine, terms[0][pair]) + product(1 - mine, terms[1][pair])
        for k in range(2):
            slot = 2 * pair + k
            jp, ip = slot // fold.count_i, slot % fold.count_i
            scale = jac * np.float32(WEIGHTS[jp] * WEIGHTS[ip])
            for number, pieces in enumerate(out_refs):
                start = (me ^ number) % count * planes
                for out_ref in pieces:
                    size = out_ref.shape[1]
                    here = pl.ds(pl.multiple_of(start, 8), size)
                    value = result_ref[here, k * LANES : (k + 1) * LANES]
                    out_ref[slot] = value * scale[:size]
                    start = start + size


def small_cost():
    return pl.CostEstimate(flops=1, bytes_accessed=1, transcendentals=0)


def smem():
    return pl.BlockSpec(memory_space=pltpu.SMEM)


def vmem(count):
    return [pl.BlockSpec(memory_space=pltpu.VMEM)] * count


def some_terms(me, geo, fields, fold, first, count):
    slots, planes, _ = fields[0].shape
    size = len(fields) * fields[0].size
    return pl.pallas_call(
        functools.partial(terms_kernel, fold, first, count),
        in_specs=[smem()] + vmem(1 + len(fields)),
        out_specs=vmem(1)[0],
        out_shape=jax.ShapeDtypeStruct(
            (slots // 2, 4 * count * planes, 2 * LANES), jnp.bfloat16
        ),
        scratch_shapes=[pltpu.VMEM((slots, 16, LANES), jnp.float32)],
        compiler_params=pltpu.CompilerParams(vmem_limit_bytes=16 * MIB),
        cost_estimate=pl.CostEstimate(
            flops=80 * size, bytes_accessed=12 * size, transcendentals=0
        ),
    )(me, geo, *fields)


def transform_tables(total):
    table = fourier_table(total).astype(np.float32).astype(np.float64)
    wave = ((np.arange(total) + 1) // 2).astype(np.float64)
    upper, lower = two_parts(table)
    upper_b, lower_b = two_parts(-axial_mobility * (wave * wave)[:, None] * table)
    kinds = [upper, upper_b, upper, upper_b, lower, lower_b]
    halves = np.split(np.stack(kinds), 2, axis=2)
    return jnp.asarray(np.stack([np.concatenate(list(half), axis=1) for half in halves]))


def far_modes(me, geo, tables, near, far, field, fold, count, sizes):
    slots, planes, _ = field.shape
    size = count * field.size
    chunks = len(sizes)
    pieces = [jax.ShapeDtypeStruct((slots, k, LANES), jnp.float32) for k in sizes]
    *outs, far = pl.pallas_call(
        functools.partial(far_kernel, fold, count, sizes),
        in_specs=[smem()] + vmem(5),
        out_specs=vmem(chunks * count + 1),
        input_output_aliases={4: chunks * count},
        out_shape=pieces * count + [jax.ShapeDtypeStruct(near.shape, jnp.bfloat16)],
        scratch_shapes=[
            pltpu.VMEM((slots, 16, LANES), jnp.float32),
            pltpu.VMEM((count * planes, 2 * LANES), jnp.float32),
        ],
        compiler_params=pltpu.CompilerParams(vmem_limit_bytes=24 * MIB),
        cost_estimate=pl.CostEstimate(
            flops=12 * count * planes * size, bytes_accessed=8 * size, transcendentals=0
        ),
    )(me, geo, tables, near, far, field)
    return [outs[k::chunks] for k in range(chunks)], far


def near_modes(me, geo, tables, near, far, fold, planes):
    slots = fold.slots
    count = near.shape[1] // (4 * planes)
    size = count * slots * planes * LANES
    slot = jax.ShapeDtypeStruct((slots, planes, LANES), jnp.float32)
    return pl.pallas_call(
        functools.partial(near_modes_kernel, fold),
        in_specs=[smem()] + vmem(4),
        out_specs=vmem(count),
        out_shape=[slot] * count,
        scratch_shapes=[pltpu.VMEM((count * planes, 2 * LANES), jnp.float32)],
        compiler_params=pltpu.CompilerParams(vmem_limit_bytes=16 * MIB),
        cost_estimate=pl.CostEstimate(
            flops=12 * count * planes * size, bytes_accessed=8 * size, transcendentals=0
        ),
    )(me, geo, tables, near, far)


def edge_send(mask_ref, edge, write):
    for t in range(8):
        total = None
        for a in range(4):
            term = edge(a, t) * mask_ref[a : a + 1, :]
            total = term if total is None else total + term
        write(t, total)


def send_from(field_ref, mask_ref, out_ref, start):
    modes, elems = field_ref.shape[1:]
    lane = lane_of((modes, LANES))

    def edge(a, t):
        node = EDGE_NODES[a][t]
        ends = field_ref[node, :, :LANES], field_ref[node, :, elems - LANES :]
        return jnp.where(lane < ROWS, ends[0], ends[1])

    def write(t, value):
        out_ref[t, start : start + modes, :] = value

    edge_send(mask_ref, edge, write)


def unpack_kernel(fold, groups, start, me_ref, mask_ref, *refs):
    parts, (r0_ref, send_ref) = refs[:groups], refs[-2:]
    modes = r0_ref.shape[1]
    me = me_ref[0]

    def tile(part, _):
        rows = pl.ds(pl.multiple_of(part * 8, 8), 8)
        whole_rows = pl.ds(pl.multiple_of(part * 8 + start, 8), 8)

        def load(ref, slot):
            return ref[slot, rows if ref.shape[1] == modes else whole_rows, :]

        lane = lane_of((8, LANES))
        for k in range(groups // fold.parts):
            block = k ^ (me // fold.parts)
            lanes = pl.ds(pl.multiple_of(block * LANES, LANES), LANES)
            mine = parts[k * fold.parts : (k + 1) * fold.parts]
            for jp in range(fold.count_j):
                for ip in range(fold.count_i):
                    loads = swapped(me, [load(ref, fold.slot(jp, ip)) for ref in mine])
                    for q in range(fold.parts):
                        shifts = [
                            rolled(loads[r], (r - q) * fold.width) for r in range(fold.parts)
                        ]
                        value = by_part(shifts, lane, fold.width)
                        r0_ref[fold.node(jp, ip, q), rows, lanes] = value
        return 0

    lax.fori_loop(0, modes // 8, tile, 0)
    if start:
        send_ref[:, :start, :] = refs[groups][...]
    send_from(r0_ref, mask_ref, send_ref, start)


def unpack(me, mask, parts, fold, sends):
    _, modes, _ = parts[-1].shape
    groups = len(parts)
    elems = groups * fold.width
    start = sum(value.shape[1] for value in sends)
    return pl.pallas_call(
        functools.partial(unpack_kernel, fold, groups, start),
        in_specs=[smem()] + vmem(1 + groups + len(sends)),
        out_specs=vmem(2),
        out_shape=[
            jax.ShapeDtypeStruct((64, modes, elems), jnp.float32),
            jax.ShapeDtypeStruct((8, start + modes, LANES), jnp.float32),
        ],
        compiler_params=pltpu.CompilerParams(vmem_limit_bytes=4 * MIB),
        cost_estimate=small_cost(),
    )(me, mask, *parts, *sends)


def volume(
    field_ref, geo_ref, mass_ref, first, image_ref, sums_ref, row_of_sums, acc_ref, start=0, step=1
):
    modes, elems = field_ref.shape[1:]
    tiles = modes // 8

    def tile(number, _):
        row = pl.multiple_of(number % tiles * 8, 8)
        rows = pl.ds(row, 8)
        sum_rows = pl.ds(row + row_of_sums, 8)
        block = number // tiles * step + start
        lanes = pl.ds(pl.multiple_of(block * LANES, LANES), LANES)
        jac = geo_ref[0:1, lanes] * mass_ref[pl.ds(row + first, 8), :]
        square_x = jnp.broadcast_to(geo_ref[0:1, lanes] * geo_ref[1:2, lanes], (8, LANES))
        square_y = jnp.broadcast_to(geo_ref[0:1, lanes] * geo_ref[2:3, lanes], (8, LANES))
        stiff = plane_stiffness * STIFF
        for j in range(8):
            values = [field_ref[8 * j + i, rows, lanes] for i in range(8)]
            result = line_apply(stiff, values, 1)
            scale = square_x * np.float32(WEIGHTS[j])
            mass = jac * np.float32(WEIGHTS[j])
            for i in range(8):
                acc_ref[8 * j + i] = result[i] * scale + (mass * np.float32(WEIGHTS[i])) * values[i]
        totals = [None, None]
        for i in range(8):
            values = [field_ref[8 * j + i, rows, lanes] for j in range(8)]
            result = line_apply(stiff, values, 1)
            scale = square_y * np.float32(WEIGHTS[i])
            for j in range(8):
                image = acc_ref[8 * j + i] + result[j] * scale
                if image_ref is not None:
                    image_ref[8 * j + i, rows, lanes] = image
                for k, term in enumerate((values[j] * values[j], values[j] * image)):
                    totals[k] = term if totals[k] is None else totals[k] + term
        for k in range(2):
            sums_ref[k, sum_rows, :] += totals[k]
        return 0

    blocks = -(-(elems // LANES - start) // step)
    lax.fori_loop(0, tiles * blocks, tile, 0)


def inner_kernel(field_ref, geo_ref, mass_ref, sums_ref, acc_ref):
    sums_ref[...] = jnp.zeros_like(sums_ref)
    blocks = field_ref.shape[2] // LANES
    for block in range(1, blocks - 1):
        volume(field_ref, geo_ref, mass_ref, 0, None, sums_ref, 0, acc_ref, block, blocks)


def inner_sums(field, geo, mass):
    _, modes, _ = field.shape
    return pl.pallas_call(
        inner_kernel,
        in_specs=vmem(3),
        out_specs=vmem(1)[0],
        out_shape=jax.ShapeDtypeStruct((2, modes, LANES), jnp.float32),
        scratch_shapes=[pltpu.VMEM((64, 8, LANES), jnp.float32)],
        compiler_params=pltpu.CompilerParams(vmem_limit_bytes=4 * MIB),
        cost_estimate=small_cost(),
    )(field, geo, mass)


def fill_pairs(target_ref, first, modes, lanes, value_of, parts):
    total = target_ref.shape[0] // (8 * parts)
    for t in range(0, 8, 2):
        pieces = split(jnp.concatenate([value_of(t), value_of(t + 1)], axis=0))
        for part in range(parts):
            row = (8 * part + t) * total
            target_ref[pl.ds(row, 2 * total), lanes] = pieces[part]


def gathered(trace_ref, table, parts):
    value = jnp.dot(trace_ref[...], table, preferred_element_type=jnp.float32)
    if parts == 2:
        half = value.shape[0] // 2
        value = value[:half] + value[half:]
    return value.reshape(8, value.shape[0] // 8, value.shape[1])


def local_edges(fields, first, flag_ref, local_ref, edges_ref, trace_ref, val_ref, parts, visit):
    elems = val_ref.shape[2]
    for a in range(4):

        def value_of(t):
            pieces = [field_ref[EDGE_NODES[a][t]] for field_ref in fields]
            return pieces[0] if len(pieces) == 1 else jnp.concatenate(pieces, axis=0)

        fill_pairs(trace_ref, 0, 0, pl.ds(a * elems, elems), value_of, parts)
    for edge in range(4):
        val_ref[...] = gathered(
            trace_ref, local_ref[:, edge * elems : (edge + 1) * elems], parts
        )
        for block in range(elems // LANES):
            lanes = pl.ds(block * LANES, LANES)
            wall = edges_ref[8 * edge : 8 * edge + 1, lanes]
            flip = edges_ref[8 * edge + 1 : 8 * edge + 2, lanes]
            start = 0
            for chunk, field_ref in enumerate(fields):
                modes = field_ref.shape[1]
                rows = slice(start, start + modes)
                start += modes
                turned = jnp.broadcast_to(flip, (modes, LANES)) > 0.5
                coef = 1.0 - wall * (1.0 - flag_ref[first + start - modes : first + start])
                for t in range(8):
                    node = EDGE_NODES[edge][t]
                    value = field_ref[node, :, lanes]
                    other = jnp.where(turned, val_ref[7 - t, rows, lanes], val_ref[t, rows, lanes])
                    weight = np.float32(edge_penalty * WEIGHTS[t])
                    visit(chunk, rows, node, lanes, value, weight * (coef * value - other))


def far_edges(after_ref, before_ref, far_ref, edges_ref, trace_ref, elems, visit):
    modes = after_ref.shape[1]
    lane = lane_of((modes, LANES))

    def value_of(t):
        return jnp.where(lane < ROWS, after_ref[t], before_ref[t])

    fill_pairs(trace_ref, 0, modes, pl.ds(0, LANES), value_of, 2)
    for edge in range(4):
        values = gathered(trace_ref, far_ref[:, edge * LANES : (edge + 1) * LANES], 2)
        flips = edges_ref[8 * edge + 1 : 8 * edge + 2, :]
        flip = jnp.where(lane < ROWS, flips[:, :LANES], flips[:, elems - LANES :])
        for t in range(8):
            other = jnp.where(flip > 0.5, values[7 - t], values[t])
            visit(edge, t, other * np.float32(-edge_penalty * WEIGHTS[t]))


def apply_kernel(want_image, count, first, given, *refs):
    fields, refs = refs[:count], refs[count:]
    inner, refs = refs[:given], refs[given:]
    geo_ref, mass_ref, flag_ref, local_ref, edges_ref = refs[:5]
    refs = refs[5:]
    image_ref = refs[0] if want_image else None
    sums_ref, trace_ref, val_ref, acc_ref = refs[-4:]
    sums_ref[...] = jnp.zeros_like(sums_ref)
    start = 0
    for field_ref in fields:
        row = first + start
        step = 1
        if inner and start == 0:
            sums_ref[:, : field_ref.shape[1], :] = inner[0][...]
            step = field_ref.shape[2] // LANES - 1
        volume(field_ref, geo_ref, mass_ref, row, image_ref, sums_ref, start, acc_ref, 0, step)
        start += field_ref.shape[1]
    totals = [None] * count

    def visit(chunk, rows, node, lanes, value, term):
        if want_image:
            image_ref[node, :, lanes] += term
        product = value * term
        totals[chunk] = product if totals[chunk] is None else totals[chunk] + product

    parts = 2 if want_image else 1
    local_edges(
        fields, first, flag_ref, local_ref, edges_ref, trace_ref, val_ref, parts, visit
    )
    start = 0
    for chunk, field_ref in enumerate(fields):
        rows = slice(start, start + field_ref.shape[1])
        start = rows.stop
        sums_ref[1, rows, :] += totals[chunk]


def apply_local(fields, first, geo, mass, flag, local, edges, want_image, inner=()):
    elems = fields[0].shape[2]
    modes = sum(field.shape[1] for field in fields)
    sums = jax.ShapeDtypeStruct((2, modes, LANES), jnp.float32)
    shapes = [jax.ShapeDtypeStruct(fields[0].shape, jnp.float32), sums] if want_image else [sums]
    parts = 2 if want_image else 1
    return pl.pallas_call(
        functools.partial(apply_kernel, want_image, len(fields), first, len(inner)),
        in_specs=vmem(5 + len(fields) + len(inner)),
        out_specs=vmem(len(shapes)),
        out_shape=shapes,
        scratch_shapes=[
            pltpu.VMEM((parts * 8 * modes, 4 * elems), jnp.bfloat16),
            pltpu.VMEM((8, modes, elems), jnp.float32),
            pltpu.VMEM((64, 8, LANES), jnp.float32),
        ],
        compiler_params=pltpu.CompilerParams(vmem_limit_bytes=16 * MIB),
        cost_estimate=small_cost(),
    )(*fields, *inner, geo, mass, flag, local, edges)


def ends_of(node, field_refs, lane):
    elems = field_refs[0].shape[2]
    pieces = []
    for ref in field_refs:
        pieces.append((ref[node, :, :LANES], ref[node, :, elems - LANES :]))
    first = [p[0] for p in pieces]
    last = [p[1] for p in pieces]
    if len(pieces) > 1:
        first, last = [jnp.concatenate(first, axis=0)], [jnp.concatenate(last, axis=0)]
    return jnp.where(lane < ROWS, first[0], last[0])


def first_far_kernel(count, *refs):
    images, fields, refs = refs[:count], refs[count : 2 * count], refs[2 * count :]
    sum_refs, refs = refs[:count], refs[count:]
    after_ref, before_ref, far_ref, edges_ref, mask_ref = refs[:5]
    outs, (send_ref, out_ref, trace_ref) = refs[5 : 5 + count], refs[5 + count :]
    modes = after_ref.shape[1]
    elems = fields[0].shape[2]
    lane = lane_of((modes, LANES))
    sums = [[ref[k] for ref in sum_refs] for k in range(2)]
    sums = [jnp.concatenate(pieces, axis=0) if count > 1 else pieces[0] for pieces in sums]
    totals = [sums[1]]
    done = set()

    def visit(edge, t, term):
        node = EDGE_NODES[edge][t]
        totals[0] = totals[0] + ends_of(node, fields, lane) * term
        start = 0
        for image_ref, ref in zip(images, outs):
            size = ref.shape[1]
            part = term[start : start + size]
            here = lane_of((size, LANES)) < ROWS
            start += size
            source = ref if node in done else image_ref
            ref[node, :, :LANES] = source[node, :, :LANES] + jnp.where(here, part, 0.0)
            ref[node, :, elems - LANES :] = source[node, :, elems - LANES :] + jnp.where(
                here, 0.0, part
            )
        done.add(node)

    far_edges(after_ref, before_ref, far_ref, edges_ref, trace_ref, elems, visit)
    out_ref[0] = sums[0]
    out_ref[1] = totals[0]
    start = 0
    for ref in outs:
        send_from(ref, mask_ref, send_ref, start)
        start += ref.shape[1]


def first_far(images, fields, halo, far, edges, mask, sums):
    count = len(fields)
    modes = sum(value.shape[1] for value in sums)
    return pl.pallas_call(
        functools.partial(first_far_kernel, count),
        in_specs=vmem(3 * count + 5),
        out_specs=vmem(count + 2),
        out_shape=[jax.ShapeDtypeStruct(image.shape, jnp.float32) for image in images]
        + [
            jax.ShapeDtypeStruct((8, modes, LANES), jnp.float32),
            jax.ShapeDtypeStruct((2, modes, LANES), jnp.float32),
        ],
        scratch_shapes=[pltpu.VMEM((16 * modes, LANES), jnp.bfloat16)],
        input_output_aliases={k: k for k in range(count)},
        compiler_params=pltpu.CompilerParams(vmem_limit_bytes=8 * MIB),
        cost_estimate=small_cost(),
    )(*images, *fields, *sums, *halo, far, edges, mask)


def second_far_kernel(count, *refs):
    fields, refs = refs[:count], refs[count:]
    after_ref, before_ref, far_ref, edges_ref, first_ref, more_ref, out_ref, trace_ref = refs
    modes = after_ref.shape[1]
    elems = fields[0].shape[2]
    lane = lane_of((modes, LANES))
    totals = [more_ref[1]]

    def visit(edge, t, term):
        totals[0] = totals[0] + ends_of(EDGE_NODES[edge][t], fields, lane) * term

    far_edges(after_ref, before_ref, far_ref, edges_ref, trace_ref, elems, visit)
    sums = [first_ref[0], first_ref[1], more_ref[0], totals[0]]
    packed = jnp.zeros((modes, LANES), jnp.float32)
    for k, value in enumerate(sums):
        packed = jnp.where(lane == k, jnp.sum(value, axis=1, keepdims=True), packed)
    out_ref[...] = packed


def second_far(fields, halo, far, edges, first, more):
    modes = first.shape[1]
    return pl.pallas_call(
        functools.partial(second_far_kernel, len(fields)),
        in_specs=vmem(6 + len(fields)),
        out_specs=vmem(1)[0],
        out_shape=jax.ShapeDtypeStruct((modes, LANES), jnp.float32),
        scratch_shapes=[pltpu.VMEM((16 * modes, LANES), jnp.bfloat16)],
        compiler_params=pltpu.CompilerParams(vmem_limit_bytes=8 * MIB),
        cost_estimate=small_cost(),
    )(*fields, *halo, far, edges, first, more)


def finish_kernel(count, chunks, *refs):
    fields, refs = refs[: 2 * chunks], refs[2 * chunks :]
    sum_refs, (out_ref, buffer_ref, sems) = refs[:count], refs[count:]
    total = sum_refs[0][...]
    for ref in sum_refs[1:]:
        total = total + ref[...]
    m0, m1, m2, m3 = [total[:, k : k + 1] for k in range(4)]
    alpha = m0 / m1
    norm = alpha * (alpha * m2) - 2.0 * (alpha * m1) + m0
    energy = m1 - 2.0 * (alpha * m2) + alpha * (alpha * m3)
    beta = norm / m0
    second = norm / (energy - beta * (norm / alpha))
    on_r = jnp.broadcast_to(alpha + second * (1.0 + beta), total.shape)
    on_q = jnp.broadcast_to(second * alpha, total.shape)
    elems = out_ref.shape[2]
    slots = buffer_ref.shape[0]
    tiles = total.shape[0] // 8

    def copy(tile):
        target = out_ref.at[pl.ds(8 * tile, 8)]
        return pltpu.make_async_copy(buffer_ref.at[tile % slots], target, sems.at[tile % slots])

    tile = 0
    for chunk in range(chunks):
        r0_ref, q0_ref = fields[2 * chunk : 2 * chunk + 2]
        for first in range(0, r0_ref.shape[1], 8):
            if tile >= slots:
                copy(tile - slots).wait()
            mine = slice(8 * tile, 8 * tile + 8)
            rows = slice(first, first + 8)
            on_r0, on_q0 = on_r[mine], on_q[mine]
            for block in range(elems // LANES):
                lanes = slice(block * LANES, (block + 1) * LANES)
                for j in range(8):
                    nodes = slice(8 * j, 8 * j + 8)
                    value = on_r0 * r0_ref[nodes, rows, lanes] - on_q0 * q0_ref[nodes, rows, lanes]
                    buffer_ref[tile % slots, :, nodes, lanes] = jnp.swapaxes(value, 0, 1)
            copy(tile).start()
            tile += 1
    for left in range(max(tiles - slots, 0), tiles):
        copy(left).wait()


def finish(fields, sums):
    elems = fields[0].shape[2]
    total = sums[0].shape[0]
    slots = min(4, total // 8)
    return pl.pallas_call(
        functools.partial(finish_kernel, len(sums), len(fields) // 2),
        in_specs=vmem(len(fields) + len(sums)),
        out_specs=pl.BlockSpec(memory_space=pl.ANY),
        out_shape=jax.ShapeDtypeStruct((total, 64, elems), jnp.float32),
        scratch_shapes=[
            pltpu.VMEM((slots, 8, 64, elems), jnp.float32),
            pltpu.SemaphoreType.DMA((slots,)),
        ],
        compiler_params=pltpu.CompilerParams(vmem_limit_bytes=16 * MIB),
    )(*fields, *sums)


def shifted(value, axis, steps):
    size = lax.axis_size(axis)
    return lax.ppermute(value, axis, [(i, (i + steps) % size) for i in range(size)])


def exchanged(slots, first=0):
    size = lax.axis_size("gz")
    out = []
    for number, value in enumerate(slots):
        d = first + number
        out.append(lax.ppermute(value, "gz", [(i, i ^ d) for i in range(size)]) if d else value)
    return out


def both_sides(send):
    return [shifted(send, "xy", -1), shifted(send, "xy", 1)]


def pad_rows(values, rows=8):
    return jnp.pad(values, ((0, rows - values.shape[0]), (0, 0)))


def edge_tables(nbr_elem, nbr_edge):
    elems = nbr_elem.shape[1]
    me, size = lax.axis_index("xy"), lax.axis_size("xy")
    wall = nbr_elem < 0
    ids = jnp.maximum(nbr_elem, 0)
    owner, local_id = ids // elems, ids % elems
    here = (owner == me) & ~wall
    after = (owner == (me + 1) % size) & ~wall & ~here
    before = ~wall & ~here & ~after
    place = jnp.where(here, nbr_edge % 4 * elems + local_id, -1).reshape(-1)
    source = jnp.arange(4 * elems, dtype=jnp.int32)[:, None]
    local = (source == place[None, :]).astype(jnp.bfloat16)
    first = jnp.arange(LANES) < ROWS

    def ends(table):
        return jnp.where(first[None, :], table[:, :LANES], table[:, elems - LANES :])

    send = jnp.where(first[None, :], before[:, :LANES], after[:, elems - LANES :])
    slot = jnp.where(after, local_id, local_id - (elems - ROWS) + ROWS)
    slot = jnp.where(send, ends(slot), -1).reshape(-1)
    far = (jnp.arange(LANES, dtype=jnp.int32)[:, None] == slot[None, :]).astype(jnp.bfloat16)
    flags = jnp.stack([wall, nbr_edge >= 4], axis=1).astype(jnp.float32)
    flags = jnp.pad(flags, ((0, 0), (0, 6), (0, 0))).reshape(32, elems)
    return local, far, pad_rows(send.astype(jnp.float32)), flags


def per_device(concentration, geometry, nbr_elem, nbr_edge, wall_flags):
    planes, _, elems = concentration.shape
    groups = lax.axis_size("gz")
    me = lax.axis_index("gz")
    fold = Fold(elems // groups)
    scale_x, scale_y = geometry[0], geometry[1]
    geo = pad_rows(jnp.stack([1.0 / (scale_x * scale_y), scale_x * scale_x, scale_y * scale_y]))
    mine = lax.dynamic_slice_in_dim(geo, me * fold.width, fold.width, axis=1)
    mine = jnp.tile(mine, (1, fold.parts))
    index = me.astype(jnp.int32).reshape(1)
    mode_ids = me * planes + jnp.arange(planes, dtype=jnp.int32)
    wave = ((mode_ids + 1) // 2).astype(jnp.float32)
    mass = jnp.broadcast_to(
        (1.0 / time_step + axial_stiffness * wave * wave)[:, None], (planes, LANES)
    )
    flag = jnp.broadcast_to(wall_flags.astype(jnp.float32)[:, None], (planes, LANES))
    tables = edge_tables(nbr_elem, nbr_edge)
    half = groups // 2
    far_sent = list(pack(index, concentration, fold, groups, half, fold.parts))
    more = half - fold.parts
    far_sent += pack(index, concentration, fold, groups, half + fold.parts, more) if more else []
    near_sent = pack(index, concentration, fold, groups, 0, half)
    near_field = exchanged(near_sent)
    near_field[2], far_sent[-1] = lax.optimization_barrier((near_field[2], far_sent[-1]))
    far_field = exchanged(far_sent, half)
    near_field, geo, mine, mass, flag, tables = lax.optimization_barrier(
        (near_field, geo, mine, mass, flag, tables)
    )
    local, far, mask, edges = tables
    near = some_terms(index, mine, near_field, fold, 0, half)
    far_terms = some_terms(index, mine, far_field[:-1], fold, half, half)
    sizes = [planes - 8, 8] if planes > 16 else [planes]
    tables = transform_tables(planes * groups)
    sent, far_terms = far_modes(
        index, mine, tables, near, far_terms, far_field[-1], fold, half, sizes
    )
    far_parts = [exchanged(piece, groups // 2) for piece in sent]
    near_parts = exchanged(near_modes(index, mine, tables, near, far_terms, fold, planes))
    fields, images, sums, sends, inner = [], [], [], [], []
    start = 0
    for piece, size in enumerate(sizes):
        parts = near_parts + far_parts[piece]
        field, send = unpack(index, mask, parts, fold, sends)
        sends = [send]
        image, more = apply_local([field], start, geo, mass, flag, local, edges, True)
        start += size
        if piece + 1 < len(sizes):
            inner = [inner_sums(image, geo, mass)]
            mask, inner = lax.optimization_barrier((mask, inner))
        fields.append(field)
        images.append(image)
        sums.append(more)
    halo = both_sides(sends[0])
    *images, send, sums = first_far(images, fields, halo, far, edges, mask, sums)
    (more,) = apply_local(images, 0, geo, mass, flag, local, edges, False, inner)
    packed = second_far(images, both_sides(send), far, edges, sums, more)
    size = lax.axis_size("xy")
    pairs = [value for pair in zip(fields, images) for value in pair]
    return finish(pairs, [packed] + [shifted(packed, "xy", k) for k in range(1, size)])


def solution(mesh):
    return jax.shard_map(
        per_device,
        mesh=mesh,
        in_specs=(P("gz", None, "xy"), P(None, "xy"), P(None, "xy"), P(None, "xy"), P("gz")),
        out_specs=P("gz", None, "xy"),
        check_vma=False,
    )
```

```python
import functools

import jax
import jax.numpy as jnp
import ml_dtypes
import numpy as np
from jax import lax
from jax.experimental import pallas as pl
from jax.experimental.pallas import tpu as pltpu
from jax.sharding import PartitionSpec as P

ROWS = 64
LANES = 128
MIB = 1024 * 1024

time_step = 0.2
axial_stiffness = 0.002
plane_stiffness = 1.0
edge_penalty = 4.0
axial_mobility = 0.002
mobility_floor = 0.05


def point_tables():
    degree = 7
    points = np.arange(degree + 1)
    theta = np.pi * points / degree
    nodes_x = np.cos(theta)
    signs = np.where((points == 0) | (points == degree), 2.0, 1.0) * (-1.0) ** points
    differ = nodes_x[:, None] - nodes_x[None, :]
    deriv = np.outer(signs, 1.0 / signs) / (differ + np.eye(degree + 1))
    deriv = deriv - np.eye(degree + 1) * deriv.sum(axis=1)[:, None]
    inner = np.ones(degree - 1)
    for number in range(1, (degree - 1) // 2 + 1):
        inner = inner - 2.0 * np.cos(2 * number * theta[1:degree]) / (4 * number * number - 1)
    weights = np.zeros(degree + 1)
    weights[1:degree] = 2.0 * inner / degree
    weights[0] = 1.0 / degree**2
    weights[degree] = 1.0 / degree**2
    return (deriv, weights)


def fourier_table(length):
    planes = np.arange(length)
    wave_no = (planes + 1) // 2
    phase = np.outer(wave_no, planes) % length * (2.0 * np.pi / length)
    table = np.where((planes % 2 == 1)[:, None], np.cos(phase), np.sin(phase)) * np.sqrt(
        2.0 / length
    )
    table[0] = 1.0 / np.sqrt(length)
    table[length - 1] = np.cos(phase[length - 1]) / np.sqrt(length)
    return table


DERIV, WEIGHTS = point_tables()
BACK = DERIV.T * WEIGHTS[None, :]
STIFF = BACK @ DERIV
BACK_SCALED = BACK / WEIGHTS[:, None]


def two_parts(table):
    upper = table.astype(np.float32).astype(ml_dtypes.bfloat16)
    lower = (table - upper.astype(np.float64)).astype(np.float32).astype(ml_dtypes.bfloat16)
    return upper, lower


def split(value):
    upper = value.astype(jnp.bfloat16)
    lower = (value - upper.astype(jnp.float32)).astype(jnp.bfloat16)
    return upper, lower


class Fold:
    def __init__(self, width):
        self.width = width
        self.parts = LANES // width
        self.fold_j = 2 if self.parts >= 2 else 1
        self.fold_i = 2 if self.parts >= 4 else 1
        self.count_j = 8 // self.fold_j
        self.count_i = 8 // self.fold_i
        self.slots = self.count_j * self.count_i

    def slot(self, jp, ip):
        return jp * self.count_i + ip

    def node(self, jp, ip, part):
        half_j, half_i = part // self.fold_i, part % self.fold_i
        j = 7 - jp if half_j else jp
        i = 7 - ip if half_i else ip
        return 8 * j + i

    def place(self, node):
        j, i = node // 8, node % 8
        half_j = 1 if j >= self.count_j else 0
        half_i = 1 if i >= self.count_i else 0
        jp = 7 - j if half_j else j
        ip = 7 - i if half_i else i
        return self.slot(jp, ip), half_j * self.fold_i + half_i


def lane_of(shape):
    return lax.broadcasted_iota(jnp.int32, shape, len(shape) - 1)


def rolled(value, lanes):
    lanes = lanes % LANES
    return value if lanes == 0 else pltpu.roll(value, lanes, value.ndim - 1)


def by_part(values, lane, width):
    out = values[0]
    for r in range(1, len(values)):
        out = jnp.where(lane >= r * width, values[r], out)
    return out


def mirrored(value, lane, shift):
    if 2 * shift == LANES:
        return rolled(value, shift)
    return jnp.where((lane & shift) == 0, rolled(value, -shift), rolled(value, shift))


def combine(coefs, values):
    total = None
    for c, v in zip(coefs, values):
        term = v * np.float32(c)
        total = term if total is None else total + term
    return total


def line_apply(matrix, values, sign):
    even = [values[k] + values[7 - k] for k in range(4)]
    odd = [values[k] - values[7 - k] for k in range(4)]
    out = [None] * 8
    for a in range(4):
        from_even = combine([(matrix[a, b] + matrix[a, 7 - b]) / 2 for b in range(4)], even)
        from_odd = combine([(matrix[a, b] - matrix[a, 7 - b]) / 2 for b in range(4)], odd)
        out[a] = from_even + from_odd
        out[7 - a] = from_even - from_odd if sign > 0 else from_odd - from_even
    return out


def derivative_line(matrix, values, mirror):
    if mirror is None:
        return line_apply(matrix, values, -1)
    swap, sign, first = mirror
    mixed = [swap(v) + v * sign for v in values]
    out = []
    for a in range(4):
        total = None
        for b in range(4):
            upper = np.float32((matrix[a, b] + matrix[a, 7 - b]) / 2)
            lower = np.float32((matrix[a, b] - matrix[a, 7 - b]) / 2)
            term = mixed[b] * jnp.where(first, upper, lower)
            total = term if total is None else total + term
        out.append(total + swap(total) * sign)
    return out


EDGE_NODES = [
    [t for t in range(8)],
    [8 * t + 7 for t in range(8)],
    [56 + t for t in range(8)],
    [8 * t for t in range(8)],
]


def swapped(me, values):
    bit = 1
    while bit < len(values):
        flip = (me & bit) != 0
        values = [jnp.where(flip, values[r ^ bit], values[r]) for r in range(len(values))]
        bit *= 2
    return values


def pack_kernel(fold, me_ref, c_ref, *out_refs):
    lane = lane_of((c_ref.shape[0], LANES))
    me = me_ref[0]
    for step in range(len(out_refs) // fold.parts):

        @pl.when(pl.program_id(0) == step)
        def _():
            by_node = jnp.swapaxes(c_ref[...], 0, 1)
            for jp in range(fold.count_j):
                for ip in range(fold.count_i):
                    loads = [by_node[fold.node(jp, ip, q)] for q in range(fold.parts)]
                    made = []
                    for r in range(fold.parts):
                        parts = [rolled(loads[q], (q - r) * fold.width) for q in range(fold.parts)]
                        made.append(by_part(parts, lane, fold.width))
                    for p, value in enumerate(swapped(me, made)):
                        out_refs[step * fold.parts + p][fold.slot(jp, ip)] = value


def pack(me, conc, fold, groups, first, count):
    planes, nodes, elems = conc.shape
    offset = first // fold.parts

    def block(step, me_ref):
        return (0, 0, (step + offset) ^ (me_ref[0] // fold.parts))

    slot = jax.ShapeDtypeStruct((fold.slots, planes, LANES), jnp.float32)
    return pl.pallas_call(
        functools.partial(pack_kernel, fold),
        grid_spec=pltpu.PrefetchScalarGridSpec(
            num_scalar_prefetch=1,
            grid=(count // fold.parts,),
            in_specs=[pl.BlockSpec((planes, nodes, LANES), block)],
            out_specs=[pl.BlockSpec(slot.shape, lambda s, me_ref: (0, 0, 0))] * count,
        ),
        out_shape=[slot] * count,
        compiler_params=pltpu.CompilerParams(vmem_limit_bytes=60 * MIB),
        cost_estimate=pl.CostEstimate(
            flops=conc.size, bytes_accessed=4 * conc.size, transcendentals=0
        ),
    )(me, conc)


def plane_terms(fold, y_ref, geo_ref, x_ref, acc_ref, row, base, half):
    lane = lane_of((16, LANES))
    square_x = jnp.broadcast_to(geo_ref[1:2, :], (16, LANES))
    square_y = jnp.broadcast_to(geo_ref[2:3, :], (16, LANES))

    def mirror(shift):
        first = (lane & shift) == 0
        return (lambda v: mirrored(v, lane, shift), jnp.where(first, 1.0, -1.0), first)

    mirror_i = mirror(fold.width) if fold.fold_i == 2 else None
    mirror_j = mirror(fold.width * fold.fold_i) if fold.fold_j == 2 else None
    for jp in range(fold.count_j):
        chem, mobility = [], []
        for ip in range(fold.count_i):
            slot = fold.slot(jp, ip)
            c = y_ref[slot, pl.ds(base, 16), :]
            square = c * c
            chem.append(square * c - c)
            mobility.append(jnp.maximum(1.0 - square, mobility_floor))
            acc_ref[0, slot] = c * np.float32(1.0 / time_step)
            acc_ref[1, slot] = chem[ip]
            acc_ref[2, slot] = mobility[ip]
        slope = derivative_line(DERIV, chem, mirror_i)
        result = derivative_line(BACK_SCALED, [s * m for s, m in zip(slope, mobility)], mirror_i)
        for ip in range(fold.count_i):
            acc_ref[0, fold.slot(jp, ip)] -= result[ip] * square_x
    for ip in range(fold.count_i):
        slots = [fold.slot(jp, ip) for jp in range(fold.count_j)]
        chem = [acc_ref[1, slot] for slot in slots]
        slope = derivative_line(DERIV, chem, mirror_j)
        scaled = [s * acc_ref[2, slot] for s, slot in zip(slope, slots)]
        result = derivative_line(BACK_SCALED, scaled, mirror_j)
        for jp, slot in enumerate(slots):
            explicit = acc_ref[0, slot] - result[jp] * square_y
            where = pl.ds((slot % 2) * LANES, LANES)
            for kind, value in enumerate((explicit, chem[jp])):
                upper, lower = split(value)
                x_ref[slot // 2, pl.ds(kind * half + row, 16), where] = upper
                x_ref[slot // 2, pl.ds((2 + kind) * half + row, 16), where] = lower


def slot_terms(fold, me, first, count, y_refs, geo_ref, x_ref, acc_ref):
    planes = y_refs[0].shape[1]
    half = count * planes
    for number, y_ref in enumerate(y_refs):
        place = (me ^ (first + number)) % count

        def chunk(part, _, y_ref=y_ref, place=place):
            base = pl.multiple_of(part * 16, 16)
            row = pl.multiple_of(place * planes + base, 16)
            plane_terms(fold, y_ref, geo_ref, x_ref, acc_ref, row, base, half)
            return 0

        lax.fori_loop(0, planes // 16, chunk, 0)


def terms_kernel(fold, first, count, clear, me_ref, geo_ref, *refs):
    y_refs, (x_ref, acc_ref) = refs[:-2], refs[-2:]
    me = me_ref[0]
    if clear:
        planes = y_refs[0].shape[1]
        place = (me ^ (2 * count - 1)) % count
        for kind in range(4):
            row = pl.multiple_of((kind * count + place) * planes, 16)
            x_ref[:, pl.ds(row, planes), :] = jnp.zeros(
                (x_ref.shape[0], planes, 2 * LANES), jnp.bfloat16
            )
    slot_terms(fold, me, first, count, y_refs, geo_ref, x_ref, acc_ref)


def product(table, data):
    split_at = data.shape[0]
    return jnp.dot(table[:, :split_at], data, preferred_element_type=jnp.float32) + jnp.dot(
        table[:, split_at:], data[: split_at // 2], preferred_element_type=jnp.float32
    )


def rows_of(me, count, planes, other):
    half = count * planes
    return pl.ds(pl.multiple_of((me // count ^ other) * half, 16), half)


def partial_kernel(count, planes, other, me_ref, table_ref, near_ref, far_ref, out_ref):
    mine = me_ref[0] // count
    rows = rows_of(me_ref[0], count, planes, other)
    for pair in range(near_ref.shape[0]):
        out_ref[pair] = product(table_ref[mine, rows, :], near_ref[pair]) + product(
            table_ref[1 - mine, rows, :], far_ref[pair]
        )


def far_kernel(fold, count, sizes, me_ref, geo_ref, last_ref, partial_ref, y_ref, *refs):
    chunks = len(sizes)
    out_refs = [refs[k * chunks : (k + 1) * chunks] for k in range(count)]
    x_ref, acc_ref, result_ref = refs[count * chunks :]
    slot_terms(fold, me_ref[0], 0, 1, [y_ref], geo_ref, x_ref, acc_ref)
    transform(fold, 1, me_ref, geo_ref, last_ref, partial_ref, x_ref, out_refs, result_ref)


def near_modes_kernel(fold, me_ref, geo_ref, last_ref, partial_ref, x_ref, *refs):
    out_refs, result_ref = [[ref] for ref in refs[:-1]], refs[-1]
    transform(fold, 0, me_ref, geo_ref, last_ref, partial_ref, x_ref, out_refs, result_ref)


def transform(fold, other, me_ref, geo_ref, last_ref, partial_ref, x_ref, out_refs, result_ref):
    count = len(out_refs)
    planes = result_ref.shape[0] // count
    me = me_ref[0]
    jac = jnp.broadcast_to(geo_ref[0:1, :], (planes, LANES))
    table = last_ref[rows_of(me, count, planes, other), :]
    for pair in range(fold.slots // 2):
        result_ref[...] = partial_ref[pair] + product(table, x_ref[pair])
        for k in range(2):
            slot = 2 * pair + k
            jp, ip = slot // fold.count_i, slot % fold.count_i
            scale = jac * np.float32(WEIGHTS[jp] * WEIGHTS[ip])
            lanes = slice(k * LANES, (k + 1) * LANES)
            for number, pieces in enumerate(out_refs):
                start = (me ^ number) % count * planes
                for out_ref in pieces:
                    size = out_ref.shape[1]
                    here = pl.ds(pl.multiple_of(start, 8), size)
                    out_ref[slot] = result_ref[here, lanes] * scale[:size]
                    start = start + size


def small_cost():
    return pl.CostEstimate(flops=1, bytes_accessed=1, transcendentals=0)


def smem():
    return pl.BlockSpec(memory_space=pltpu.SMEM)


def vmem(count):
    return [pl.BlockSpec(memory_space=pltpu.VMEM)] * count


def some_terms(me, geo, fields, fold, first, count, clear=False):
    slots, planes, _ = fields[0].shape
    size = len(fields) * fields[0].size
    return pl.pallas_call(
        functools.partial(terms_kernel, fold, first, count, clear),
        in_specs=[smem()] + vmem(1 + len(fields)),
        out_specs=vmem(1)[0],
        out_shape=jax.ShapeDtypeStruct(
            (slots // 2, 4 * count * planes, 2 * LANES), jnp.bfloat16
        ),
        scratch_shapes=[pltpu.VMEM((3, slots, 16, LANES), jnp.float32)],
        compiler_params=pltpu.CompilerParams(vmem_limit_bytes=16 * MIB),
        cost_estimate=pl.CostEstimate(
            flops=80 * size, bytes_accessed=12 * size, transcendentals=0
        ),
    )(me, geo, *fields)


def transform_tables(total, planes):
    table = fourier_table(total).astype(np.float32).astype(np.float64)
    wave = ((np.arange(total) + 1) // 2).astype(np.float64)
    upper, lower = two_parts(table)
    upper_b, lower_b = two_parts(-axial_mobility * (wave * wave)[:, None] * table)
    kinds = np.stack([upper, upper_b, upper, upper_b, lower, lower_b])

    def cut(pieces):
        parts = np.split(kinds, pieces, axis=2)
        return jnp.asarray(np.stack([np.concatenate(list(part), axis=1) for part in parts]))

    return cut(2), cut(total // planes)


def partial_modes(me, tables, near, far, count, planes, other):
    half = count * planes
    shape = (near.shape[0], half, 2 * LANES)
    return pl.pallas_call(
        functools.partial(partial_kernel, count, planes, other),
        in_specs=[smem()] + vmem(3),
        out_specs=vmem(1)[0],
        out_shape=jax.ShapeDtypeStruct(shape, jnp.float32),
        compiler_params=pltpu.CompilerParams(vmem_limit_bytes=16 * MIB),
        cost_estimate=small_cost(),
    )(me, tables, near, far)


def far_modes(me, geo, last, partial, field, fold, count, sizes):
    slots, planes, _ = field.shape
    chunks = len(sizes)
    pieces = [jax.ShapeDtypeStruct((slots, k, LANES), jnp.float32) for k in sizes]
    *outs, terms = pl.pallas_call(
        functools.partial(far_kernel, fold, count, sizes),
        in_specs=[smem()] + vmem(4),
        out_specs=vmem(chunks * count + 1),
        out_shape=pieces * count
        + [jax.ShapeDtypeStruct((slots // 2, 4 * planes, 2 * LANES), jnp.bfloat16)],
        scratch_shapes=[
            pltpu.VMEM((3, slots, 16, LANES), jnp.float32),
            pltpu.VMEM((count * planes, 2 * LANES), jnp.float32),
        ],
        compiler_params=pltpu.CompilerParams(vmem_limit_bytes=16 * MIB),
        cost_estimate=pl.CostEstimate(
            flops=80 * field.size, bytes_accessed=8 * field.size, transcendentals=0
        ),
    )(me, geo, last, partial, field)
    return [outs[k::chunks] for k in range(chunks)], terms


def near_modes(me, geo, last, partial, terms, fold, count, planes):
    slot = jax.ShapeDtypeStruct((fold.slots, planes, LANES), jnp.float32)
    return pl.pallas_call(
        functools.partial(near_modes_kernel, fold),
        in_specs=[smem()] + vmem(4),
        out_specs=vmem(count),
        out_shape=[slot] * count,
        scratch_shapes=[pltpu.VMEM((count * planes, 2 * LANES), jnp.float32)],
        compiler_params=pltpu.CompilerParams(vmem_limit_bytes=16 * MIB),
        cost_estimate=pl.CostEstimate(
            flops=80 * slot.size, bytes_accessed=8 * slot.size, transcendentals=0
        ),
    )(me, geo, last, partial, terms)


def edge_send(mask_ref, edge, write):
    for t in range(8):
        total = None
        for a in range(4):
            term = edge(a, t) * mask_ref[a : a + 1, :]
            total = term if total is None else total + term
        write(t, total)


def send_from(field_ref, mask_ref, out_ref, start):
    modes, elems = field_ref.shape[1:]
    lane = lane_of((modes, LANES))

    def edge(a, t):
        node = EDGE_NODES[a][t]
        ends = field_ref[node, :, :LANES], field_ref[node, :, elems - LANES :]
        return jnp.where(lane < ROWS, ends[0], ends[1])

    def write(t, value):
        out_ref[t, start : start + modes, :] = value

    edge_send(mask_ref, edge, write)


def unpack_kernel(fold, groups, start, me_ref, mask_ref, *refs):
    parts, (r0_ref, send_ref) = refs[:groups], refs[-2:]
    modes = r0_ref.shape[1]
    me = me_ref[0]

    def tile(part, _):
        rows = pl.ds(pl.multiple_of(part * 8, 8), 8)
        whole_rows = pl.ds(pl.multiple_of(part * 8 + start, 8), 8)

        def load(ref, slot):
            return ref[slot, rows if ref.shape[1] == modes else whole_rows, :]

        lane = lane_of((8, LANES))
        for k in range(groups // fold.parts):
            block = k ^ (me // fold.parts)
            lanes = pl.ds(pl.multiple_of(block * LANES, LANES), LANES)
            mine = parts[k * fold.parts : (k + 1) * fold.parts]
            for jp in range(fold.count_j):
                for ip in range(fold.count_i):
                    loads = swapped(me, [load(ref, fold.slot(jp, ip)) for ref in mine])
                    for q in range(fold.parts):
                        shifts = [
                            rolled(loads[r], (r - q) * fold.width) for r in range(fold.parts)
                        ]
                        value = by_part(shifts, lane, fold.width)
                        r0_ref[fold.node(jp, ip, q), rows, lanes] = value
        return 0

    lax.fori_loop(0, modes // 8, tile, 0)
    if start:
        send_ref[:, :start, :] = refs[groups][...]
    send_from(r0_ref, mask_ref, send_ref, start)


def unpack(me, mask, parts, fold, sends):
    _, modes, _ = parts[-1].shape
    groups = len(parts)
    elems = groups * fold.width
    start = sum(value.shape[1] for value in sends)
    return pl.pallas_call(
        functools.partial(unpack_kernel, fold, groups, start),
        in_specs=[smem()] + vmem(1 + groups + len(sends)),
        out_specs=vmem(2),
        out_shape=[
            jax.ShapeDtypeStruct((64, modes, elems), jnp.float32),
            jax.ShapeDtypeStruct((8, start + modes, LANES), jnp.float32),
        ],
        compiler_params=pltpu.CompilerParams(vmem_limit_bytes=4 * MIB),
        cost_estimate=small_cost(),
    )(me, mask, *parts, *sends)


def volume(
    field_ref, geo_ref, mass_ref, first, image_ref, sums_ref, row_of_sums, acc_ref, start=0, step=1
):
    modes, elems = field_ref.shape[1:]
    tiles = modes // 8

    def tile(number, _):
        row = pl.multiple_of(number % tiles * 8, 8)
        rows = pl.ds(row, 8)
        sum_rows = pl.ds(row + row_of_sums, 8)
        block = number // tiles * step + start
        lanes = pl.ds(pl.multiple_of(block * LANES, LANES), LANES)
        jac = geo_ref[0:1, lanes] * mass_ref[pl.ds(row + first, 8), :]
        square_x = jnp.broadcast_to(geo_ref[0:1, lanes] * geo_ref[1:2, lanes], (8, LANES))
        square_y = jnp.broadcast_to(geo_ref[0:1, lanes] * geo_ref[2:3, lanes], (8, LANES))
        stiff = plane_stiffness * STIFF
        for j in range(8):
            values = [field_ref[8 * j + i, rows, lanes] for i in range(8)]
            result = line_apply(stiff, values, 1)
            scale = square_x * np.float32(WEIGHTS[j])
            mass = jac * np.float32(WEIGHTS[j])
            for i in range(8):
                acc_ref[8 * j + i] = result[i] * scale + (mass * np.float32(WEIGHTS[i])) * values[i]
        totals = [None, None]
        for i in range(8):
            values = [field_ref[8 * j + i, rows, lanes] for j in range(8)]
            result = line_apply(stiff, values, 1)
            scale = square_y * np.float32(WEIGHTS[i])
            for j in range(8):
                image = acc_ref[8 * j + i] + result[j] * scale
                if image_ref is not None:
                    image_ref[8 * j + i, rows, lanes] = image
                for k, term in enumerate((values[j] * values[j], values[j] * image)):
                    totals[k] = term if totals[k] is None else totals[k] + term
        for k in range(2):
            sums_ref[k, sum_rows, :] += totals[k]
        return 0

    blocks = -(-(elems // LANES - start) // step)
    lax.fori_loop(0, tiles * blocks, tile, 0)


def inner_kernel(field_ref, geo_ref, mass_ref, sums_ref, acc_ref):
    sums_ref[...] = jnp.zeros_like(sums_ref)
    blocks = field_ref.shape[2] // LANES
    for block in range(1, blocks - 1):
        volume(field_ref, geo_ref, mass_ref, 0, None, sums_ref, 0, acc_ref, block, blocks)


def inner_sums(field, geo, mass):
    _, modes, _ = field.shape
    return pl.pallas_call(
        inner_kernel,
        in_specs=vmem(3),
        out_specs=vmem(1)[0],
        out_shape=jax.ShapeDtypeStruct((2, modes, LANES), jnp.float32),
        scratch_shapes=[pltpu.VMEM((64, 8, LANES), jnp.float32)],
        compiler_params=pltpu.CompilerParams(vmem_limit_bytes=4 * MIB),
        cost_estimate=small_cost(),
    )(field, geo, mass)


def fill_pairs(target_ref, first, modes, lanes, value_of, parts):
    total = target_ref.shape[0] // (8 * parts)
    for t in range(0, 8, 2):
        pieces = split(jnp.concatenate([value_of(t), value_of(t + 1)], axis=0))
        for part in range(parts):
            row = (8 * part + t) * total
            target_ref[pl.ds(row, 2 * total), lanes] = pieces[part]


def gathered(trace, table, parts):
    value = jnp.dot(trace, table, preferred_element_type=jnp.float32)
    if parts == 2:
        half = value.shape[0] // 2
        value = value[:half] + value[half:]
    return value.reshape(8, value.shape[0] // 8, value.shape[1])


def local_edges(fields, first, flag_ref, local_ref, edges_ref, trace_ref, val_ref, parts, visit):
    elems = val_ref.shape[2]
    for a in range(4):

        def value_of(t):
            pieces = [field_ref[EDGE_NODES[a][t]] for field_ref in fields]
            return pieces[0] if len(pieces) == 1 else jnp.concatenate(pieces, axis=0)

        fill_pairs(trace_ref, 0, 0, pl.ds(a * elems, elems), value_of, parts)
    for edge in range(4):
        mine = slice(edge * elems, (edge + 1) * elems)
        if parts == 2:
            val_ref[...] = gathered(trace_ref[...], local_ref[:, mine], parts)
        else:
            value = gathered(trace_ref[:, mine], local_ref[mine, mine], parts)
            if edge:
                left = slice(0, edge * elems)
                value = value + 2.0 * gathered(trace_ref[:, left], local_ref[left, mine], parts)
            val_ref[...] = value
        for block in range(elems // LANES):
            lanes = pl.ds(block * LANES, LANES)
            wall = edges_ref[8 * edge : 8 * edge + 1, lanes]
            flip = edges_ref[8 * edge + 1 : 8 * edge + 2, lanes]
            start = 0
            for chunk, field_ref in enumerate(fields):
                modes = field_ref.shape[1]
                rows = slice(start, start + modes)
                start += modes
                turned = jnp.broadcast_to(flip, (modes, LANES)) > 0.5
                coef = 1.0 - wall * (1.0 - flag_ref[first + start - modes : first + start])
                for t in range(8):
                    node = EDGE_NODES[edge][t]
                    value = field_ref[node, :, lanes]
                    other = jnp.where(turned, val_ref[7 - t, rows, lanes], val_ref[t, rows, lanes])
                    weight = np.float32(edge_penalty * WEIGHTS[t])
                    visit(chunk, rows, node, lanes, value, weight * (coef * value - other))


def far_edges(after_ref, before_ref, far_ref, edges_ref, trace_ref, elems, visit):
    modes = after_ref.shape[1]
    lane = lane_of((modes, LANES))

    def value_of(t):
        return jnp.where(lane < ROWS, after_ref[t], before_ref[t])

    fill_pairs(trace_ref, 0, modes, pl.ds(0, LANES), value_of, 2)
    for edge in range(4):
        values = gathered(trace_ref[...], far_ref[:, edge * LANES : (edge + 1) * LANES], 2)
        flips = edges_ref[8 * edge + 1 : 8 * edge + 2, :]
        flip = jnp.where(lane < ROWS, flips[:, :LANES], flips[:, elems - LANES :])
        for t in range(8):
            other = jnp.where(flip > 0.5, values[7 - t], values[t])
            visit(edge, t, other * np.float32(-edge_penalty * WEIGHTS[t]))


def apply_kernel(want_image, count, first, given, *refs):
    fields, refs = refs[:count], refs[count:]
    inner, refs = refs[:given], refs[given:]
    geo_ref, mass_ref, flag_ref, local_ref, edges_ref = refs[:5]
    refs = refs[5:]
    image_ref = refs[0] if want_image else None
    sums_ref, trace_ref, val_ref, acc_ref = refs[-4:]
    sums_ref[...] = jnp.zeros_like(sums_ref)
    start = 0
    for field_ref in fields:
        row = first + start
        step = 1
        if inner and start == 0:
            sums_ref[:, : field_ref.shape[1], :] = inner[0][...]
            step = field_ref.shape[2] // LANES - 1
        volume(field_ref, geo_ref, mass_ref, row, image_ref, sums_ref, start, acc_ref, 0, step)
        start += field_ref.shape[1]
    totals = [None] * count

    def visit(chunk, rows, node, lanes, value, term):
        if want_image:
            image_ref[node, :, lanes] += term
        product = value * term
        totals[chunk] = product if totals[chunk] is None else totals[chunk] + product

    parts = 2 if want_image else 1
    local_edges(
        fields, first, flag_ref, local_ref, edges_ref, trace_ref, val_ref, parts, visit
    )
    start = 0
    for chunk, field_ref in enumerate(fields):
        rows = slice(start, start + field_ref.shape[1])
        start = rows.stop
        sums_ref[1, rows, :] += totals[chunk]


def apply_local(fields, first, geo, mass, flag, local, edges, want_image, inner=()):
    elems = fields[0].shape[2]
    modes = sum(field.shape[1] for field in fields)
    sums = jax.ShapeDtypeStruct((2, modes, LANES), jnp.float32)
    shapes = [jax.ShapeDtypeStruct(fields[0].shape, jnp.float32), sums] if want_image else [sums]
    parts = 2 if want_image else 1
    return pl.pallas_call(
        functools.partial(apply_kernel, want_image, len(fields), first, len(inner)),
        in_specs=vmem(5 + len(fields) + len(inner)),
        out_specs=vmem(len(shapes)),
        out_shape=shapes,
        scratch_shapes=[
            pltpu.VMEM((parts * 8 * modes, 4 * elems), jnp.bfloat16),
            pltpu.VMEM((8, modes, elems), jnp.float32),
            pltpu.VMEM((64, 8, LANES), jnp.float32),
        ],
        compiler_params=pltpu.CompilerParams(vmem_limit_bytes=16 * MIB),
        cost_estimate=small_cost(),
    )(*fields, *inner, geo, mass, flag, local, edges)


def ends_of(node, field_refs, lane):
    elems = field_refs[0].shape[2]
    pieces = []
    for ref in field_refs:
        pieces.append((ref[node, :, :LANES], ref[node, :, elems - LANES :]))
    first = [p[0] for p in pieces]
    last = [p[1] for p in pieces]
    if len(pieces) > 1:
        first, last = [jnp.concatenate(first, axis=0)], [jnp.concatenate(last, axis=0)]
    return jnp.where(lane < ROWS, first[0], last[0])


def first_far_kernel(count, *refs):
    images, fields, refs = refs[:count], refs[count : 2 * count], refs[2 * count :]
    sum_refs, refs = refs[:count], refs[count:]
    after_ref, before_ref, far_ref, edges_ref, mask_ref = refs[:5]
    outs, (send_ref, out_ref, trace_ref) = refs[5 : 5 + count], refs[5 + count :]
    modes = after_ref.shape[1]
    elems = fields[0].shape[2]
    lane = lane_of((modes, LANES))
    sums = [[ref[k] for ref in sum_refs] for k in range(2)]
    sums = [jnp.concatenate(pieces, axis=0) if count > 1 else pieces[0] for pieces in sums]
    totals = [sums[1]]
    done = set()

    def visit(edge, t, term):
        node = EDGE_NODES[edge][t]
        totals[0] = totals[0] + ends_of(node, fields, lane) * term
        start = 0
        for image_ref, ref in zip(images, outs):
            size = ref.shape[1]
            part = term[start : start + size]
            here = lane_of((size, LANES)) < ROWS
            start += size
            source = ref if node in done else image_ref
            ref[node, :, :LANES] = source[node, :, :LANES] + jnp.where(here, part, 0.0)
            ref[node, :, elems - LANES :] = source[node, :, elems - LANES :] + jnp.where(
                here, 0.0, part
            )
        done.add(node)

    far_edges(after_ref, before_ref, far_ref, edges_ref, trace_ref, elems, visit)
    out_ref[0] = sums[0]
    out_ref[1] = totals[0]
    start = 0
    for ref in outs:
        send_from(ref, mask_ref, send_ref, start)
        start += ref.shape[1]


def first_far(images, fields, halo, far, edges, mask, sums):
    count = len(fields)
    modes = sum(value.shape[1] for value in sums)
    return pl.pallas_call(
        functools.partial(first_far_kernel, count),
        in_specs=vmem(3 * count + 5),
        out_specs=vmem(count + 2),
        out_shape=[jax.ShapeDtypeStruct(image.shape, jnp.float32) for image in images]
        + [
            jax.ShapeDtypeStruct((8, modes, LANES), jnp.float32),
            jax.ShapeDtypeStruct((2, modes, LANES), jnp.float32),
        ],
        scratch_shapes=[pltpu.VMEM((16 * modes, LANES), jnp.bfloat16)],
        input_output_aliases={k: k for k in range(count)},
        compiler_params=pltpu.CompilerParams(vmem_limit_bytes=8 * MIB),
        cost_estimate=small_cost(),
    )(*images, *fields, *sums, *halo, far, edges, mask)


def second_far_kernel(count, *refs):
    fields, refs = refs[:count], refs[count:]
    after_ref, before_ref, far_ref, edges_ref, first_ref, more_ref, out_ref, trace_ref = refs
    modes = after_ref.shape[1]
    elems = fields[0].shape[2]
    lane = lane_of((modes, LANES))
    totals = [more_ref[1]]

    def visit(edge, t, term):
        totals[0] = totals[0] + ends_of(EDGE_NODES[edge][t], fields, lane) * term

    far_edges(after_ref, before_ref, far_ref, edges_ref, trace_ref, elems, visit)
    sums = [first_ref[0], first_ref[1], more_ref[0], totals[0]]
    packed = jnp.zeros((modes, LANES), jnp.float32)
    for k, value in enumerate(sums):
        packed = jnp.where(lane == k, jnp.sum(value, axis=1, keepdims=True), packed)
    out_ref[...] = packed


def second_far(fields, halo, far, edges, first, more):
    modes = first.shape[1]
    return pl.pallas_call(
        functools.partial(second_far_kernel, len(fields)),
        in_specs=vmem(6 + len(fields)),
        out_specs=vmem(1)[0],
        out_shape=jax.ShapeDtypeStruct((modes, LANES), jnp.float32),
        scratch_shapes=[pltpu.VMEM((16 * modes, LANES), jnp.bfloat16)],
        compiler_params=pltpu.CompilerParams(vmem_limit_bytes=8 * MIB),
        cost_estimate=small_cost(),
    )(*fields, *halo, far, edges, first, more)


def finish_kernel(count, chunks, *refs):
    fields, refs = refs[: 2 * chunks], refs[2 * chunks :]
    sum_refs, (out_ref, buffer_ref, sems) = refs[:count], refs[count:]
    total = sum_refs[0][...]
    for ref in sum_refs[1:]:
        total = total + ref[...]
    m0, m1, m2, m3 = [total[:, k : k + 1] for k in range(4)]
    alpha = m0 / m1
    norm = alpha * (alpha * m2) - 2.0 * (alpha * m1) + m0
    energy = m1 - 2.0 * (alpha * m2) + alpha * (alpha * m3)
    beta = norm / m0
    second = norm / (energy - beta * (norm / alpha))
    on_r = jnp.broadcast_to(alpha + second * (1.0 + beta), total.shape)
    on_q = jnp.broadcast_to(second * alpha, total.shape)
    elems = out_ref.shape[2]
    slots = buffer_ref.shape[0]
    tiles = total.shape[0] // 8

    def copy(tile):
        target = out_ref.at[pl.ds(8 * tile, 8)]
        return pltpu.make_async_copy(buffer_ref.at[tile % slots], target, sems.at[tile % slots])

    tile = 0
    for chunk in range(chunks):
        r0_ref, q0_ref = fields[2 * chunk : 2 * chunk + 2]
        for first in range(0, r0_ref.shape[1], 8):
            if tile >= slots:
                copy(tile - slots).wait()
            mine = slice(8 * tile, 8 * tile + 8)
            rows = slice(first, first + 8)
            on_r0, on_q0 = on_r[mine], on_q[mine]
            for block in range(elems // LANES):
                lanes = slice(block * LANES, (block + 1) * LANES)
                for j in range(8):
                    nodes = slice(8 * j, 8 * j + 8)
                    value = on_r0 * r0_ref[nodes, rows, lanes] - on_q0 * q0_ref[nodes, rows, lanes]
                    buffer_ref[tile % slots, :, nodes, lanes] = jnp.swapaxes(value, 0, 1)
            copy(tile).start()
            tile += 1
    for left in range(max(tiles - slots, 0), tiles):
        copy(left).wait()


def finish(fields, sums):
    elems = fields[0].shape[2]
    total = sums[0].shape[0]
    slots = min(4, total // 8)
    return pl.pallas_call(
        functools.partial(finish_kernel, len(sums), len(fields) // 2),
        in_specs=vmem(len(fields) + len(sums)),
        out_specs=pl.BlockSpec(memory_space=pl.ANY),
        out_shape=jax.ShapeDtypeStruct((total, 64, elems), jnp.float32),
        scratch_shapes=[
            pltpu.VMEM((slots, 8, 64, elems), jnp.float32),
            pltpu.SemaphoreType.DMA((slots,)),
        ],
        compiler_params=pltpu.CompilerParams(vmem_limit_bytes=16 * MIB),
    )(*fields, *sums)


def shifted(value, axis, steps):
    size = lax.axis_size(axis)
    return lax.ppermute(value, axis, [(i, (i + steps) % size) for i in range(size)])


def exchanged(slots, first=0):
    size = lax.axis_size("gz")
    out = []
    for number, value in enumerate(slots):
        d = first + number
        out.append(lax.ppermute(value, "gz", [(i, i ^ d) for i in range(size)]) if d else value)
    return out


def both_sides(send):
    return [shifted(send, "xy", -1), shifted(send, "xy", 1)]


def pad_rows(values, rows=8):
    return jnp.pad(values, ((0, rows - values.shape[0]), (0, 0)))


def edge_tables(nbr_elem, nbr_edge):
    elems = nbr_elem.shape[1]
    me, size = lax.axis_index("xy"), lax.axis_size("xy")
    wall = nbr_elem < 0
    ids = jnp.maximum(nbr_elem, 0)
    owner, local_id = ids // elems, ids % elems
    here = (owner == me) & ~wall
    after = (owner == (me + 1) % size) & ~wall & ~here
    before = ~wall & ~here & ~after
    place = jnp.where(here, nbr_edge % 4 * elems + local_id, -1).reshape(-1)
    source = jnp.arange(4 * elems, dtype=jnp.int32)[:, None]
    local = (source == place[None, :]).astype(jnp.bfloat16)
    first = jnp.arange(LANES) < ROWS

    def ends(table):
        return jnp.where(first[None, :], table[:, :LANES], table[:, elems - LANES :])

    send = jnp.where(first[None, :], before[:, :LANES], after[:, elems - LANES :])
    slot = jnp.where(after, local_id, local_id - (elems - ROWS) + ROWS)
    slot = jnp.where(send, ends(slot), -1).reshape(-1)
    far = (jnp.arange(LANES, dtype=jnp.int32)[:, None] == slot[None, :]).astype(jnp.bfloat16)
    flags = jnp.stack([wall, nbr_edge >= 4], axis=1).astype(jnp.float32)
    flags = jnp.pad(flags, ((0, 0), (0, 6), (0, 0))).reshape(32, elems)
    return local, far, pad_rows(send.astype(jnp.float32)), flags


def per_device(concentration, geometry, nbr_elem, nbr_edge, wall_flags):
    planes, _, elems = concentration.shape
    groups = lax.axis_size("gz")
    me = lax.axis_index("gz")
    fold = Fold(elems // groups)
    scale_x, scale_y = geometry[0], geometry[1]
    geo = pad_rows(jnp.stack([1.0 / (scale_x * scale_y), scale_x * scale_x, scale_y * scale_y]))
    mine = lax.dynamic_slice_in_dim(geo, me * fold.width, fold.width, axis=1)
    mine = jnp.tile(mine, (1, fold.parts))
    index = me.astype(jnp.int32).reshape(1)
    mode_ids = me * planes + jnp.arange(planes, dtype=jnp.int32)
    wave = ((mode_ids + 1) // 2).astype(jnp.float32)
    mass = jnp.broadcast_to(
        (1.0 / time_step + axial_stiffness * wave * wave)[:, None], (planes, LANES)
    )
    flag = jnp.broadcast_to(wall_flags.astype(jnp.float32)[:, None], (planes, LANES))
    tables = edge_tables(nbr_elem, nbr_edge)
    half = groups // 2
    far_sent = list(pack(index, concentration, fold, groups, half, fold.parts))
    more = half - fold.parts
    far_sent += pack(index, concentration, fold, groups, half + fold.parts, more) if more else []
    near_sent = pack(index, concentration, fold, groups, 0, half)
    near_field = exchanged(near_sent)
    near_field[2], far_sent[-1] = lax.optimization_barrier((near_field[2], far_sent[-1]))
    far_field = exchanged(far_sent, half)
    halves, pieces = transform_tables(planes * groups, planes)
    last = lax.dynamic_index_in_dim(pieces, me ^ (groups - 1), 0, keepdims=False)
    near_field, geo, mine, mass, flag, tables, last = lax.optimization_barrier(
        (near_field, geo, mine, mass, flag, tables, last)
    )
    local, far, mask, edges = tables
    near = some_terms(index, mine, near_field, fold, 0, half)
    far_terms = some_terms(index, mine, far_field[:-1], fold, half, half, clear=True)
    sizes = [planes - 8, 8] if planes > 16 else [planes]
    partial = partial_modes(index, halves, near, far_terms, half, planes, 1)
    sent, terms = far_modes(index, mine, last, partial, far_field[-1], fold, half, sizes)
    far_parts = [exchanged(piece, half) for piece in sent]
    partial = partial_modes(index, halves, near, far_terms, half, planes, 0)
    near_parts = exchanged(near_modes(index, mine, last, partial, terms, fold, half, planes))
    fields, images, sums, sends, inner = [], [], [], [], []
    start = 0
    for piece, size in enumerate(sizes):
        parts = near_parts + far_parts[piece]
        field, send = unpack(index, mask, parts, fold, sends)
        sends = [send]
        image, more = apply_local([field], start, geo, mass, flag, local, edges, True)
        start += size
        if piece + 1 < len(sizes):
            inner = [inner_sums(image, geo, mass)]
            mask, inner = lax.optimization_barrier((mask, inner))
        fields.append(field)
        images.append(image)
        sums.append(more)
    halo = both_sides(sends[0])
    *images, send, sums = first_far(images, fields, halo, far, edges, mask, sums)
    (more,) = apply_local(images, 0, geo, mass, flag, local, edges, False, inner)
    packed = second_far(images, both_sides(send), far, edges, sums, more)
    size = lax.axis_size("xy")
    pairs = [value for pair in zip(fields, images) for value in pair]
    return finish(pairs, [packed] + [shifted(packed, "xy", k) for k in range(1, size)])


def solution(mesh):
    return jax.shard_map(
        per_device,
        mesh=mesh,
        in_specs=(P("gz", None, "xy"), P(None, "xy"), P(None, "xy"), P(None, "xy"), P("gz")),
        out_specs=P("gz", None, "xy"),
        check_vma=False,
    )
```

```python
import functools

import jax
import jax.numpy as jnp
import ml_dtypes
import numpy as np
from jax import lax
from jax.experimental import pallas as pl
from jax.experimental.pallas import tpu as pltpu
from jax.sharding import PartitionSpec as P

ROWS = 64
LANES = 128
MIB = 1024 * 1024

time_step = 0.2
axial_stiffness = 0.002
plane_stiffness = 1.0
edge_penalty = 4.0
axial_mobility = 0.002
mobility_floor = 0.05


def point_tables():
    degree = 7
    points = np.arange(degree + 1)
    theta = np.pi * points / degree
    nodes_x = np.cos(theta)
    signs = np.where((points == 0) | (points == degree), 2.0, 1.0) * (-1.0) ** points
    differ = nodes_x[:, None] - nodes_x[None, :]
    deriv = np.outer(signs, 1.0 / signs) / (differ + np.eye(degree + 1))
    deriv = deriv - np.eye(degree + 1) * deriv.sum(axis=1)[:, None]
    inner = np.ones(degree - 1)
    for number in range(1, (degree - 1) // 2 + 1):
        inner = inner - 2.0 * np.cos(2 * number * theta[1:degree]) / (4 * number * number - 1)
    weights = np.zeros(degree + 1)
    weights[1:degree] = 2.0 * inner / degree
    weights[0] = 1.0 / degree**2
    weights[degree] = 1.0 / degree**2
    return (deriv, weights)


def fourier_table(length):
    planes = np.arange(length)
    wave_no = (planes + 1) // 2
    phase = np.outer(wave_no, planes) % length * (2.0 * np.pi / length)
    table = np.where((planes % 2 == 1)[:, None], np.cos(phase), np.sin(phase)) * np.sqrt(
        2.0 / length
    )
    table[0] = 1.0 / np.sqrt(length)
    table[length - 1] = np.cos(phase[length - 1]) / np.sqrt(length)
    return table


DERIV, WEIGHTS = point_tables()
BACK = DERIV.T * WEIGHTS[None, :]
STIFF = BACK @ DERIV
BACK_SCALED = BACK / WEIGHTS[:, None]


def two_parts(table):
    upper = table.astype(np.float32).astype(ml_dtypes.bfloat16)
    lower = (table - upper.astype(np.float64)).astype(np.float32).astype(ml_dtypes.bfloat16)
    return upper, lower


def split(value):
    upper = value.astype(jnp.bfloat16)
    lower = (value - upper.astype(jnp.float32)).astype(jnp.bfloat16)
    return upper, lower


class Fold:
    def __init__(self, width):
        self.width = width
        self.parts = LANES // width
        self.fold_j = 2 if self.parts >= 2 else 1
        self.fold_i = 2 if self.parts >= 4 else 1
        self.count_j = 8 // self.fold_j
        self.count_i = 8 // self.fold_i
        self.slots = self.count_j * self.count_i

    def slot(self, jp, ip):
        return jp * self.count_i + ip

    def node(self, jp, ip, part):
        half_j, half_i = part // self.fold_i, part % self.fold_i
        j = 7 - jp if half_j else jp
        i = 7 - ip if half_i else ip
        return 8 * j + i

    def place(self, node):
        j, i = node // 8, node % 8
        half_j = 1 if j >= self.count_j else 0
        half_i = 1 if i >= self.count_i else 0
        jp = 7 - j if half_j else j
        ip = 7 - i if half_i else i
        return self.slot(jp, ip), half_j * self.fold_i + half_i


def lane_of(shape):
    return lax.broadcasted_iota(jnp.int32, shape, len(shape) - 1)


def rolled(value, lanes):
    lanes = lanes % LANES
    return value if lanes == 0 else pltpu.roll(value, lanes, value.ndim - 1)


def by_part(values, lane, width):
    out = values[0]
    for r in range(1, len(values)):
        out = jnp.where(lane >= r * width, values[r], out)
    return out


def mirrored(value, lane, shift):
    if 2 * shift == LANES:
        return rolled(value, shift)
    return jnp.where((lane & shift) == 0, rolled(value, -shift), rolled(value, shift))


def combine(coefs, values):
    total = None
    for c, v in zip(coefs, values):
        term = v * np.float32(c)
        total = term if total is None else total + term
    return total


def line_apply(matrix, values, sign):
    even = [values[k] + values[7 - k] for k in range(4)]
    odd = [values[k] - values[7 - k] for k in range(4)]
    out = [None] * 8
    for a in range(4):
        from_even = combine([(matrix[a, b] + matrix[a, 7 - b]) / 2 for b in range(4)], even)
        from_odd = combine([(matrix[a, b] - matrix[a, 7 - b]) / 2 for b in range(4)], odd)
        out[a] = from_even + from_odd
        out[7 - a] = from_even - from_odd if sign > 0 else from_odd - from_even
    return out


def derivative_line(matrix, values, mirror):
    if mirror is None:
        return line_apply(matrix, values, -1)
    swap, sign, first = mirror
    mixed = [swap(v) + v * sign for v in values]
    out = []
    for a in range(4):
        total = None
        for b in range(4):
            upper = np.float32((matrix[a, b] + matrix[a, 7 - b]) / 2)
            lower = np.float32((matrix[a, b] - matrix[a, 7 - b]) / 2)
            term = mixed[b] * jnp.where(first, upper, lower)
            total = term if total is None else total + term
        out.append(total + swap(total) * sign)
    return out


EDGE_NODES = [
    [t for t in range(8)],
    [8 * t + 7 for t in range(8)],
    [56 + t for t in range(8)],
    [8 * t for t in range(8)],
]


def swapped(me, values):
    bit = 1
    while bit < len(values):
        flip = (me & bit) != 0
        values = [jnp.where(flip, values[r ^ bit], values[r]) for r in range(len(values))]
        bit *= 2
    return values


def pack_kernel(fold, me_ref, c_ref, *out_refs):
    lane = lane_of((c_ref.shape[0], LANES))
    me = me_ref[0]
    for step in range(len(out_refs) // fold.parts):

        @pl.when(pl.program_id(0) == step)
        def _():
            by_node = jnp.swapaxes(c_ref[...], 0, 1)
            for jp in range(fold.count_j):
                for ip in range(fold.count_i):
                    loads = [by_node[fold.node(jp, ip, q)] for q in range(fold.parts)]
                    made = []
                    for r in range(fold.parts):
                        parts = [rolled(loads[q], (q - r) * fold.width) for q in range(fold.parts)]
                        made.append(by_part(parts, lane, fold.width))
                    for p, value in enumerate(swapped(me, made)):
                        out_refs[step * fold.parts + p][fold.slot(jp, ip)] = value


def pack(me, conc, fold, groups, first, count):
    planes, nodes, elems = conc.shape
    offset = first // fold.parts

    def block(step, me_ref):
        return (0, 0, (step + offset) ^ (me_ref[0] // fold.parts))

    slot = jax.ShapeDtypeStruct((fold.slots, planes, LANES), jnp.float32)
    return pl.pallas_call(
        functools.partial(pack_kernel, fold),
        grid_spec=pltpu.PrefetchScalarGridSpec(
            num_scalar_prefetch=1,
            grid=(count // fold.parts,),
            in_specs=[pl.BlockSpec((planes, nodes, LANES), block)],
            out_specs=[pl.BlockSpec(slot.shape, lambda s, me_ref: (0, 0, 0))] * count,
        ),
        out_shape=[slot] * count,
        compiler_params=pltpu.CompilerParams(vmem_limit_bytes=60 * MIB),
        cost_estimate=pl.CostEstimate(
            flops=conc.size, bytes_accessed=4 * conc.size, transcendentals=0
        ),
    )(me, conc)


def plane_terms(fold, y_ref, geo_ref, x_ref, acc_ref, row, base, half):
    lane = lane_of((16, LANES))
    square_x = jnp.broadcast_to(geo_ref[1:2, :], (16, LANES))
    square_y = jnp.broadcast_to(geo_ref[2:3, :], (16, LANES))

    def mirror(shift):
        first = (lane & shift) == 0
        return (lambda v: mirrored(v, lane, shift), jnp.where(first, 1.0, -1.0), first)

    mirror_i = mirror(fold.width) if fold.fold_i == 2 else None
    mirror_j = mirror(fold.width * fold.fold_i) if fold.fold_j == 2 else None
    for jp in range(fold.count_j):
        chem, mobility = [], []
        for ip in range(fold.count_i):
            slot = fold.slot(jp, ip)
            c = y_ref[slot, pl.ds(base, 16), :]
            square = c * c
            chem.append(square * c - c)
            mobility.append(jnp.maximum(1.0 - square, mobility_floor))
            acc_ref[0, slot] = c * np.float32(1.0 / time_step)
            acc_ref[1, slot] = chem[ip]
            acc_ref[2, slot] = mobility[ip]
        slope = derivative_line(DERIV, chem, mirror_i)
        result = derivative_line(BACK_SCALED, [s * m for s, m in zip(slope, mobility)], mirror_i)
        for ip in range(fold.count_i):
            acc_ref[0, fold.slot(jp, ip)] -= result[ip] * square_x
    for ip in range(fold.count_i):
        slots = [fold.slot(jp, ip) for jp in range(fold.count_j)]
        chem = [acc_ref[1, slot] for slot in slots]
        slope = derivative_line(DERIV, chem, mirror_j)
        scaled = [s * acc_ref[2, slot] for s, slot in zip(slope, slots)]
        result = derivative_line(BACK_SCALED, scaled, mirror_j)
        for jp, slot in enumerate(slots):
            explicit = acc_ref[0, slot] - result[jp] * square_y
            where = pl.ds((slot % 2) * LANES, LANES)
            for kind, value in enumerate((explicit, chem[jp])):
                upper, lower = split(value)
                x_ref[slot // 2, pl.ds(kind * half + row, 16), where] = upper
                x_ref[slot // 2, pl.ds((2 + kind) * half + row, 16), where] = lower


def slot_terms(fold, me, first, count, y_refs, geo_ref, x_ref, acc_ref):
    planes = y_refs[0].shape[1]
    half = count * planes
    for number, y_ref in enumerate(y_refs):
        place = (me ^ (first + number)) % count

        def chunk(part, _, y_ref=y_ref, place=place):
            base = pl.multiple_of(part * 16, 16)
            row = pl.multiple_of(place * planes + base, 16)
            plane_terms(fold, y_ref, geo_ref, x_ref, acc_ref, row, base, half)
            return 0

        lax.fori_loop(0, planes // 16, chunk, 0)


def terms_kernel(fold, first, count, clear, me_ref, geo_ref, *refs):
    y_refs, (x_ref, acc_ref) = refs[:-2], refs[-2:]
    me = me_ref[0]
    if clear:
        planes = y_refs[0].shape[1]
        place = (me ^ (2 * count - 1)) % count
        for kind in range(4):
            row = pl.multiple_of((kind * count + place) * planes, 16)
            x_ref[:, pl.ds(row, planes), :] = jnp.zeros(
                (x_ref.shape[0], planes, 2 * LANES), jnp.bfloat16
            )
    slot_terms(fold, me, first, count, y_refs, geo_ref, x_ref, acc_ref)


def product(table, data):
    split_at = data.shape[0]
    return jnp.dot(table[:, :split_at], data, preferred_element_type=jnp.float32) + jnp.dot(
        table[:, split_at:], data[: split_at // 2], preferred_element_type=jnp.float32
    )


def rows_of(me, count, planes, other):
    half = count * planes
    return pl.ds(pl.multiple_of((me // count ^ other) * half, 16), half)


def partial_kernel(count, planes, other, me_ref, table_ref, near_ref, far_ref, out_ref):
    mine = me_ref[0] // count
    rows = rows_of(me_ref[0], count, planes, other)
    for pair in range(near_ref.shape[0]):
        out_ref[pair] = product(table_ref[mine, rows, :], near_ref[pair]) + product(
            table_ref[1 - mine, rows, :], far_ref[pair]
        )


def far_kernel(fold, count, sizes, me_ref, geo_ref, last_ref, partial_ref, y_ref, *refs):
    chunks = len(sizes)
    out_refs = [refs[k * chunks : (k + 1) * chunks] for k in range(count)]
    x_ref, acc_ref, result_ref = refs[count * chunks :]
    slot_terms(fold, me_ref[0], 0, 1, [y_ref], geo_ref, x_ref, acc_ref)
    transform(fold, 1, me_ref, geo_ref, last_ref, partial_ref, x_ref, out_refs, result_ref)


def near_modes_kernel(fold, me_ref, geo_ref, last_ref, partial_ref, x_ref, *refs):
    out_refs, result_ref = [[ref] for ref in refs[:-1]], refs[-1]
    transform(fold, 0, me_ref, geo_ref, last_ref, partial_ref, x_ref, out_refs, result_ref)


def transform(fold, other, me_ref, geo_ref, last_ref, partial_ref, x_ref, out_refs, result_ref):
    count = len(out_refs)
    planes = result_ref.shape[0] // count
    me = me_ref[0]
    jac = jnp.broadcast_to(geo_ref[0:1, :], (planes, LANES))
    table = last_ref[rows_of(me, count, planes, other), :]
    for pair in range(fold.slots // 2):
        result_ref[...] = partial_ref[pair] + product(table, x_ref[pair])
        for k in range(2):
            slot = 2 * pair + k
            jp, ip = slot // fold.count_i, slot % fold.count_i
            scale = jac * np.float32(WEIGHTS[jp] * WEIGHTS[ip])
            lanes = slice(k * LANES, (k + 1) * LANES)
            for number, pieces in enumerate(out_refs):
                start = (me ^ number) % count * planes
                for out_ref in pieces:
                    size = out_ref.shape[1]
                    here = pl.ds(pl.multiple_of(start, 8), size)
                    out_ref[slot] = result_ref[here, lanes] * scale[:size]
                    start = start + size


def small_cost():
    return pl.CostEstimate(flops=1, bytes_accessed=1, transcendentals=0)


def smem():
    return pl.BlockSpec(memory_space=pltpu.SMEM)


def vmem(count):
    return [pl.BlockSpec(memory_space=pltpu.VMEM)] * count


def some_terms(me, geo, fields, fold, first, count, clear=False):
    slots, planes, _ = fields[0].shape
    size = len(fields) * fields[0].size
    return pl.pallas_call(
        functools.partial(terms_kernel, fold, first, count, clear),
        in_specs=[smem()] + vmem(1 + len(fields)),
        out_specs=vmem(1)[0],
        out_shape=jax.ShapeDtypeStruct(
            (slots // 2, 4 * count * planes, 2 * LANES), jnp.bfloat16
        ),
        scratch_shapes=[pltpu.VMEM((3, slots, 16, LANES), jnp.float32)],
        compiler_params=pltpu.CompilerParams(vmem_limit_bytes=16 * MIB),
        cost_estimate=pl.CostEstimate(
            flops=80 * size, bytes_accessed=12 * size, transcendentals=0
        ),
    )(me, geo, *fields)


def transform_tables(total, planes):
    table = fourier_table(total).astype(np.float32).astype(np.float64)
    wave = ((np.arange(total) + 1) // 2).astype(np.float64)
    upper, lower = two_parts(table)
    upper_b, lower_b = two_parts(-axial_mobility * (wave * wave)[:, None] * table)
    kinds = np.stack([upper, upper_b, upper, upper_b, lower, lower_b])

    def cut(pieces):
        parts = np.split(kinds, pieces, axis=2)
        return jnp.asarray(np.stack([np.concatenate(list(part), axis=1) for part in parts]))

    return cut(2), cut(total // planes)


def partial_modes(me, tables, near, far, count, planes, other):
    half = count * planes
    shape = (near.shape[0], half, 2 * LANES)
    return pl.pallas_call(
        functools.partial(partial_kernel, count, planes, other),
        in_specs=[smem()] + vmem(3),
        out_specs=vmem(1)[0],
        out_shape=jax.ShapeDtypeStruct(shape, jnp.float32),
        compiler_params=pltpu.CompilerParams(vmem_limit_bytes=16 * MIB),
        cost_estimate=small_cost(),
    )(me, tables, near, far)


def far_modes(me, geo, last, partial, field, fold, count, sizes):
    slots, planes, _ = field.shape
    chunks = len(sizes)
    pieces = [jax.ShapeDtypeStruct((slots, k, LANES), jnp.float32) for k in sizes]
    *outs, terms = pl.pallas_call(
        functools.partial(far_kernel, fold, count, sizes),
        in_specs=[smem()] + vmem(4),
        out_specs=vmem(chunks * count + 1),
        out_shape=pieces * count
        + [jax.ShapeDtypeStruct((slots // 2, 4 * planes, 2 * LANES), jnp.bfloat16)],
        scratch_shapes=[
            pltpu.VMEM((3, slots, 16, LANES), jnp.float32),
            pltpu.VMEM((count * planes, 2 * LANES), jnp.float32),
        ],
        compiler_params=pltpu.CompilerParams(vmem_limit_bytes=16 * MIB),
        cost_estimate=pl.CostEstimate(
            flops=80 * field.size, bytes_accessed=8 * field.size, transcendentals=0
        ),
    )(me, geo, last, partial, field)
    return [outs[k::chunks] for k in range(chunks)], terms


def near_modes(me, geo, last, partial, terms, fold, count, planes):
    slot = jax.ShapeDtypeStruct((fold.slots, planes, LANES), jnp.float32)
    return pl.pallas_call(
        functools.partial(near_modes_kernel, fold),
        in_specs=[smem()] + vmem(4),
        out_specs=vmem(count),
        out_shape=[slot] * count,
        scratch_shapes=[pltpu.VMEM((count * planes, 2 * LANES), jnp.float32)],
        compiler_params=pltpu.CompilerParams(vmem_limit_bytes=16 * MIB),
        cost_estimate=pl.CostEstimate(
            flops=80 * slot.size, bytes_accessed=8 * slot.size, transcendentals=0
        ),
    )(me, geo, last, partial, terms)


def edge_send(mask_ref, edge, write):
    for t in range(8):
        total = None
        for a in range(4):
            term = edge(a, t) * mask_ref[a : a + 1, :]
            total = term if total is None else total + term
        write(t, total)


def send_from(field_ref, mask_ref, out_ref, start):
    modes, elems = field_ref.shape[1:]
    lane = lane_of((modes, LANES))

    def edge(a, t):
        node = EDGE_NODES[a][t]
        ends = field_ref[node, :, :LANES], field_ref[node, :, elems - LANES :]
        return jnp.where(lane < ROWS, ends[0], ends[1])

    def write(t, value):
        out_ref[t, start : start + modes, :] = value

    edge_send(mask_ref, edge, write)


def unpack_kernel(fold, groups, start, me_ref, mask_ref, *refs):
    parts, (r0_ref, send_ref) = refs[:groups], refs[-2:]
    modes = r0_ref.shape[1]
    me = me_ref[0]

    def tile(part, _):
        rows = pl.ds(pl.multiple_of(part * 8, 8), 8)
        whole_rows = pl.ds(pl.multiple_of(part * 8 + start, 8), 8)

        def load(ref, slot):
            return ref[slot, rows if ref.shape[1] == modes else whole_rows, :]

        lane = lane_of((8, LANES))
        for k in range(groups // fold.parts):
            block = k ^ (me // fold.parts)
            lanes = pl.ds(pl.multiple_of(block * LANES, LANES), LANES)
            mine = parts[k * fold.parts : (k + 1) * fold.parts]
            for jp in range(fold.count_j):
                for ip in range(fold.count_i):
                    loads = swapped(me, [load(ref, fold.slot(jp, ip)) for ref in mine])
                    for q in range(fold.parts):
                        shifts = [
                            rolled(loads[r], (r - q) * fold.width) for r in range(fold.parts)
                        ]
                        value = by_part(shifts, lane, fold.width)
                        r0_ref[fold.node(jp, ip, q), rows, lanes] = value
        return 0

    lax.fori_loop(0, modes // 8, tile, 0)
    if start:
        send_ref[:, :start, :] = refs[groups][...]
    send_from(r0_ref, mask_ref, send_ref, start)


def unpack(me, mask, parts, fold, sends):
    _, modes, _ = parts[-1].shape
    groups = len(parts)
    elems = groups * fold.width
    start = sum(value.shape[1] for value in sends)
    return pl.pallas_call(
        functools.partial(unpack_kernel, fold, groups, start),
        in_specs=[smem()] + vmem(1 + groups + len(sends)),
        out_specs=vmem(2),
        out_shape=[
            jax.ShapeDtypeStruct((64, modes, elems), jnp.float32),
            jax.ShapeDtypeStruct((8, start + modes, LANES), jnp.float32),
        ],
        compiler_params=pltpu.CompilerParams(vmem_limit_bytes=4 * MIB),
        cost_estimate=small_cost(),
    )(me, mask, *parts, *sends)


def volume(
    field_ref, geo_ref, mass_ref, first, image_ref, sums_ref, row_of_sums, acc_ref, start=0, step=1
):
    modes, elems = field_ref.shape[1:]
    tiles = modes // 8

    def tile(number, _):
        row = pl.multiple_of(number % tiles * 8, 8)
        rows = pl.ds(row, 8)
        sum_rows = pl.ds(row + row_of_sums, 8)
        block = number // tiles * step + start
        lanes = pl.ds(pl.multiple_of(block * LANES, LANES), LANES)
        jac = geo_ref[0:1, lanes] * mass_ref[pl.ds(row + first, 8), :]
        square_x = jnp.broadcast_to(geo_ref[0:1, lanes] * geo_ref[1:2, lanes], (8, LANES))
        square_y = jnp.broadcast_to(geo_ref[0:1, lanes] * geo_ref[2:3, lanes], (8, LANES))
        stiff = plane_stiffness * STIFF
        for j in range(8):
            values = [field_ref[8 * j + i, rows, lanes] for i in range(8)]
            result = line_apply(stiff, values, 1)
            scale = square_x * np.float32(WEIGHTS[j])
            mass = jac * np.float32(WEIGHTS[j])
            for i in range(8):
                acc_ref[8 * j + i] = result[i] * scale + (mass * np.float32(WEIGHTS[i])) * values[i]
        totals = [None, None]
        for i in range(8):
            values = [field_ref[8 * j + i, rows, lanes] for j in range(8)]
            result = line_apply(stiff, values, 1)
            scale = square_y * np.float32(WEIGHTS[i])
            for j in range(8):
                image = acc_ref[8 * j + i] + result[j] * scale
                if image_ref is not None:
                    image_ref[8 * j + i, rows, lanes] = image
                for k, term in enumerate((values[j] * values[j], values[j] * image)):
                    totals[k] = term if totals[k] is None else totals[k] + term
        for k in range(2):
            sums_ref[k, sum_rows, :] += totals[k]
        return 0

    blocks = -(-(elems // LANES - start) // step)
    lax.fori_loop(0, tiles * blocks, tile, 0)


def inner_kernel(field_ref, geo_ref, mass_ref, sums_ref, acc_ref):
    sums_ref[...] = jnp.zeros_like(sums_ref)
    blocks = field_ref.shape[2] // LANES
    for block in range(1, blocks - 1):
        volume(field_ref, geo_ref, mass_ref, 0, None, sums_ref, 0, acc_ref, block, blocks)


def inner_sums(field, geo, mass):
    _, modes, _ = field.shape
    return pl.pallas_call(
        inner_kernel,
        in_specs=vmem(3),
        out_specs=vmem(1)[0],
        out_shape=jax.ShapeDtypeStruct((2, modes, LANES), jnp.float32),
        scratch_shapes=[pltpu.VMEM((64, 8, LANES), jnp.float32)],
        compiler_params=pltpu.CompilerParams(vmem_limit_bytes=4 * MIB),
        cost_estimate=small_cost(),
    )(field, geo, mass)


def fill_pairs(target_ref, first, modes, lanes, value_of, parts):
    total = target_ref.shape[0] // (8 * parts)
    for t in range(0, 8, 2):
        pieces = split(jnp.concatenate([value_of(t), value_of(t + 1)], axis=0))
        for part in range(parts):
            row = (8 * part + t) * total
            target_ref[pl.ds(row, 2 * total), lanes] = pieces[part]


def gathered(trace, table, parts):
    value = jnp.dot(trace, table, preferred_element_type=jnp.float32)
    if parts == 2:
        half = value.shape[0] // 2
        value = value[:half] + value[half:]
    return value.reshape(8, value.shape[0] // 8, value.shape[1])


def local_edges(fields, first, flag_ref, local_ref, edges_ref, trace_ref, val_ref, parts, visit):
    elems = val_ref.shape[2]
    for a in range(4):

        def value_of(t):
            pieces = [field_ref[EDGE_NODES[a][t]] for field_ref in fields]
            return pieces[0] if len(pieces) == 1 else jnp.concatenate(pieces, axis=0)

        fill_pairs(trace_ref, 0, 0, pl.ds(a * elems, elems), value_of, parts)
    for edge in range(4):
        mine = slice(edge * elems, (edge + 1) * elems)
        if parts == 2:
            val_ref[...] = gathered(trace_ref[...], local_ref[:, mine], parts)
        else:
            value = gathered(trace_ref[:, mine], local_ref[mine, mine], parts)
            if edge:
                left = slice(0, edge * elems)
                value = value + 2.0 * gathered(trace_ref[:, left], local_ref[left, mine], parts)
            val_ref[...] = value
        for block in range(elems // LANES):
            lanes = pl.ds(block * LANES, LANES)
            wall = edges_ref[8 * edge : 8 * edge + 1, lanes]
            flip = edges_ref[8 * edge + 1 : 8 * edge + 2, lanes]
            start = 0
            for chunk, field_ref in enumerate(fields):
                modes = field_ref.shape[1]
                rows = slice(start, start + modes)
                start += modes
                turned = jnp.broadcast_to(flip, (modes, LANES)) > 0.5
                coef = 1.0 - wall * (1.0 - flag_ref[first + start - modes : first + start])
                for t in range(8):
                    node = EDGE_NODES[edge][t]
                    value = field_ref[node, :, lanes]
                    other = jnp.where(turned, val_ref[7 - t, rows, lanes], val_ref[t, rows, lanes])
                    weight = np.float32(edge_penalty * WEIGHTS[t])
                    visit(chunk, rows, node, lanes, value, weight * (coef * value - other))


def far_edges(after_ref, before_ref, far_ref, edges_ref, trace_ref, elems, visit):
    modes = after_ref.shape[1]
    lane = lane_of((modes, LANES))

    def value_of(t):
        return jnp.where(lane < ROWS, after_ref[t], before_ref[t])

    fill_pairs(trace_ref, 0, modes, pl.ds(0, LANES), value_of, 2)
    for edge in range(4):
        values = gathered(trace_ref[...], far_ref[:, edge * LANES : (edge + 1) * LANES], 2)
        flips = edges_ref[8 * edge + 1 : 8 * edge + 2, :]
        flip = jnp.where(lane < ROWS, flips[:, :LANES], flips[:, elems - LANES :])
        for t in range(8):
            other = jnp.where(flip > 0.5, values[7 - t], values[t])
            visit(edge, t, other * np.float32(-edge_penalty * WEIGHTS[t]))


def apply_kernel(want_image, count, first, given, *refs):
    fields, refs = refs[:count], refs[count:]
    inner, refs = refs[:given], refs[given:]
    geo_ref, mass_ref, flag_ref, local_ref, edges_ref = refs[:5]
    refs = refs[5:]
    image_ref = refs[0] if want_image else None
    sums_ref, trace_ref, val_ref, acc_ref = refs[-4:]
    sums_ref[...] = jnp.zeros_like(sums_ref)
    start = 0
    for field_ref in fields:
        row = first + start
        step = 1
        if inner and start == 0:
            sums_ref[:, : field_ref.shape[1], :] = inner[0][...]
            step = field_ref.shape[2] // LANES - 1
        volume(field_ref, geo_ref, mass_ref, row, image_ref, sums_ref, start, acc_ref, 0, step)
        start += field_ref.shape[1]
    totals = [None] * count

    def visit(chunk, rows, node, lanes, value, term):
        if want_image:
            image_ref[node, :, lanes] += term
        product = value * term
        totals[chunk] = product if totals[chunk] is None else totals[chunk] + product

    parts = 2 if want_image else 1
    local_edges(
        fields, first, flag_ref, local_ref, edges_ref, trace_ref, val_ref, parts, visit
    )
    start = 0
    for chunk, field_ref in enumerate(fields):
        rows = slice(start, start + field_ref.shape[1])
        start = rows.stop
        sums_ref[1, rows, :] += totals[chunk]


def apply_local(fields, first, geo, mass, flag, local, edges, want_image, inner=()):
    elems = fields[0].shape[2]
    modes = sum(field.shape[1] for field in fields)
    sums = jax.ShapeDtypeStruct((2, modes, LANES), jnp.float32)
    shapes = [jax.ShapeDtypeStruct(fields[0].shape, jnp.float32), sums] if want_image else [sums]
    parts = 2 if want_image else 1
    return pl.pallas_call(
        functools.partial(apply_kernel, want_image, len(fields), first, len(inner)),
        in_specs=vmem(5 + len(fields) + len(inner)),
        out_specs=vmem(len(shapes)),
        out_shape=shapes,
        scratch_shapes=[
            pltpu.VMEM((parts * 8 * modes, 4 * elems), jnp.bfloat16),
            pltpu.VMEM((8, modes, elems), jnp.float32),
            pltpu.VMEM((64, 8, LANES), jnp.float32),
        ],
        compiler_params=pltpu.CompilerParams(vmem_limit_bytes=16 * MIB),
        cost_estimate=small_cost(),
    )(*fields, *inner, geo, mass, flag, local, edges)


def ends_of(node, field_refs, lane):
    elems = field_refs[0].shape[2]
    pieces = []
    for ref in field_refs:
        pieces.append((ref[node, :, :LANES], ref[node, :, elems - LANES :]))
    first = [p[0] for p in pieces]
    last = [p[1] for p in pieces]
    if len(pieces) > 1:
        first, last = [jnp.concatenate(first, axis=0)], [jnp.concatenate(last, axis=0)]
    return jnp.where(lane < ROWS, first[0], last[0])


def first_far_kernel(count, *refs):
    images, fields, refs = refs[:count], refs[count : 2 * count], refs[2 * count :]
    sum_refs, refs = refs[:count], refs[count:]
    after_ref, before_ref, far_ref, edges_ref, mask_ref = refs[:5]
    outs, (send_ref, out_ref, trace_ref) = refs[5 : 5 + count], refs[5 + count :]
    modes = after_ref.shape[1]
    elems = fields[0].shape[2]
    lane = lane_of((modes, LANES))
    sums = [[ref[k] for ref in sum_refs] for k in range(2)]
    sums = [jnp.concatenate(pieces, axis=0) if count > 1 else pieces[0] for pieces in sums]
    totals = [sums[1]]
    done = set()

    def visit(edge, t, term):
        node = EDGE_NODES[edge][t]
        totals[0] = totals[0] + ends_of(node, fields, lane) * term
        start = 0
        for image_ref, ref in zip(images, outs):
            size = ref.shape[1]
            part = term[start : start + size]
            here = lane_of((size, LANES)) < ROWS
            start += size
            source = ref if node in done else image_ref
            ref[node, :, :LANES] = source[node, :, :LANES] + jnp.where(here, part, 0.0)
            ref[node, :, elems - LANES :] = source[node, :, elems - LANES :] + jnp.where(
                here, 0.0, part
            )
        done.add(node)

    far_edges(after_ref, before_ref, far_ref, edges_ref, trace_ref, elems, visit)
    out_ref[0] = sums[0]
    out_ref[1] = totals[0]
    start = 0
    for ref in outs:
        send_from(ref, mask_ref, send_ref, start)
        start += ref.shape[1]


def first_far(images, fields, halo, far, edges, mask, sums):
    count = len(fields)
    modes = sum(value.shape[1] for value in sums)
    return pl.pallas_call(
        functools.partial(first_far_kernel, count),
        in_specs=vmem(3 * count + 5),
        out_specs=vmem(count + 2),
        out_shape=[jax.ShapeDtypeStruct(image.shape, jnp.float32) for image in images]
        + [
            jax.ShapeDtypeStruct((8, modes, LANES), jnp.float32),
            jax.ShapeDtypeStruct((2, modes, LANES), jnp.float32),
        ],
        scratch_shapes=[pltpu.VMEM((16 * modes, LANES), jnp.bfloat16)],
        input_output_aliases={k: k for k in range(count)},
        compiler_params=pltpu.CompilerParams(vmem_limit_bytes=8 * MIB),
        cost_estimate=small_cost(),
    )(*images, *fields, *sums, *halo, far, edges, mask)


def second_far_kernel(count, *refs):
    fields, refs = refs[:count], refs[count:]
    after_ref, before_ref, far_ref, edges_ref, first_ref, more_ref, out_ref, trace_ref = refs
    modes = after_ref.shape[1]
    elems = fields[0].shape[2]
    lane = lane_of((modes, LANES))
    totals = [more_ref[1]]

    def visit(edge, t, term):
        totals[0] = totals[0] + ends_of(EDGE_NODES[edge][t], fields, lane) * term

    far_edges(after_ref, before_ref, far_ref, edges_ref, trace_ref, elems, visit)
    sums = [first_ref[0], first_ref[1], more_ref[0], totals[0]]
    packed = jnp.zeros((modes, LANES), jnp.float32)
    for k, value in enumerate(sums):
        packed = jnp.where(lane == k, jnp.sum(value, axis=1, keepdims=True), packed)
    out_ref[...] = packed


def second_far(fields, halo, far, edges, first, more):
    modes = first.shape[1]
    return pl.pallas_call(
        functools.partial(second_far_kernel, len(fields)),
        in_specs=vmem(6 + len(fields)),
        out_specs=vmem(1)[0],
        out_shape=jax.ShapeDtypeStruct((modes, LANES), jnp.float32),
        scratch_shapes=[pltpu.VMEM((16 * modes, LANES), jnp.bfloat16)],
        compiler_params=pltpu.CompilerParams(vmem_limit_bytes=8 * MIB),
        cost_estimate=small_cost(),
    )(*fields, *halo, far, edges, first, more)


def finish_kernel(count, chunks, *refs):
    fields, refs = refs[: 2 * chunks], refs[2 * chunks :]
    sum_refs, (out_ref, buffer_ref, sems) = refs[:count], refs[count:]
    total = sum_refs[0][...]
    for ref in sum_refs[1:]:
        total = total + ref[...]
    m0, m1, m2, m3 = [total[:, k : k + 1] for k in range(4)]
    alpha = m0 / m1
    norm = alpha * (alpha * m2) - 2.0 * (alpha * m1) + m0
    energy = m1 - 2.0 * (alpha * m2) + alpha * (alpha * m3)
    beta = norm / m0
    second = norm / (energy - beta * (norm / alpha))
    on_r = jnp.broadcast_to(alpha + second * (1.0 + beta), total.shape)
    on_q = jnp.broadcast_to(second * alpha, total.shape)
    elems = out_ref.shape[2]
    slots = buffer_ref.shape[0]
    tiles = total.shape[0] // 8

    def copy(tile):
        target = out_ref.at[pl.ds(8 * tile, 8)]
        return pltpu.make_async_copy(buffer_ref.at[tile % slots], target, sems.at[tile % slots])

    tile = 0
    for chunk in range(chunks):
        r0_ref, q0_ref = fields[2 * chunk : 2 * chunk + 2]
        for first in range(0, r0_ref.shape[1], 8):
            if tile >= slots:
                copy(tile - slots).wait()
            mine = slice(8 * tile, 8 * tile + 8)
            rows = slice(first, first + 8)
            on_r0, on_q0 = on_r[mine], on_q[mine]
            for block in range(elems // LANES):
                lanes = slice(block * LANES, (block + 1) * LANES)
                for j in range(8):
                    nodes = slice(8 * j, 8 * j + 8)
                    value = on_r0 * r0_ref[nodes, rows, lanes] - on_q0 * q0_ref[nodes, rows, lanes]
                    buffer_ref[tile % slots, :, nodes, lanes] = jnp.swapaxes(value, 0, 1)
            copy(tile).start()
            tile += 1
    for left in range(max(tiles - slots, 0), tiles):
        copy(left).wait()


def finish(fields, sums):
    elems = fields[0].shape[2]
    total = sums[0].shape[0]
    slots = min(4, total // 8)
    return pl.pallas_call(
        functools.partial(finish_kernel, len(sums), len(fields) // 2),
        in_specs=vmem(len(fields) + len(sums)),
        out_specs=pl.BlockSpec(memory_space=pl.ANY),
        out_shape=jax.ShapeDtypeStruct((total, 64, elems), jnp.float32),
        scratch_shapes=[
            pltpu.VMEM((slots, 8, 64, elems), jnp.float32),
            pltpu.SemaphoreType.DMA((slots,)),
        ],
        compiler_params=pltpu.CompilerParams(vmem_limit_bytes=16 * MIB),
    )(*fields, *sums)


def shifted(value, axis, steps):
    size = lax.axis_size(axis)
    return lax.ppermute(value, axis, [(i, (i + steps) % size) for i in range(size)])


def exchanged(slots, first=0):
    size = lax.axis_size("gz")
    out = []
    for number, value in enumerate(slots):
        d = first + number
        out.append(lax.ppermute(value, "gz", [(i, i ^ d) for i in range(size)]) if d else value)
    return out


def both_sides(send):
    return [shifted(send, "xy", -1), shifted(send, "xy", 1)]


def pad_rows(values, rows=8):
    return jnp.pad(values, ((0, rows - values.shape[0]), (0, 0)))


def edge_tables(nbr_elem, nbr_edge):
    elems = nbr_elem.shape[1]
    me, size = lax.axis_index("xy"), lax.axis_size("xy")
    wall = nbr_elem < 0
    ids = jnp.maximum(nbr_elem, 0)
    owner, local_id = ids // elems, ids % elems
    here = (owner == me) & ~wall
    after = (owner == (me + 1) % size) & ~wall & ~here
    before = ~wall & ~here & ~after
    place = jnp.where(here, nbr_edge % 4 * elems + local_id, -1).reshape(-1)
    source = jnp.arange(4 * elems, dtype=jnp.int32)[:, None]
    local = (source == place[None, :]).astype(jnp.bfloat16)
    first = jnp.arange(LANES) < ROWS

    def ends(table):
        return jnp.where(first[None, :], table[:, :LANES], table[:, elems - LANES :])

    send = jnp.where(first[None, :], before[:, :LANES], after[:, elems - LANES :])
    slot = jnp.where(after, local_id, local_id - (elems - ROWS) + ROWS)
    slot = jnp.where(send, ends(slot), -1).reshape(-1)
    far = (jnp.arange(LANES, dtype=jnp.int32)[:, None] == slot[None, :]).astype(jnp.bfloat16)
    flags = jnp.stack([wall, nbr_edge >= 4], axis=1).astype(jnp.float32)
    flags = jnp.pad(flags, ((0, 0), (0, 6), (0, 0))).reshape(32, elems)
    return local, far, pad_rows(send.astype(jnp.float32)), flags


def per_device(concentration, geometry, nbr_elem, nbr_edge, wall_flags):
    planes, _, elems = concentration.shape
    groups = lax.axis_size("gz")
    me = lax.axis_index("gz")
    fold = Fold(elems // groups)
    scale_x, scale_y = geometry[0], geometry[1]
    geo = pad_rows(jnp.stack([1.0 / (scale_x * scale_y), scale_x * scale_x, scale_y * scale_y]))
    mine = lax.dynamic_slice_in_dim(geo, me * fold.width, fold.width, axis=1)
    mine = jnp.tile(mine, (1, fold.parts))
    index = me.astype(jnp.int32).reshape(1)
    mode_ids = me * planes + jnp.arange(planes, dtype=jnp.int32)
    wave = ((mode_ids + 1) // 2).astype(jnp.float32)
    mass = jnp.broadcast_to(
        (1.0 / time_step + axial_stiffness * wave * wave)[:, None], (planes, LANES)
    )
    flag = jnp.broadcast_to(wall_flags.astype(jnp.float32)[:, None], (planes, LANES))
    tables = edge_tables(nbr_elem, nbr_edge)
    half = groups // 2
    far_sent = list(pack(index, concentration, fold, groups, half, fold.parts))
    more = half - fold.parts
    far_sent += pack(index, concentration, fold, groups, half + fold.parts, more) if more else []
    near_sent = pack(index, concentration, fold, groups, 0, half)
    near_field = exchanged(near_sent)
    near_field[2], far_sent[-1] = lax.optimization_barrier((near_field[2], far_sent[-1]))
    near_field[1], far_sent[2] = lax.optimization_barrier((near_field[1], far_sent[2]))
    far_field = exchanged(far_sent, half)
    halves, pieces = transform_tables(planes * groups, planes)
    last = lax.dynamic_index_in_dim(pieces, me ^ (groups - 1), 0, keepdims=False)
    near_field, geo, mine, mass, flag, tables, last = lax.optimization_barrier(
        (near_field, geo, mine, mass, flag, tables, last)
    )
    local, far, mask, edges = tables
    near = some_terms(index, mine, near_field, fold, 0, half)
    near, *some_far = lax.optimization_barrier((near, *far_field[:-1]))
    far_terms = some_terms(index, mine, some_far, fold, half, half, clear=True)
    sizes = [planes - 8, 8] if planes > 16 else [planes]
    partial = partial_modes(index, halves, near, far_terms, half, planes, 1)
    sent, terms = far_modes(index, mine, last, partial, far_field[-1], fold, half, sizes)
    far_parts = [exchanged(piece, half) for piece in sent]
    partial = partial_modes(index, halves, near, far_terms, half, planes, 0)
    near_parts = exchanged(near_modes(index, mine, last, partial, terms, fold, half, planes))
    fields, images, sums, sends, inner = [], [], [], [], []
    start = 0
    for piece, size in enumerate(sizes):
        parts = near_parts + far_parts[piece]
        field, send = unpack(index, mask, parts, fold, sends)
        sends = [send]
        image, more = apply_local([field], start, geo, mass, flag, local, edges, True)
        start += size
        if piece + 1 < len(sizes):
            inner = [inner_sums(image, geo, mass)]
            mask, inner = lax.optimization_barrier((mask, inner))
        fields.append(field)
        images.append(image)
        sums.append(more)
    halo = both_sides(sends[0])
    *images, send, sums = first_far(images, fields, halo, far, edges, mask, sums)
    (more,) = apply_local(images, 0, geo, mass, flag, local, edges, False, inner)
    packed = second_far(images, both_sides(send), far, edges, sums, more)
    size = lax.axis_size("xy")
    pairs = [value for pair in zip(fields, images) for value in pair]
    return finish(pairs, [packed] + [shifted(packed, "xy", k) for k in range(1, size)])


def solution(mesh):
    return jax.shard_map(
        per_device,
        mesh=mesh,
        in_specs=(P("gz", None, "xy"), P(None, "xy"), P(None, "xy"), P(None, "xy"), P("gz")),
        out_specs=P("gz", None, "xy"),
        check_vma=False,
    )
```
